32 devices in a mesh: section: 2 (over core), seq: 4 (over y, x), dp: 4 (over z).
Axes of the slice: x: 2, y: 2, z: 4, core: 2. Of those that a mesh axis runs over, the one named last changes fastest.
Arguments:
- tokens: bfloat16 [8, 1024, 1024], P('dp', 'seq'), may hold values from -6 to 6
- out_grad: bfloat16 [8, 1024, 1024], P('dp', 'seq'), may hold values from -6 to 6
- lengths: int32 [8, 4], P('dp'), may hold values from 0 to 1024, as said below
- ln1_gain: bfloat16 [2, 1024], P('section', 'seq'), may hold values from 0.5 to 1.5
- w_in: bfloat16 [2, 1024, 3072], P('section', 'seq'), may hold values from -0.1875 to 0.1875
- short_w: bfloat16 [2, 3, 3072], P('section', None, 'seq'), may hold values from -3 to 3
- filt_in: bfloat16 [2, 33, 64], P('section', None, 'seq'), may hold values from -1 to 1
- filt_shift: bfloat16 [2, 64], P('section', 'seq'), may hold values from -3.140625 to 3.140625
- sine_freq: bfloat16 [2, 64], P('section', 'seq'), may hold values from 2 to 30
- filt_out: bfloat16 [2, 64, 1024], P('section', 'seq'), may hold values from -0.0625 to 0.0625
- decay: bfloat16 [2, 1024], P('section', 'seq'), may hold values from 0.5 to 32
- filter_bias: bfloat16 [2, 1024], P('section', 'seq'), may hold values from -4 to 4
- w_out: bfloat16 [2, 1024, 1024], P('section', 'seq'), may hold values from -0.1875 to 0.1875
- ln2_gain: bfloat16 [2, 1024], P('section', 'seq'), may hold values from 0.5 to 1.5
- mlp_up: bfloat16 [2, 1024, 4096], P('section', 'seq'), may hold values from -0.1875 to 0.1875
- mlp_down: bfloat16 [2, 4096, 1024], P('section', 'seq'), may hold values from -0.09375 to 0.09375
Outputs:
- layer_outputs: bfloat16 [2, 8, 1024, 1024], P('section', 'dp', 'seq')
- input_grads: bfloat16 [2, 8, 1024, 1024], P('section', 'dp', 'seq')
- grad_ln1_gain: float32 [2, 1024], P('section', 'seq')
- grad_w_in: float32 [2, 1024, 3072], P('section', 'seq')
- grad_short_w: float32 [2, 3, 3072], P('section', None, 'seq')
- grad_filt_in: float32 [2, 33, 64], P('section', None, 'seq')
- grad_filt_shift: float32 [2, 64], P('section', 'seq')
- grad_sine_freq: float32 [2, 64], P('section', 'seq')
- grad_filt_out: float32 [2, 64, 1024], P('section', 'seq')
- grad_decay: float32 [2, 1024], P('section', 'seq')
- grad_filter_bias: float32 [2, 1024], P('section', 'seq')
- grad_w_out: float32 [2, 1024, 1024], P('section', 'seq')
- grad_ln2_gain: float32 [2, 1024], P('section', 'seq')
- grad_mlp_up: float32 [2, 1024, 4096], P('section', 'seq')
- grad_mlp_down: float32 [2, 4096, 1024], P('section', 'seq')
The draws below stay inside these ranges and needn't reach their ends.
Inputs may be any that keep to these rules, and one draw needn't show every extreme that they name: `lengths`: row by row: an entry is the length in tokens of the document that starts at that block's first position, or 0 where no document starts; entry 0 is positive; a document of length n covers ceil(n / 256) blocks from its start and the next document starts in the block after them; the last one ends in the last block; among each replica's 2 rows, one holds a single document of 1024 tokens.
All inputs are finite; a program needn't handle non-finite values.
Results may differ from the reference program's by a relative error of at most 0.04.
Values may be sent and summed in bfloat16 or wider, within the bound.
A program may use at most 448 MiB of HBM per device.

```python
import math
import jax
import jax.numpy as jnp
from jax import lax

D = 1024
FF = 4096
FREQS = 16
FILT = 64
TOK_BLK = 256
MICRO = 2
EMB = 33
SLOTS = 1024
SEQ_BLOCKS = 4
BATCHES = 8
N_SEQ = 4


def draw_lengths(key, part):
    key = jax.random.fold_in(key, 7)
    key_flags = jax.random.fold_in(key, 1)
    key_long = jax.random.fold_in(key, 2)
    key_sizes = jax.random.fold_in(key, 3)
    index_all = jnp.arange(SEQ_BLOCKS, dtype=jnp.int32)
    flags = jax.random.randint(key_flags, (BATCHES, SEQ_BLOCKS), 0, 2)
    flags = jnp.where(index_all[None, :] == 0, 1, flags)
    chosen = jax.random.randint(key_long, (BATCHES // MICRO,), 0, MICRO)
    row_slot = jnp.arange(BATCHES, dtype=jnp.int32) % MICRO
    is_long = row_slot == jnp.repeat(chosen, MICRO)
    flags = jnp.where(is_long[:, None], (index_all[None, :] == 0).astype(jnp.int32), flags)
    positions = jnp.where(flags > 0, index_all[None, :], SEQ_BLOCKS)
    following = jnp.concatenate([positions[:, 1:], jnp.full((BATCHES, 1), SEQ_BLOCKS, jnp.int32)], axis=1)
    next_start = lax.cummin(following, axis=1, reverse=True)
    span = jnp.maximum(next_start - index_all[None, :], 1)
    sizes = jax.random.randint(key_sizes, (BATCHES, SEQ_BLOCKS), (span - 1) * TOK_BLK + 1, span * TOK_BLK + 1)
    sizes = jnp.where(is_long[:, None], span * TOK_BLK, sizes)
    return jnp.where(flags > 0, sizes, 0).astype(jnp.int32)


def level_of(own_key, shape, shards, smallest, high):
    def one(dim, blocks):
        draws = jax.random.uniform(jax.random.fold_in(jax.random.fold_in(own_key, 6), dim), (blocks,), jnp.float32, smallest / len(shards), high / len(shards))
        return jnp.repeat(jnp.exp(draws), shape[dim] // blocks).reshape((-1,) + (1,) * (len(shape) - dim - 1))

    loudness = one(*shards[0])
    for cut in shards[1:]:
        loudness = loudness * one(*cut)
    return loudness


def normal_values(key, dims, spread, limit, split=(), kind=jnp.bfloat16):
    result = jax.random.normal(key, dims, jnp.float32) * spread
    if len(split) > 0:
        result = level_of(key, dims, split, -0.22, 0.18) * result
    return jnp.clip(result, min=-limit, max=limit).astype(kind)


def setup_inputs(seed: int = 0) -> dict:
    arg_keys = jax.random.split(jax.random.key(seed), 17)
    tokens = normal_values(arg_keys[0], (BATCHES, SLOTS, D), 1.0, 6.0, ((0, 4), (1, 4)))
    out_grad = normal_values(arg_keys[1], (BATCHES, SLOTS, D), 1.0, 6.0, ((0, 4), (1, 4)))
    lengths = draw_lengths(jax.random.fold_in(arg_keys[16], 71), 0)
    ln1_gain = jnp.clip(1.0 + 0.1 * jax.random.normal(arg_keys[3], (2, D), jnp.float32), 0.5, 1.5).astype(jnp.bfloat16)
    w_in = normal_values(arg_keys[4], (2, D, 3 * D), D ** -0.5, 0.1875, ((0, 2), (1, 4)))
    short_w = normal_values(arg_keys[5], (2, 3, 3 * D), 0.5, 3.0, ((0, 2), (2, 4)))
    filt_in = normal_values(arg_keys[6], (2, EMB, FILT), EMB ** -0.5, 1.0, ((0, 2), (2, 4)))
    filt_shift = jnp.clip(jax.random.uniform(arg_keys[7], (2, FILT), jnp.float32, -3.140625, 3.140625), -3.140625, 3.140625).astype(jnp.bfloat16)
    sine_freq = jnp.clip(jnp.exp(math.log(30.0) - 2.7080502 * jax.random.uniform(arg_keys[8], (2, FILT), jnp.float32) ** level_of(arg_keys[8], (2, FILT), ((0, 2), (1, 4)), -0.2, 0.2)), 2.0, 30.0).astype(jnp.bfloat16)
    filt_out = normal_values(arg_keys[9], (2, FILT, D), (8 * SLOTS) ** -0.5, 0.0625, ((0, 2), (1, 4)))
    decay = jnp.clip(jnp.exp(math.log(32.0) - 4.158883 * jax.random.uniform(arg_keys[10], (2, D), jnp.float32) ** level_of(arg_keys[10], (2, D), ((0, 2), (1, 4)), -0.2, 0.2)), 0.5, 32.0).astype(jnp.bfloat16)
    filter_bias = normal_values(arg_keys[11], (2, D), 1.0, 4.0, ((0, 2), (1, 4)))
    w_out = normal_values(arg_keys[12], (2, D, D), D ** -0.5, 0.1875, ((0, 2), (1, 4)))
    ln2_gain = jnp.clip(1.0 + 0.1 * jax.random.normal(arg_keys[13], (2, D), jnp.float32), 0.5, 1.5).astype(jnp.bfloat16)
    mlp_up = normal_values(arg_keys[14], (2, D, FF), D ** -0.5, 0.1875, ((0, 2), (1, 4)))
    mlp_down = normal_values(arg_keys[15], (2, FF, D), FF ** -0.5, 0.09375, ((0, 2), (1, 4)))
    return dict(tokens=tokens, out_grad=out_grad, lengths=lengths, ln1_gain=ln1_gain, w_in=w_in, short_w=short_w, filt_in=filt_in, filt_shift=filt_shift, sine_freq=sine_freq, filt_out=filt_out, decay=decay, filter_bias=filter_bias, w_out=w_out, ln2_gain=ln2_gain, mlp_up=mlp_up, mlp_down=mlp_down)


PRECISE = lax.Precision.HIGHEST
EPSILON = 1e-05

@jax.custom_vjp
def low(v):
    return lax.optimization_barrier(v.astype(jnp.bfloat16)).astype(jnp.float32)

@jax.custom_vjp
def low_back(v):
    return v

def low_keep(v):
    return (low(v), None)

def low_pass(kept, grad):
    return (grad,)

def back_keep(v):
    return (v, None)

def back_low(kept, grad):
    return (low(grad),)
low.defvjp(low_keep, low_pass)
low_back.defvjp(back_keep, back_low)

def matmul_high(left, right):
    return jnp.dot(left, right, preferred_element_type=jnp.float32, precision=PRECISE)

def layer_norm(values, gains):
    row_mean = lax.optimization_barrier(jnp.mean(values, axis=-1, keepdims=True))
    centered = values - row_mean
    variance = lax.optimization_barrier(jnp.mean(centered * centered, axis=-1, keepdims=True))
    return centered * lax.rsqrt(variance + EPSILON) * gains

def positions_embedding(slots, harmonic_count):
    steps_all = jnp.arange(slots, dtype=jnp.int32)
    scaled = steps_all.astype(jnp.float32) / slots
    harmonics = jnp.arange(1, harmonic_count + 1, dtype=jnp.int32)
    phase = (steps_all[:, None] * harmonics[None, :] % slots).astype(jnp.float32) * (2.0 * math.pi / slots)
    return jnp.concatenate([scaled[:, None], jnp.cos(phase), jnp.sin(phase)], axis=1)

def filter_taps(filt_in, filt_shift, sine_freq, filt_out, decay, embedding):
    slots = embedding.shape[0]
    hidden_sine = jnp.sin(sine_freq * (matmul_high(embedding, filt_in) + filt_shift))
    scaled = jnp.arange(slots, dtype=jnp.int32).astype(jnp.float32) / slots
    return matmul_high(hidden_sine, filt_out) * jnp.exp(-decay[None, :] * scaled[:, None])

def region_and_valid(length_row):
    count = length_row.shape[0]
    index_all = jnp.arange(count, dtype=jnp.int32)
    first_block = lax.cummax(jnp.where(length_row > 0, index_all, 0), axis=0)
    doc_length = lax.optimization_barrier(jnp.sum(jnp.where(first_block[:, None] == index_all[None, :], length_row[None, :], 0), axis=1))
    region = jnp.repeat(first_block, TOK_BLK)
    offsets = jnp.arange(SLOTS, dtype=jnp.int32) - region * TOK_BLK
    valid_rows = (offsets < jnp.repeat(doc_length, TOK_BLK)).astype(jnp.float32)
    return (region, valid_rows)

def long_convolution(masked, taps, region):
    count = masked.shape[0]
    size = 2 * count
    taps_spec = jnp.fft.rfft(taps, n=size, axis=0)
    total = jnp.zeros_like(masked)
    for document in range(N_SEQ):
        select = (region == document).astype(masked.dtype)[:, None]
        full = jnp.fft.irfft(jnp.fft.rfft(masked * select, n=size, axis=0) * taps_spec, n=size, axis=0)
        total = total + select * full[:count]
    return total

def layer(params, layer_in, region, valid_rows):
    gain_one, in_matrix, short_weights, filt_in, filt_shift, sine_freq, filt_out, decay, filter_bias, out_matrix, gain_two, up_matrix, down_matrix = params
    width = layer_in.shape[1]
    normed = low(layer_norm(layer_in, gain_one))
    projected = low(low_back(matmul_high(normed, in_matrix)))
    same_one = jnp.concatenate([jnp.zeros((1,), jnp.float32), (region[1:] == region[:-1]).astype(jnp.float32)])
    same_two = jnp.concatenate([jnp.zeros((2,), jnp.float32), (region[2:] == region[:-2]).astype(jnp.float32)])
    back_one = jnp.concatenate([jnp.zeros((1, 3 * width), jnp.float32), projected[:-1]], axis=0) * same_one[:, None]
    back_two = jnp.concatenate([jnp.zeros((2, 3 * width), jnp.float32), projected[:-2]], axis=0) * same_two[:, None]
    mixed = short_weights[0] * projected + short_weights[1] * back_one + short_weights[2] * back_two
    first_part = mixed[:, :width]
    second_part = mixed[:, width:2 * width]
    third_part = mixed[:, 2 * width:]
    signal = first_part * third_part
    masked = signal * valid_rows[:, None]
    taps = filter_taps(filt_in, filt_shift, sine_freq, filt_out, decay, positions_embedding(SLOTS, FREQS))
    filtered = long_convolution(masked, taps, region) * valid_rows[:, None] + filter_bias * signal
    gated = low(second_part * filtered)
    residual = layer_in + low_back(matmul_high(gated, out_matrix))
    normed_two = low(layer_norm(residual, gain_two))
    upward = low_back(matmul_high(normed_two, up_matrix))
    activated = low(jax.nn.gelu(upward, approximate=True))
    return residual + matmul_high(activated, down_matrix)

def reference(tokens, out_grad, lengths, ln1_gain, w_in, short_w, filt_in, filt_shift, sine_freq, filt_out, decay, filter_bias, w_out, ln2_gain, mlp_up, mlp_down):
    stacked = [array.astype(jnp.float32) for array in (ln1_gain, w_in, short_w, filt_in, filt_shift, sine_freq, filt_out, decay, filter_bias, w_out, ln2_gain, mlp_up, mlp_down)]
    params_first = tuple((array[0] for array in stacked))
    params_second = tuple((array[1] for array in stacked))

    def one_batch(sums, inputs):
        tokens_row, grad_row, length_row = inputs
        region, valid_rows = region_and_valid(length_row)
        start_in = tokens_row.astype(jnp.float32)
        out_first, pull_first = jax.vjp(lambda params, values: layer(params, values, region, valid_rows), params_first, start_in)
        middle = out_first.astype(jnp.bfloat16)
        out_second, pull_second = jax.vjp(lambda params, values: layer(params, values, region, valid_rows), params_second, middle.astype(jnp.float32))
        grads_second, back_middle = pull_second(grad_row.astype(jnp.float32))
        middle_grad = back_middle.astype(jnp.bfloat16)
        grads_first, back_start = pull_first(middle_grad.astype(jnp.float32))
        sums_first = tuple((earlier + latest for earlier, latest in zip(sums[0], grads_first)))
        sums_second = tuple((earlier + latest for earlier, latest in zip(sums[1], grads_second)))
        return ((sums_first, sums_second), (middle, out_second.astype(jnp.bfloat16), back_start.astype(jnp.bfloat16), middle_grad))
    zeros_first = tuple((jnp.zeros_like(array) for array in params_first))
    zeros_second = tuple((jnp.zeros_like(array) for array in params_second))
    sums, outputs = lax.scan(one_batch, (zeros_first, zeros_second), (tokens, out_grad, lengths))
    middle_all, last_all, start_grads, middle_grads = outputs
    layer_outputs = jnp.stack([middle_all, last_all])
    input_grads = jnp.stack([start_grads, middle_grads])
    grads = [jnp.stack([sums[0][index], sums[1][index]]) for index in range(13)]
    return (layer_outputs, input_grads, grads[0], grads[1], grads[2], grads[3], grads[4], grads[5], grads[6], grads[7], grads[8], grads[9], grads[10], grads[11], grads[12])
```

```python
import functools
import math

import jax
import jax.numpy as jnp
import numpy as np
from jax import lax
from jax.experimental import pallas as pl
from jax.experimental.pallas import tpu as pltpu
from jax.sharding import PartitionSpec as P

FREQS = 16
PRECISE = lax.Precision.HIGHEST
EPSILON = 1e-05
BF = jnp.bfloat16
F32 = jnp.float32


def dot(left, right):
    return jnp.dot(left, right, preferred_element_type=F32)


def dot_left(left, right):
    return lax.dot_general(left, right, (((0,), (0,)), ((), ())), preferred_element_type=F32)


def dot_right(left, right):
    return lax.dot_general(left, right, (((1,), (1,)), ((), ())), preferred_element_type=F32)


def layer_norm(values, gains):
    row_mean = jnp.mean(values, axis=-1, keepdims=True)
    centered = values - row_mean
    variance = jnp.mean(centered * centered, axis=-1, keepdims=True)
    return centered * lax.rsqrt(variance + EPSILON) * gains


def gelu_tanh(values):
    return jax.nn.gelu(values, approximate=True)


def positions_embedding(slots, harmonic_count):
    steps_all = np.arange(slots)
    scaled = steps_all / slots
    harmonics = np.arange(1, harmonic_count + 1)
    phase = (steps_all[:, None] * harmonics[None, :] % slots) * (2.0 * math.pi / slots)
    both = np.concatenate([scaled[:, None], np.cos(phase), np.sin(phase)], axis=1)
    return both.astype(np.float32)


def filter_taps(filt_in, filt_shift, sine_freq, filt_out, decay, embedding):
    slots = embedding.shape[0]
    inner = jnp.dot(embedding, filt_in, preferred_element_type=F32, precision=PRECISE)
    hidden_sine = jnp.sin(sine_freq * (inner + filt_shift))
    scaled = jnp.arange(slots, dtype=jnp.int32).astype(F32) / slots
    summed = jnp.dot(hidden_sine, filt_out, preferred_element_type=F32, precision=PRECISE)
    return summed * jnp.exp(-decay[None, :] * scaled[:, None])


def short_mix(rim_values, proj_values, weight_values, carried_on):
    total_rows = proj_values.shape[0]
    extended = jnp.concatenate([rim_values * carried_on, proj_values], axis=0)
    return (
        weight_values[0] * extended[2:]
        + weight_values[1] * extended[1 : total_rows + 1]
        + weight_values[2] * extended[:total_rows]
    )


def packed_dft(rows):
    size = 2 * rows
    phase = (np.arange(rows)[:, None] * np.arange(rows)[None, :] % size) * (2.0 * math.pi / size)
    lower = -np.sin(phase)
    lower[0] = 1 - 2 * (np.arange(rows) % 2)
    table = np.concatenate([np.cos(phase), lower], axis=0)
    weight = np.full((size, 1), 2.0 / size)
    weight[0] = weight[rows] = 1.0 / size
    parity = 1.0 - 2.0 * (np.arange(rows) % 2)
    parity = np.concatenate([parity, parity])[:, None]
    parity[rows] = 1 - 2 * (rows % 2)
    return table.astype(np.float32), weight.astype(np.float32), parity.astype(np.float32)


def spectra_rows(table_ref, source_ref, target_ref, blocks, rows):
    for block in range(blocks):
        target_ref[block] = jnp.dot(
            table_ref[...], source_ref[pl.ds(block * rows, rows), :], preferred_element_type=F32
        )


def convolve_kernel(blocks, rows, step, same_ref, table_ref, back_ref, filt_ref, x_ref, y_ref, spec_ref, out_ref):
    spectra_rows(table_ref, x_ref, spec_ref, blocks, rows)

    def chunk(index, carry):
        real = pl.ds(pl.multiple_of(index * step, step), step)
        imag = pl.ds(pl.multiple_of(rows + index * step, step), step)
        width = x_ref.shape[1]
        first = (lax.broadcasted_iota(jnp.int32, (step, width), 0) + index * step) == 0
        for i in range(blocks):
            total_real = jnp.zeros((step, width), F32)
            total_imag = jnp.zeros((step, width), F32)
            for lag in range(i + 1):
                weight = same_ref[i, i - lag]
                fr = filt_ref[lag, real, :]
                fi = filt_ref[lag, imag, :]
                cross = jnp.where(first, 0.0, fi)
                own = jnp.where(first, fi, fr)
                xr = spec_ref[i - lag, real, :] * weight
                xi = spec_ref[i - lag, imag, :] * weight
                total_real = total_real + (fr * xr - cross * xi)
                total_imag = total_imag + (cross * xr + own * xi)
            out_ref[i, real, :] = total_real.astype(BF)
            out_ref[i, imag, :] = total_imag.astype(BF)
        return carry

    lax.fori_loop(0, rows // step, chunk, 0)
    for block in range(blocks):
        y_ref[pl.ds(block * rows, rows), :] = jnp.dot(
            back_ref[...], out_ref[block], preferred_element_type=F32
        ).astype(BF)


def correlate_kernel(
    blocks, rows, step, same_ref, table_ref, back_ref, scale_ref, filt_ref, x_ref, g_ref,
    dx_ref, dt_ref, spec_ref, grad_ref, out_ref, tap_ref,
):
    spectra_rows(table_ref, x_ref, spec_ref, blocks, rows)
    spectra_rows(table_ref, g_ref, grad_ref, blocks, rows)

    def chunk(index, carry):
        real = pl.ds(pl.multiple_of(index * step, step), step)
        imag = pl.ds(pl.multiple_of(rows + index * step, step), step)
        width = x_ref.shape[1]
        first = (lax.broadcasted_iota(jnp.int32, (step, width), 0) + index * step) == 0
        for j in range(blocks):
            total_real = jnp.zeros((step, width), F32)
            total_imag = jnp.zeros((step, width), F32)
            for lag in range(blocks - j):
                weight = same_ref[j + lag, j]
                fr = filt_ref[lag, real, :]
                fi = filt_ref[lag, imag, :]
                cross = jnp.where(first, 0.0, fi)
                own = jnp.where(first, fi, fr)
                gr = grad_ref[j + lag, real, :] * weight
                gi = grad_ref[j + lag, imag, :] * weight
                total_real = total_real + (fr * gr + cross * gi)
                total_imag = total_imag + (own * gi - cross * gr)
            out_ref[j, real, :] = total_real.astype(BF)
            out_ref[j, imag, :] = total_imag.astype(BF)
        for lag in range(blocks):
            one = jnp.zeros((step, width), F32)
            two = jnp.zeros((step, width), F32)
            three = jnp.zeros((step, width), F32)
            for i in range(lag, blocks):
                weight = same_ref[i, i - lag]
                gr = grad_ref[i, real, :] * weight
                gi = grad_ref[i, imag, :] * weight
                xr = spec_ref[i - lag, real, :]
                xi = spec_ref[i - lag, imag, :]
                one = one + xr * gr
                two = two + xi * gi
                three = three + (xr * gi - xi * gr)
            tap_ref[lag, real, :] = (one + jnp.where(first, 0.0, two)) * scale_ref[real, 0:1]
            tap_ref[lag, imag, :] = jnp.where(first, two, three) * scale_ref[imag, 0:1]
        return carry

    lax.fori_loop(0, rows // step, chunk, 0)
    for block in range(blocks):
        where = pl.ds(block * rows, rows)
        dx_ref[where, :] = jnp.dot(back_ref[...], out_ref[block], preferred_element_type=F32).astype(BF)
        total = tap_ref[block]
        if block + 1 < blocks:
            total = total + scale_ref[:, 1:2] * tap_ref[block + 1]
        dt_ref[where, :] = jnp.dot(back_ref[...], total.astype(BF), preferred_element_type=F32)


VMEM_SPEC = pl.BlockSpec(memory_space=pltpu.VMEM)
SMEM_SPEC = pl.BlockSpec(memory_space=pltpu.SMEM)
KERNEL_BYTES = 48 * 1024 * 1024


def convolve(same, table, back, filt, x_cols, blocks, rows):
    width = x_cols.shape[1]
    return pl.pallas_call(
        functools.partial(convolve_kernel, blocks, rows, min(32, rows)),
        out_shape=jax.ShapeDtypeStruct(x_cols.shape, BF),
        in_specs=[SMEM_SPEC] + [VMEM_SPEC] * 4,
        out_specs=VMEM_SPEC,
        scratch_shapes=[
            pltpu.VMEM((blocks, 2 * rows, width), F32),
            pltpu.VMEM((blocks, 2 * rows, width), BF),
        ],
        compiler_params=pltpu.CompilerParams(vmem_limit_bytes=KERNEL_BYTES),
        name="convolve",
    )(same, table, back, filt, x_cols)


def correlate(same, table, back, scale, filt, x_cols, g_cols, blocks, rows):
    width = x_cols.shape[1]
    return pl.pallas_call(
        functools.partial(correlate_kernel, blocks, rows, min(32, rows)),
        out_shape=(
            jax.ShapeDtypeStruct(x_cols.shape, BF),
            jax.ShapeDtypeStruct(x_cols.shape, F32),
        ),
        in_specs=[SMEM_SPEC] + [VMEM_SPEC] * 6,
        out_specs=(VMEM_SPEC, VMEM_SPEC),
        scratch_shapes=[
            pltpu.VMEM((blocks, 2 * rows, width), F32),
            pltpu.VMEM((blocks, 2 * rows, width), F32),
            pltpu.VMEM((blocks, 2 * rows, width), BF),
            pltpu.VMEM((blocks, 2 * rows, width), F32),
        ],
        compiler_params=pltpu.CompilerParams(vmem_limit_bytes=KERNEL_BYTES),
        name="correlate",
    )(same, table, back, scale, filt, x_cols, g_cols)


def shifted(block, axis, distance):
    devices = range(lax.axis_size(axis))
    route = [(i - distance, i) for i in devices if i - distance in devices]
    return lax.ppermute(block, axis, route)


def swap(block, bit):
    return lax.ppermute(block, "seq", [(i, i ^ bit) for i in range(lax.axis_size("seq"))])


def core_swap(block):
    return lax.ppermute(block, "section", [(0, 1), (1, 0)])


MESH = pl.DeviceIdType.MESH


def shared_rows(rows):
    return rows // 48 * 16 if rows >= 96 else 0


def gather_kernel(sizes, count, *refs):
    total = len(sizes)
    own_refs, out_refs = refs[:total], refs[total : 2 * total]
    send, recv, local = refs[2 * total :]
    core, here, plane = lax.axis_index("section"), lax.axis_index("seq"), lax.axis_index("dp")
    by_x, by_y, far = here + 1 - 2 * (here % 2), (here + 2) % 4, 3 - here
    odd = plane % 2
    to_x, to_y = (core, by_x, plane), (core, by_y, plane)
    to_z, to_core = (core, here, plane + 1 - 2 * odd), (1 - core, here, plane)
    barrier = pltpu.get_barrier_semaphore()
    for target in (to_x, to_y, to_z, to_core):
        pl.semaphore_signal(barrier, inc=1, device_id=target, device_id_type=MESH)
    pl.semaphore_wait(barrier, 4)

    def window(m, block, start, length):
        first = (core * count + block) * sizes[m] + start
        return out_refs[m].at[pl.ds(pl.multiple_of(first, 16), length)]

    def copy(kind, m, source, target_ref, target):
        return pltpu.make_async_remote_copy(
            src_ref=source, dst_ref=target_ref, send_sem=send.at[kind, m], recv_sem=recv.at[kind, m],
            device_id=target, device_id_type=MESH,
        )

    def forward(kind, m, block, start, length, target):
        where = window(m, block, start, length)
        return copy(kind, m, where, where, target)

    started = []

    def go(item):
        item.start()
        started.append(item)
        return item

    def from_own(kind, m, start, length, target):
        source = own_refs[m].at[pl.ds(pl.multiple_of(start, 16), length)]
        return go(copy(kind, m, source, window(m, here, start, length), target))

    kept, thirds, lows, begins = [], [], [], []
    for m in range(total):
        third = shared_rows(sizes[m])
        thirds.append(third)
        begins.append(odd * third)
        lows.append(-(-(sizes[m] - third) // 32) * 16)
    direct, cross, side = {}, {}, {}

    def first_hop(m):
        length = sizes[m] - thirds[m]
        direct[m] = (
            from_own(0, m, begins[m], length, to_x), from_own(1, m, begins[m], length, to_y)
        )

    def given(m):
        return odd * (sizes[m] - thirds[m])

    def second_hop(m):
        length, low = sizes[m] - thirds[m], lows[m]
        direct[m][0].wait_recv()
        low_copy = go(forward(2, m, by_x, begins[m], low, to_y))
        if thirds[m]:
            side[m] = [go(forward(4, m, by_x, given(m), thirds[m], to_z))]
        kept.append(go(forward(7, m, by_x, begins[m], length, to_core)))
        direct[m][1].wait_recv()
        high_copy = go(forward(3, m, by_y, begins[m] + low, length - low, to_x))
        if thirds[m]:
            side[m].append(go(forward(5, m, by_y, given(m), thirds[m], to_z)))
        kept.append(go(forward(8, m, by_y, begins[m], length, to_core)))
        cross[m] = (low_copy, high_copy)

    def third_hop(m):
        length = sizes[m] - thirds[m]
        cross[m][0].wait_recv()
        cross[m][1].wait_recv()
        if thirds[m]:
            side[m].append(go(forward(6, m, far, given(m), thirds[m], to_z)))
        kept.append(go(forward(9, m, far, begins[m], length, to_core)))

    def last_hop(m):
        if thirds[m]:
            missing = (1 - odd) * (sizes[m] - thirds[m])
            for k, block in enumerate((by_x, by_y, far)):
                side[m][k].wait_recv()
                kept.append(go(forward(10 + k, m, block, missing, thirds[m], to_core)))

    first_hop(0)
    first_hop(1)
    locals_ = []
    for m in range(total):
        mine = pltpu.make_async_copy(own_refs[m], window(m, here, 0, sizes[m]), local.at[m])
        mine.start()
        locals_.append(mine)
    for m in range(total):
        second_hop(m)
        if m + 2 < total:
            first_hop(m + 2)
        kept.append(from_own(13, m, 0, sizes[m], to_core))
        if m >= 1:
            third_hop(m - 1)
        if m >= 2:
            last_hop(m - 2)
    third_hop(total - 1)
    for m in range(max(total - 2, 0), total):
        last_hop(m)
    for mine in locals_:
        mine.wait()
    for item in kept:
        item.wait_recv()
    for item in started:
        item.wait_send()


def gather_shards(shards):
    count = lax.axis_size("seq")
    core = lax.axis_index("section")
    if count != 4 or lax.axis_size("dp") % 2:
        result = []
        for shard in shards:
            whole = lax.all_gather(shard, "seq", axis=0, tiled=True)
            other = core_swap(whole)
            low = jnp.where(core == 0, whole, other)
            result.append(jnp.concatenate([low, jnp.where(core == 0, other, whole)], axis=0))
        return result
    sizes = [shard.shape[0] for shard in shards]
    return pl.pallas_call(
        functools.partial(gather_kernel, sizes, count),
        out_shape=[jax.ShapeDtypeStruct((2 * count * a.shape[0], a.shape[1]), a.dtype) for a in shards],
        in_specs=[pl.BlockSpec(memory_space=pl.ANY)] * len(shards),
        out_specs=[pl.BlockSpec(memory_space=pl.ANY)] * len(shards),
        scratch_shapes=[
            pltpu.SemaphoreType.DMA((14, len(shards))),
            pltpu.SemaphoreType.DMA((14, len(shards))),
            pltpu.SemaphoreType.DMA((len(shards),)),
        ],
        compiler_params=pltpu.CompilerParams(collective_id=0, has_side_effects=True),
        name="gather_shards",
    )(*shards)


def core_halves(core, values):
    width = values.shape[1] // 2
    return (
        lax.dynamic_slice_in_dim(values, core * width, width, 1),
        lax.dynamic_slice_in_dim(values, (1 - core) * width, width, 1),
    )


def blocks_by(values, order, axis=1):
    here = lax.axis_index("seq")
    width = values.shape[axis] // 4
    return jnp.concatenate(
        [lax.dynamic_slice_in_dim(values, (here ^ k) * width, width, axis) for k in order], axis=axis
    )


def tied(value, *before):
    for array in before:
        first = array[(0,) * array.ndim].astype(F32)
        value = value + jnp.where(jnp.isnan(first), first, 0.0)
    return value


X_FIRST = (0, 2, 1, 3)
Y_FIRST = (0, 1, 2, 3)


def chip_and_seq_sum(keep, sent, order):
    got = core_swap(sent)
    middle = sent.shape[0] // 2
    near_bit, far_bit = (2, 1) if order == X_FIRST else (1, 2)
    far = (keep(True) + got[middle:].astype(F32)).astype(BF)
    arrived = swap(far, far_bit)
    near = keep(False) + got[:middle].astype(F32) + arrived.astype(F32)
    last = swap(near[middle // 2 :].astype(BF), near_bit)
    return near[: middle // 2] + last.astype(F32), arrived, last


def product_reduce(left, keep, send, order):
    if lax.axis_size("seq") != 4:
        chip = dot_left(left, keep) + core_swap(dot_left(left, send).astype(BF)).astype(F32)
        summed = lax.psum_scatter(chip.astype(BF), "seq", scatter_dimension=0, tiled=True).astype(F32)
        return summed, summed, summed
    left = blocks_by(left, order)
    middle = left.shape[1] // 2

    def kept(far):
        return dot_left(left[:, middle:] if far else left[:, :middle], keep)

    return chip_and_seq_sum(kept, dot_left(left, send).astype(BF), order)


def array_reduce(values, core, order):
    count, rows, width = values.shape
    keep, send = core_halves(core, values.reshape(count * rows, width))
    if count != 4:
        chip = keep + core_swap(send.astype(BF)).astype(F32)
        summed = lax.psum_scatter(chip.astype(BF), "seq", scatter_dimension=0, tiled=True).astype(F32)
        return summed, summed, summed
    keep = blocks_by(keep, order, 0)
    middle = keep.shape[0] // 2
    sent = blocks_by(send, order, 0).astype(BF)
    return chip_and_seq_sum(lambda far: keep[middle:] if far else keep[:middle], sent, order)


def sum_planes(values):
    values = lax.optimization_barrier(values.astype(BF))
    if True:
        return lax.psum(values, "dp")
    place = lax.axis_index("dp")
    inward = lax.ppermute(values, "dp", [(0, 1), (3, 2)])
    pair = lax.optimization_barrier((values.astype(F32) + inward.astype(F32)).astype(BF))
    crossed = lax.ppermute(pair, "dp", [(1, 2), (2, 1)])
    total = lax.optimization_barrier((pair.astype(F32) + crossed.astype(F32)).astype(BF))
    outward = lax.ppermute(total, "dp", [(1, 0), (2, 3)])
    return jnp.where(jnp.logical_or(place == 0, place == 3), outward, total)


def body(
    tokens, out_grad, lengths, ln1_gain, w_in, short_w, filt_in, filt_shift, sine_freq, filt_out,
    decay, filter_bias, w_out, ln2_gain, mlp_up, mlp_down,
):
    micro, rows, width = tokens.shape
    count = lax.axis_size("seq")
    here = lax.axis_index("seq")
    core = lax.axis_index("section")
    slots = rows * count
    col_width = width // count
    hidden = mlp_up.shape[2]
    hidden_block = hidden // count
    half_block = hidden_block // 2
    table_np, weight_np, parity_np = packed_dft(rows)
    table = jnp.asarray(table_np).astype(BF)
    back = jnp.asarray(np.ascontiguousarray(table_np.T)).astype(BF)
    scale = jnp.asarray(np.concatenate([weight_np, parity_np], axis=1))
    embedding = jnp.asarray(positions_embedding(slots, FREQS))

    small = (ln1_gain, short_w, filt_in, filt_shift, sine_freq, filt_out, decay, filter_bias, ln2_gain)
    small_shapes = [a.shape[1:] for a in small]
    small_sizes = [math.prod(s) for s in small_shapes]
    lane = 1024
    packed_rows = -(-sum(small_sizes) // (lane * 16)) * 16
    flat = jnp.concatenate([a.reshape(-1) for a in small])
    flat = jnp.pad(flat, (0, packed_rows * lane - flat.shape[0])).reshape(packed_rows, lane)
    flat_all, out_all, in_all, up_all, down_all = gather_shards([flat, w_out[0], w_in[0], mlp_up[0], mlp_down[0]])
    everywhere = flat_all.reshape(2, count, packed_rows * lane)
    gathered = [
        (
            in_all[layer * width : (layer + 1) * width], out_all[layer * width : (layer + 1) * width],
            up_all[layer * width : (layer + 1) * width], down_all[layer * hidden : (layer + 1) * hidden],
        )
        for layer in range(2)
    ]
    small_axis = (0, 1, 1, 0, 0, 0, 0, 0, 0)

    def small_of(layer):
        found = []
        offset = 0
        for shape, size, axis in zip(small_shapes, small_sizes, small_axis):
            part = everywhere[layer, :, offset : offset + size].reshape((count,) + shape)
            part = jnp.moveaxis(part, 0, axis)
            full = list(shape)
            full[axis] = shape[axis] * count
            found.append(part.reshape(full).astype(F32))
            offset += size
        return found

    length_row = lax.dynamic_index_in_dim(lengths, core, 0, keepdims=False)
    index_all = jnp.arange(count, dtype=jnp.int32)
    started = jnp.logical_and(length_row[None, :] > 0, index_all[None, :] <= index_all[:, None])
    regions = jnp.max(jnp.where(started, index_all[None, :], 0), axis=1)
    doc_length = jnp.sum(jnp.where(regions[:, None] == index_all[None, :], length_row[None, :], 0), axis=1)
    own_region = jnp.sum(jnp.where(index_all == here, regions, 0))
    own_length = jnp.sum(jnp.where(index_all == here, doc_length, 0))
    last_region = jnp.sum(jnp.where(index_all == here - 1, regions, 0))
    offsets = (here - own_region) * rows + jnp.arange(rows, dtype=jnp.int32)
    valid = (offsets < own_length).astype(F32)[:, None]
    carried_on = jnp.logical_and(here > 0, last_region == own_region).astype(F32)
    same = (regions[:, None] == regions[None, :]).astype(F32)

    def to_columns(values):
        return lax.all_to_all(values.astype(BF), "seq", split_axis=1, concat_axis=0, tiled=True)

    def to_rows(values):
        return lax.all_to_all(values, "seq", split_axis=0, concat_axis=1, tiled=True).astype(F32)

    def filter_stage(layer):
        _, _, in_w, shift_w, freq_w, out_w, decay_w, _, _ = small_of(layer)
        out_cols = lax.dynamic_slice_in_dim(out_w, here * col_width, col_width, 1)
        decay_cols = lax.dynamic_slice_in_dim(decay_w, here * col_width, col_width, 0)
        taps, pull = jax.vjp(
            lambda *p: filter_taps(*p, embedding), in_w, shift_w, freq_w, out_cols, decay_cols
        )
        spectra = jnp.einsum(
            "fs,msc->mfc", table, taps.astype(BF).reshape(count, rows, col_width), preferred_element_type=F32
        )
        before = jnp.concatenate([jnp.zeros_like(spectra[:1]), spectra[:-1]], axis=0)
        return (spectra + scale[:, 1:2] * before) * scale[:, 0:1], pull

    def forward(layer_in, layer):
        gain_one, short_weights, _, _, _, _, _, bias, gain_two = small_of(layer)
        in_matrix, out_matrix, up_matrix, down_matrix = gathered[layer]
        filt, pull = filter_stage(layer)
        normed = layer_norm(layer_in, gain_one).astype(BF)
        projected = dot(normed, in_matrix).astype(BF)
        rim = shifted(projected[rows - 2 :], "seq", 1)
        mixed = short_mix(rim.astype(F32), projected.astype(F32), short_weights, carried_on)
        first, second, third = mixed[:, :width], mixed[:, width : 2 * width], mixed[:, 2 * width :]
        signal = first * third
        x_cols = to_columns(signal * valid)
        y_cols = convolve(same, table, back, filt, x_cols, count, rows)
        filtered = to_rows(y_cols) * valid + bias * signal
        gated = (second * filtered).astype(BF)
        residual = layer_in + dot(gated, out_matrix)
        normed_two = layer_norm(residual, gain_two).astype(BF)
        upward = dot(normed_two, up_matrix)
        active = gelu_tanh(upward).astype(BF)
        layer_out = residual + dot(active, down_matrix)
        stored = (
            layer_in, normed, projected, rim, mixed, signal, filtered, gated, residual, normed_two,
            upward, active, x_cols, filt, pull,
        )
        return layer_out.astype(BF), stored

    def backward(upstream, stored, layer, before):
        (
            layer_in, normed, projected, rim, mixed, signal, filtered, gated, residual, normed_two,
            upward, active, x_cols, filt, pull,
        ) = stored
        gain_one, short_weights, in_w, shift_w, freq_w, out_w, decay_w, bias, gain_two = small_of(layer)
        in_matrix, out_matrix, up_matrix, down_matrix = gathered[layer]
        upstream_keep, upstream_send = core_halves(core, upstream)
        grad_hidden = jax.vjp(gelu_tanh, upward)[1](dot_right(upstream, down_matrix))[0].astype(BF)
        hidden_keep, hidden_send = core_halves(core, grad_hidden)
        grad_down = product_reduce(active, upstream_keep, upstream_send, Y_FIRST)
        grad_up = product_reduce(normed_two, hidden_keep, hidden_send, X_FIRST)
        grad_norm_two = dot_right(grad_hidden, up_matrix)
        grad_resid_norm, grad_gain_two = jax.vjp(layer_norm, residual, gain_two)[1](grad_norm_two)
        grad_residual = upstream.astype(F32) + grad_resid_norm
        grad_branch = tied(grad_residual, *before[0]).astype(BF)
        branch_keep, branch_send = core_halves(core, grad_branch)
        grad_out = product_reduce(gated, branch_keep, branch_send, X_FIRST)
        grad_gated = dot_right(grad_branch, out_matrix)
        first, second, third = mixed[:, :width], mixed[:, width : 2 * width], mixed[:, 2 * width :]
        grad_second = grad_gated * filtered
        grad_filtered = grad_gated * second
        grad_bias = jnp.sum(grad_filtered * signal, axis=0)
        g_cols = to_columns(grad_filtered * valid)
        dx_cols, grad_taps = correlate(same, table, back, scale, filt, x_cols, g_cols, count, rows)
        grad_signal = to_rows(dx_cols) * valid + bias * grad_filtered
        grad_mixed = jnp.concatenate([grad_signal * third, grad_second, grad_signal * first], axis=1)
        short_pull = jax.vjp(
            lambda a, b, c: short_mix(a, b, c, carried_on), rim.astype(F32), projected.astype(F32), short_weights
        )[1]
        grad_rim, grad_proj, grad_short = short_pull(grad_mixed)
        returned = shifted(grad_rim, "seq", -1)
        tail = grad_proj[rows - 2 :] + returned
        grad_proj = jnp.concatenate([grad_proj[: rows - 2], tail], axis=0)
        grad_proj = tied(grad_proj, *before[1]).astype(BF)
        proj_keep, proj_send = core_halves(core, grad_proj)
        half = proj_keep.shape[1] // 2
        grad_in_low = product_reduce(normed, proj_keep[:, :half], proj_send[:, :half], X_FIRST)
        grad_in_high = product_reduce(normed, proj_keep[:, half:], proj_send[:, half:], Y_FIRST)
        grad_normed = dot_right(grad_proj, in_matrix)
        grad_norm_in, grad_gain_one = jax.vjp(layer_norm, layer_in, gain_one)[1](grad_normed)
        grad_layer_in = grad_residual + grad_norm_in
        d_in, d_shift, d_freq, d_out_cols, d_decay_cols = pull(grad_taps)
        d_out = lax.dynamic_update_slice_in_dim(jnp.zeros_like(out_w), d_out_cols, here * col_width, 1)
        d_decay = lax.dynamic_update_slice_in_dim(jnp.zeros_like(decay_w), d_decay_cols, here * col_width, 0)
        small_grads = (
            grad_gain_one, grad_short, d_in, d_shift, d_freq, d_out, d_decay, grad_bias, grad_gain_two
        )
        parts = []
        for grad, shape, axis in zip(small_grads, small_shapes, small_axis):
            split = list(grad.shape)
            split[axis : axis + 1] = [count, shape[axis]]
            parts.append(jnp.moveaxis(grad.reshape(split), axis, 0).reshape(count, -1))
        packed = jnp.concatenate(parts, axis=1)
        packed = jnp.pad(packed, ((0, 0), (0, packed_rows * lane - packed.shape[1])))
        grad_small = array_reduce(packed.reshape(count, packed_rows, lane), core, Y_FIRST)
        return grad_layer_in, (grad_small, grad_in_low, grad_in_high, grad_out, grad_up, grad_down)

    def row_of(values):
        return lax.dynamic_index_in_dim(values, core, 0, keepdims=False)

    out_first, stored_first = forward(row_of(tokens).astype(F32), 0)
    out_second, stored_second = forward(out_first.astype(F32), 1)
    grad_second, sums_second = backward(row_of(out_grad), stored_second, 1, ((), ()))
    small_two, in_low_two, in_high_two, out_two, up_two, down_two = sums_second
    grad_second = tied(grad_second, up_two[1], down_two[1]).astype(BF)
    mlp_two = [lax.psum(part[0].astype(BF), "dp") for part in (up_two, down_two)]
    before = ((up_two[2], down_two[2], in_low_two[1], in_high_two[1]), tuple(mlp_two))
    grad_first, sums_first = backward(grad_second, stored_first, 0, before)
    grad_first = grad_first.astype(BF)
    summed = [[sum_planes(part[0]) for part in sums] for sums in (sums_first, sums_second)]
    summed[1][4:] = mlp_two

    def both_rows(of_first, of_second):
        kept = jnp.where(core == 0, of_first, of_second)
        received = core_swap(jnp.where(core == 0, of_second, of_first))
        return jnp.stack([jnp.where(core == 0, kept, received), jnp.where(core == 0, received, kept)])[None]

    layer_outputs = both_rows(out_first, out_second)
    input_grads = both_rows(grad_first, grad_second)

    def finish(index, join):
        whole = []
        for layer, sums in enumerate(summed):
            own = sums[index]
            received = lax.ppermute(own, "section", [(1 - layer, layer)])
            whole.append(join(own, received) if layer == 0 else join(received, own))
        return jnp.where(core == 0, whole[0], whole[1]).astype(F32)

    def side_by_side(low, high):
        return jnp.concatenate([low, high], axis=1)

    def finish_in():
        whole = []
        for layer, sums in enumerate(summed):
            own = jnp.concatenate(sums[1:3], axis=1)
            received = lax.ppermute(own, "section", [(1 - layer, layer)])
            whole.append(side_by_side(own, received) if layer == 0 else side_by_side(received, own))
        return jnp.where(core == 0, whole[0], whole[1]).astype(F32)

    small_total = finish(0, side_by_side).reshape(-1)
    grad_in = finish_in()
    grad_out = finish(3, side_by_side)
    grad_up = finish(4, side_by_side)
    grad_down = finish(5, side_by_side)
    small_out = []
    offset = 0
    for shape, size in zip(small_shapes, small_sizes):
        small_out.append(small_total[offset : offset + size].reshape((1,) + shape))
        offset += size
    g_ln1, g_short, g_fin, g_shift, g_freq, g_fout, g_decay, g_bias, g_ln2 = small_out
    return (
        layer_outputs, input_grads, g_ln1, grad_in[None], g_short, g_fin, g_shift, g_freq, g_fout, g_decay, g_bias,
        grad_out[None], g_ln2, grad_up[None], grad_down[None],
    )


def solution(mesh):
    vector = P("section", "seq")
    matrix = P("section", "seq", None)
    last = P("section", None, "seq")
    tokens = P("dp", "seq", None)
    outputs = P("section", "dp", "seq", None)
    in_specs = (
        tokens, tokens, P("dp", None), vector, matrix, last, last, vector, vector, matrix, vector, vector, matrix,
        vector, matrix, matrix,
    )
    out_specs = (
        outputs, outputs, vector, matrix, last, last, vector, vector, matrix, vector, vector, matrix, vector, matrix,
        matrix,
    )
    return jax.shard_map(body, mesh=mesh, in_specs=in_specs, out_specs=out_specs, check_vma=False)
```

```python
import functools
import math

import jax
import jax.numpy as jnp
import numpy as np
from jax import lax
from jax.experimental import pallas as pl
from jax.experimental.pallas import tpu as pltpu
from jax.sharding import PartitionSpec as P

FREQS = 16
PRECISE = lax.Precision.HIGHEST
EPSILON = 1e-05
BF = jnp.bfloat16
F32 = jnp.float32


def dot(left, right):
    return jnp.dot(left, right, preferred_element_type=F32)


def dot_left(left, right):
    return lax.dot_general(left, right, (((0,), (0,)), ((), ())), preferred_element_type=F32)


def dot_right(left, right):
    return lax.dot_general(left, right, (((1,), (1,)), ((), ())), preferred_element_type=F32)


def layer_norm(values, gains):
    row_mean = jnp.mean(values, axis=-1, keepdims=True)
    centered = values - row_mean
    variance = jnp.mean(centered * centered, axis=-1, keepdims=True)
    return centered * lax.rsqrt(variance + EPSILON) * gains


def gelu_tanh(values):
    return jax.nn.gelu(values, approximate=True)


def positions_embedding(slots, harmonic_count):
    steps_all = np.arange(slots)
    scaled = steps_all / slots
    harmonics = np.arange(1, harmonic_count + 1)
    phase = (steps_all[:, None] * harmonics[None, :] % slots) * (2.0 * math.pi / slots)
    both = np.concatenate([scaled[:, None], np.cos(phase), np.sin(phase)], axis=1)
    return both.astype(np.float32)


def filter_taps(filt_in, filt_shift, sine_freq, filt_out, decay, embedding):
    slots = embedding.shape[0]
    inner = jnp.dot(embedding, filt_in, preferred_element_type=F32, precision=PRECISE)
    hidden_sine = jnp.sin(sine_freq * (inner + filt_shift))
    scaled = jnp.arange(slots, dtype=jnp.int32).astype(F32) / slots
    summed = jnp.dot(hidden_sine, filt_out, preferred_element_type=F32, precision=PRECISE)
    return summed * jnp.exp(-decay[None, :] * scaled[:, None])


def short_mix(rim_values, proj_values, weight_values, carried_on):
    total_rows = proj_values.shape[0]
    extended = jnp.concatenate([rim_values * carried_on, proj_values], axis=0)
    return (
        weight_values[0] * extended[2:]
        + weight_values[1] * extended[1 : total_rows + 1]
        + weight_values[2] * extended[:total_rows]
    )


def packed_dft(rows):
    size = 2 * rows
    phase = (np.arange(rows)[:, None] * np.arange(rows)[None, :] % size) * (2.0 * math.pi / size)
    lower = -np.sin(phase)
    lower[0] = 1 - 2 * (np.arange(rows) % 2)
    table = np.concatenate([np.cos(phase), lower], axis=0)
    weight = np.full((size, 1), 2.0 / size)
    weight[0] = weight[rows] = 1.0 / size
    parity = 1.0 - 2.0 * (np.arange(rows) % 2)
    parity = np.concatenate([parity, parity])[:, None]
    parity[rows] = 1 - 2 * (rows % 2)
    return table.astype(np.float32), weight.astype(np.float32), parity.astype(np.float32)


def spectra_rows(table_ref, source_ref, target_ref, blocks, rows):
    for block in range(blocks):
        target_ref[block] = jnp.dot(
            table_ref[...], source_ref[pl.ds(block * rows, rows), :], preferred_element_type=F32
        )


def convolve_kernel(blocks, rows, step, same_ref, table_ref, back_ref, filt_ref, x_ref, y_ref, spec_ref, out_ref):
    spectra_rows(table_ref, x_ref, spec_ref, blocks, rows)

    def chunk(index, carry):
        real = pl.ds(pl.multiple_of(index * step, step), step)
        imag = pl.ds(pl.multiple_of(rows + index * step, step), step)
        width = x_ref.shape[1]
        first = (lax.broadcasted_iota(jnp.int32, (step, width), 0) + index * step) == 0
        for i in range(blocks):
            total_real = jnp.zeros((step, width), F32)
            total_imag = jnp.zeros((step, width), F32)
            for lag in range(i + 1):
                weight = same_ref[i, i - lag]
                fr = filt_ref[lag, real, :]
                fi = filt_ref[lag, imag, :]
                cross = jnp.where(first, 0.0, fi)
                own = jnp.where(first, fi, fr)
                xr = spec_ref[i - lag, real, :] * weight
                xi = spec_ref[i - lag, imag, :] * weight
                total_real = total_real + (fr * xr - cross * xi)
                total_imag = total_imag + (cross * xr + own * xi)
            out_ref[i, real, :] = total_real.astype(BF)
            out_ref[i, imag, :] = total_imag.astype(BF)
        return carry

    lax.fori_loop(0, rows // step, chunk, 0)
    for block in range(blocks):
        y_ref[pl.ds(block * rows, rows), :] = jnp.dot(
            back_ref[...], out_ref[block], preferred_element_type=F32
        ).astype(BF)


def correlate_kernel(
    blocks, rows, step, same_ref, table_ref, back_ref, scale_ref, filt_ref, x_ref, g_ref,
    dx_ref, dt_ref, spec_ref, grad_ref, out_ref, tap_ref,
):
    spectra_rows(table_ref, x_ref, spec_ref, blocks, rows)
    spectra_rows(table_ref, g_ref, grad_ref, blocks, rows)

    def chunk(index, carry):
        real = pl.ds(pl.multiple_of(index * step, step), step)
        imag = pl.ds(pl.multiple_of(rows + index * step, step), step)
        width = x_ref.shape[1]
        first = (lax.broadcasted_iota(jnp.int32, (step, width), 0) + index * step) == 0
        for j in range(blocks):
            total_real = jnp.zeros((step, width), F32)
            total_imag = jnp.zeros((step, width), F32)
            for lag in range(blocks - j):
                weight = same_ref[j + lag, j]
                fr = filt_ref[lag, real, :]
                fi = filt_ref[lag, imag, :]
                cross = jnp.where(first, 0.0, fi)
                own = jnp.where(first, fi, fr)
                gr = grad_ref[j + lag, real, :] * weight
                gi = grad_ref[j + lag, imag, :] * weight
                total_real = total_real + (fr * gr + cross * gi)
                total_imag = total_imag + (own * gi - cross * gr)
            out_ref[j, real, :] = total_real.astype(BF)
            out_ref[j, imag, :] = total_imag.astype(BF)
        for lag in range(blocks):
            one = jnp.zeros((step, width), F32)
            two = jnp.zeros((step, width), F32)
            three = jnp.zeros((step, width), F32)
            for i in range(lag, blocks):
                weight = same_ref[i, i - lag]
                gr = grad_ref[i, real, :] * weight
                gi = grad_ref[i, imag, :] * weight
                xr = spec_ref[i - lag, real, :]
                xi = spec_ref[i - lag, imag, :]
                one = one + xr * gr
                two = two + xi * gi
                three = three + (xr * gi - xi * gr)
            tap_ref[lag, real, :] = (one + jnp.where(first, 0.0, two)) * scale_ref[real, 0:1]
            tap_ref[lag, imag, :] = jnp.where(first, two, three) * scale_ref[imag, 0:1]
        return carry

    lax.fori_loop(0, rows // step, chunk, 0)
    for block in range(blocks):
        where = pl.ds(block * rows, rows)
        dx_ref[where, :] = jnp.dot(back_ref[...], out_ref[block], preferred_element_type=F32).astype(BF)
        total = tap_ref[block]
        if block + 1 < blocks:
            total = total + scale_ref[:, 1:2] * tap_ref[block + 1]
        dt_ref[where, :] = jnp.dot(back_ref[...], total.astype(BF), preferred_element_type=F32)


VMEM_SPEC = pl.BlockSpec(memory_space=pltpu.VMEM)
SMEM_SPEC = pl.BlockSpec(memory_space=pltpu.SMEM)
KERNEL_BYTES = 48 * 1024 * 1024


def convolve(same, table, back, filt, x_cols, blocks, rows):
    width = x_cols.shape[1]
    return pl.pallas_call(
        functools.partial(convolve_kernel, blocks, rows, min(32, rows)),
        out_shape=jax.ShapeDtypeStruct(x_cols.shape, BF),
        in_specs=[SMEM_SPEC] + [VMEM_SPEC] * 4,
        out_specs=VMEM_SPEC,
        scratch_shapes=[
            pltpu.VMEM((blocks, 2 * rows, width), F32),
            pltpu.VMEM((blocks, 2 * rows, width), BF),
        ],
        compiler_params=pltpu.CompilerParams(vmem_limit_bytes=KERNEL_BYTES),
        name="convolve",
    )(same, table, back, filt, x_cols)


def correlate(same, table, back, scale, filt, x_cols, g_cols, blocks, rows):
    width = x_cols.shape[1]
    return pl.pallas_call(
        functools.partial(correlate_kernel, blocks, rows, min(32, rows)),
        out_shape=(
            jax.ShapeDtypeStruct(x_cols.shape, BF),
            jax.ShapeDtypeStruct(x_cols.shape, F32),
        ),
        in_specs=[SMEM_SPEC] + [VMEM_SPEC] * 6,
        out_specs=(VMEM_SPEC, VMEM_SPEC),
        scratch_shapes=[
            pltpu.VMEM((blocks, 2 * rows, width), F32),
            pltpu.VMEM((blocks, 2 * rows, width), F32),
            pltpu.VMEM((blocks, 2 * rows, width), BF),
            pltpu.VMEM((blocks, 2 * rows, width), F32),
        ],
        compiler_params=pltpu.CompilerParams(vmem_limit_bytes=KERNEL_BYTES),
        name="correlate",
    )(same, table, back, scale, filt, x_cols, g_cols)


def shifted(block, axis, distance):
    devices = range(lax.axis_size(axis))
    route = [(i - distance, i) for i in devices if i - distance in devices]
    return lax.ppermute(block, axis, route)


def core_swap(block):
    return lax.ppermute(block, "section", [(0, 1), (1, 0)])


MESH = pl.DeviceIdType.MESH


def shared_rows(rows):
    return rows // 48 * 16 if rows >= 96 else 0


def gather_kernel(sizes, count, *refs):
    total = len(sizes)
    own_refs, out_refs = refs[:total], refs[total : 2 * total]
    send, recv, local = refs[2 * total :]
    core, here, plane = lax.axis_index("section"), lax.axis_index("seq"), lax.axis_index("dp")
    by_x, by_y, far = here + 1 - 2 * (here % 2), (here + 2) % 4, 3 - here
    odd = plane % 2
    to_x, to_y = (core, by_x, plane), (core, by_y, plane)
    to_z, to_core = (core, here, plane + 1 - 2 * odd), (1 - core, here, plane)
    barrier = pltpu.get_barrier_semaphore()
    for target in (to_x, to_y, to_z, to_core):
        pl.semaphore_signal(barrier, inc=1, device_id=target, device_id_type=MESH)
    pl.semaphore_wait(barrier, 4)

    def window(m, block, start, length):
        first = (core * count + block) * sizes[m] + start
        return out_refs[m].at[pl.ds(pl.multiple_of(first, 16), length)]

    def copy(kind, m, source, target_ref, target):
        return pltpu.make_async_remote_copy(
            src_ref=source, dst_ref=target_ref, send_sem=send.at[kind, m], recv_sem=recv.at[kind, m],
            device_id=target, device_id_type=MESH,
        )

    def forward(kind, m, block, start, length, target):
        where = window(m, block, start, length)
        return copy(kind, m, where, where, target)

    started = []

    def go(item):
        item.start()
        started.append(item)
        return item

    def from_own(kind, m, start, length, target):
        source = own_refs[m].at[pl.ds(pl.multiple_of(start, 16), length)]
        return go(copy(kind, m, source, window(m, here, start, length), target))

    kept, thirds, lows, begins = [], [], [], []
    for m in range(total):
        third = shared_rows(sizes[m])
        thirds.append(third)
        begins.append(odd * third)
        lows.append(-(-(sizes[m] - third) // 32) * 16)
    direct, cross, side = {}, {}, {}

    def first_hop(m):
        length = sizes[m] - thirds[m]
        direct[m] = (
            from_own(0, m, begins[m], length, to_x), from_own(1, m, begins[m], length, to_y)
        )

    def given(m):
        return odd * (sizes[m] - thirds[m])

    def second_hop(m):
        length, low = sizes[m] - thirds[m], lows[m]
        direct[m][0].wait_recv()
        low_copy = go(forward(2, m, by_x, begins[m], low, to_y))
        if thirds[m]:
            side[m] = [go(forward(4, m, by_x, given(m), thirds[m], to_z))]
        kept.append(go(forward(7, m, by_x, begins[m], length, to_core)))
        direct[m][1].wait_recv()
        high_copy = go(forward(3, m, by_y, begins[m] + low, length - low, to_x))
        if thirds[m]:
            side[m].append(go(forward(5, m, by_y, given(m), thirds[m], to_z)))
        kept.append(go(forward(8, m, by_y, begins[m], length, to_core)))
        cross[m] = (low_copy, high_copy)

    def third_hop(m):
        length = sizes[m] - thirds[m]
        cross[m][0].wait_recv()
        cross[m][1].wait_recv()
        if thirds[m]:
            side[m].append(go(forward(6, m, far, given(m), thirds[m], to_z)))
        kept.append(go(forward(9, m, far, begins[m], length, to_core)))

    def last_hop(m):
        if thirds[m]:
            missing = (1 - odd) * (sizes[m] - thirds[m])
            for k, block in enumerate((by_x, by_y, far)):
                side[m][k].wait_recv()
                kept.append(go(forward(10 + k, m, block, missing, thirds[m], to_core)))

    first_hop(0)
    first_hop(1)
    locals_ = []
    for m in range(total):
        mine = pltpu.make_async_copy(own_refs[m], window(m, here, 0, sizes[m]), local.at[m])
        mine.start()
        locals_.append(mine)
    for m in range(total):
        second_hop(m)
        if m + 2 < total:
            first_hop(m + 2)
        kept.append(from_own(13, m, 0, sizes[m], to_core))
        if m >= 1:
            third_hop(m - 1)
        if m >= 2:
            last_hop(m - 2)
    third_hop(total - 1)
    for m in range(max(total - 2, 0), total):
        last_hop(m)
    for mine in locals_:
        mine.wait()
    for item in kept:
        item.wait_recv()
    for item in started:
        item.wait_send()


def gather_shards(shards):
    count = lax.axis_size("seq")
    core = lax.axis_index("section")
    if count != 4 or lax.axis_size("dp") % 2:
        result = []
        for shard in shards:
            whole = lax.all_gather(shard, "seq", axis=0, tiled=True)
            other = core_swap(whole)
            low = jnp.where(core == 0, whole, other)
            result.append(jnp.concatenate([low, jnp.where(core == 0, other, whole)], axis=0))
        return result
    sizes = [shard.shape[0] for shard in shards]
    return pl.pallas_call(
        functools.partial(gather_kernel, sizes, count),
        out_shape=[jax.ShapeDtypeStruct((2 * count * a.shape[0], a.shape[1]), a.dtype) for a in shards],
        in_specs=[pl.BlockSpec(memory_space=pl.ANY)] * len(shards),
        out_specs=[pl.BlockSpec(memory_space=pl.ANY)] * len(shards),
        scratch_shapes=[
            pltpu.SemaphoreType.DMA((14, len(shards))),
            pltpu.SemaphoreType.DMA((14, len(shards))),
            pltpu.SemaphoreType.DMA((len(shards),)),
        ],
        compiler_params=pltpu.CompilerParams(collective_id=0, has_side_effects=True),
        name="gather_shards",
    )(*shards)


def core_halves(core, values):
    width = values.shape[1] // 2
    return (
        lax.dynamic_slice_in_dim(values, core * width, width, 1),
        lax.dynamic_slice_in_dim(values, (1 - core) * width, width, 1),
    )


X_FIRST = (0, 2, 1, 3)
Y_FIRST = (0, 1, 2, 3)


def reduce_kernel(items, halves, planes, *refs):
    total = len(items)
    sides = len(halves) * 2 + 1
    inputs, refs = refs[:sides], refs[sides:]
    own_out, refs = refs[:total], refs[total:]
    other_out, refs = (refs[:total], refs[total:]) if planes else (own_out, refs)
    hold, inbox, far_in, near_in, plane_in, cross_in, refs = (
        refs[:total], refs[total : 2 * total], refs[2 * total : 3 * total], refs[3 * total : 4 * total],
        refs[4 * total : 5 * total], refs[5 * total : 6 * total], refs[6 * total :],
    )
    send, recv, local = refs
    core, here, plane = lax.axis_index("section"), lax.axis_index("seq"), lax.axis_index("dp")
    by_x, by_y, far = here + 1 - 2 * (here % 2), (here + 2) % 4, 3 - here
    to_x, to_y, to_core = (core, by_x, plane), (core, by_y, plane), (1 - core, here, plane)
    to_inner = (core, here, (plane + 3) // 3)
    to_outer = (core, here, 3 * (plane // 2))
    to_cross = (core, here, 3 - plane)
    outer = jnp.logical_or(plane == 0, plane == 3)
    inner = jnp.logical_and(plane > 0, plane < 3)

    barrier = pltpu.get_barrier_semaphore()

    def greet(target):
        pl.semaphore_signal(barrier, inc=1, device_id=target, device_id_type=MESH)

    for target in (to_x, to_y, to_core):
        greet(target)
    if planes:

        @pl.when(outer)
        def _():
            greet(to_inner)
            pl.semaphore_wait(barrier, 4)

        @pl.when(inner)
        def _():
            greet(to_outer)
            greet(to_cross)
            pl.semaphore_wait(barrier, 5)
    else:
        pl.semaphore_wait(barrier, 3)

    def copy(kind, m, source, target_ref, target):
        return pltpu.make_async_remote_copy(
            src_ref=source, dst_ref=target_ref, send_sem=send.at[kind, m], recv_sem=recv.at[kind, m],
            device_id=target, device_id_type=MESH,
        )

    def rows_of(ref, m, slot, slots=1):
        rows = items[m][0]
        return ref[m].at[pl.ds(slot * rows, slots * rows)]

    def copies(m):
        along_x = items[m][5] == X_FIRST
        return dict(
            core=lambda: copy(0, m, hold[m], inbox[m], to_core),
            far=lambda: copy(1, m, rows_of(hold, m, 2, 2), far_in[m], to_x if along_x else to_y),
            near=lambda: copy(2, m, rows_of(hold, m, 1), near_in[m], to_y if along_x else to_x),
            inward=lambda: copy(3, m, rows_of(hold, m, 0), plane_in[m], to_inner),
            cross=lambda: copy(4, m, rows_of(hold, m, 0), cross_in[m], to_cross),
            outward=lambda: copy(3, m, rows_of(hold, m, 0), plane_in[m], to_outer),
            last_held=lambda: copy(5, m, rows_of(hold, m, 0), other_out[m], to_core),
            last_got=lambda: copy(5, m, plane_in[m], other_out[m], to_core),
            held=lambda: pltpu.make_async_copy(rows_of(hold, m, 0), own_out[m], local.at[m]),
            got=lambda: pltpu.make_async_copy(plane_in[m], own_out[m], local.at[m]),
        )

    moves = [copies(m) for m in range(total)]

    def fill(m, slot, side, adds):
        rows, columns, left, right, first, order = items[m]
        block = {0: here, 1: by_x, 2: by_y, 3: far}[order[slot]]
        high, wide = min(rows, 256), columns if columns <= 768 else 512
        across = columns // wide
        start = side * halves[right] + first if right >= 0 else side * columns

        def step(index, carry):
            down, along = index // across, index % across
            picked = pl.ds(pl.multiple_of(block * rows + down * high, 16), high)
            which = pl.ds(pl.multiple_of(start + along * wide, 128), wide)
            if right >= 0:
                value = jnp.dot(
                    inputs[left][picked, :], inputs[len(halves) + right][:, which], preferred_element_type=F32
                )
            else:
                value = inputs[-1][picked, which]
            where = pl.ds(pl.multiple_of(along * wide, 128), wide)
            for ref, base in adds:
                value = value + ref[m][pl.ds(pl.multiple_of(base * rows + down * high, 16), high), where].astype(F32)
            hold[m][pl.ds(pl.multiple_of(slot * rows + down * high, 16), high), where] = value.astype(BF)
            return carry

        lax.fori_loop(0, rows // high * across, step, 0)

    def add_plane(m, ref):
        rows = items[m][0]
        high = min(rows, 64)

        def step(index, carry):
            where = pl.ds(pl.multiple_of(index * high, 16), high)
            value = hold[m][where, :].astype(F32) + ref[m][where, :].astype(F32)
            hold[m][where, :] = value.astype(BF)
            return carry

        lax.fori_loop(0, rows // high, step, 0)

    def to_other_core(m):
        for slot in (2, 3, 1, 0):
            fill(m, slot, 1 - core, [])
        moves[m]["core"]().start()

    def first_hop(m):
        moves[m]["core"]().wait()
        for slot in (2, 3):
            fill(m, slot, core, [(inbox, slot)])
        moves[m]["far"]().start()

    def second_hop(m):
        moves[m]["far"]().wait_recv()
        fill(m, 1, core, [(inbox, 1), (far_in, 1)])
        moves[m]["near"]().start()

    def arrive(m):
        moves[m]["near"]().wait_recv()
        fill(m, 0, core, [(inbox, 0), (far_in, 0), (near_in, 0)])
        if planes:

            @pl.when(outer)
            def _():
                moves[m]["inward"]().start()
        else:
            moves[m]["held"]().start()

    def meet(m):
        @pl.when(inner)
        def _():
            moves[m]["inward"]().wait_recv()
            add_plane(m, plane_in)
            moves[m]["cross"]().start()

    def settle(m):
        @pl.when(inner)
        def _():
            moves[m]["cross"]().wait()
            add_plane(m, cross_in)
            moves[m]["outward"]().start()
            moves[m]["last_held"]().start()
            moves[m]["held"]().start()

    def finish(m):
        @pl.when(outer)
        def _():
            moves[m]["inward"]().wait()
            moves[m]["last_got"]().start()
            moves[m]["got"]().start()

    stages = [to_other_core, first_hop, second_hop, arrive]
    if planes:
        stages = stages + [meet, settle, finish]
    for when in range(total // 2 + len(stages) - 1):
        for number in reversed(range(len(stages))):
            pair = when - number
            if 0 <= pair < total // 2:
                stages[number](2 * pair)
                stages[number](2 * pair + 1)

    for m in range(total):
        moves[m]["far"]().wait_send()
        moves[m]["near"]().wait_send()
        if planes:

            @pl.when(inner)
            def _():
                moves[m]["outward"]().wait_send()
                moves[m]["last_held"]().wait()
                moves[m]["held"]().wait()

            @pl.when(outer)
            def _():
                moves[m]["last_got"]().wait()
                moves[m]["got"]().wait()
        else:
            moves[m]["held"]().wait()


def reduce_layer(lefts, rights, packed, planes, number):
    count = lax.axis_size("seq")
    halves = [right.shape[1] // 2 for right in rights]
    small_rows, small_width = packed.shape[0] // count, packed.shape[1] // 2
    up, down, enter, leave = (left.shape[0] // count for left in lefts)
    items = [
        (leave, halves[3], 3, 3, 0, X_FIRST),
        (small_rows, small_width, -1, -1, 0, Y_FIRST),
        (enter, halves[2] // 2, 2, 2, 0, X_FIRST),
        (enter, halves[2] // 2, 2, 2, halves[2] // 2, Y_FIRST),
        (up, halves[0] // 2, 0, 0, 0, X_FIRST),
        (down, halves[1] // 2, 1, 1, 0, Y_FIRST),
        (up, halves[0] // 2, 0, 0, halves[0] // 2, X_FIRST),
        (down, halves[1] // 2, 1, 1, halves[1] // 2, Y_FIRST),
    ]
    shapes = [jax.ShapeDtypeStruct((item[0], item[1]), BF) for item in items]

    def buffers(slots):
        return [pltpu.VMEM((slots * item[0], item[1]), BF) for item in items]

    hbm = pl.BlockSpec(memory_space=pl.ANY)
    total = len(items)
    outs = 2 if planes else 1
    result = pl.pallas_call(
        functools.partial(reduce_kernel, items, halves, planes),
        out_shape=shapes * outs,
        in_specs=[VMEM_SPEC] * (2 * len(lefts) + 1),
        out_specs=[hbm] * (outs * total),
        scratch_shapes=buffers(4) + buffers(4) + buffers(2) + buffers(1) + buffers(1) + buffers(1)
        + [pltpu.SemaphoreType.DMA((6, total)), pltpu.SemaphoreType.DMA((6, total)), pltpu.SemaphoreType.DMA((total,))],
        compiler_params=pltpu.CompilerParams(
            collective_id=number, has_side_effects=True, vmem_limit_bytes=58 * 1024 * 1024
        ),
        name="reduce_layer",
    )(*lefts, *rights, packed)
    joined = []
    for part in range(outs):
        out, small, in_low, in_high, up_low, down_low, up_high, down_high = result[part * total : (part + 1) * total]
        pairs = ((up_low, up_high), (down_low, down_high), (in_low, in_high))
        joined.append([jnp.concatenate(pair, axis=1) for pair in pairs] + [out, small])
    return joined


def reduce_plain(lefts, rights, packed, core):
    own = []
    for left, right in [*zip(lefts, rights), (None, packed)]:
        full = right if left is None else dot(left, right)
        keep, send = core_halves(core, full.astype(BF))
        chip = (keep.astype(F32) + core_swap(send).astype(F32)).astype(BF)
        summed = lax.psum_scatter(chip, "seq", scatter_dimension=0, tiled=True)
        own.append(lax.psum(summed, "dp"))
    return own


def body(
    tokens, out_grad, lengths, ln1_gain, w_in, short_w, filt_in, filt_shift, sine_freq, filt_out,
    decay, filter_bias, w_out, ln2_gain, mlp_up, mlp_down,
):
    micro, rows, width = tokens.shape
    count = lax.axis_size("seq")
    here = lax.axis_index("seq")
    core = lax.axis_index("section")
    slots = rows * count
    col_width = width // count
    hidden = mlp_up.shape[2]
    hidden_block = hidden // count
    half_block = hidden_block // 2
    table_np, weight_np, parity_np = packed_dft(rows)
    table = jnp.asarray(table_np).astype(BF)
    back = jnp.asarray(np.ascontiguousarray(table_np.T)).astype(BF)
    scale = jnp.asarray(np.concatenate([weight_np, parity_np], axis=1))
    embedding = jnp.asarray(positions_embedding(slots, FREQS))

    small = (ln1_gain, short_w, filt_in, filt_shift, sine_freq, filt_out, decay, filter_bias, ln2_gain)
    small_shapes = [a.shape[1:] for a in small]
    small_sizes = [math.prod(s) for s in small_shapes]
    lane = 1024
    packed_rows = -(-sum(small_sizes) // (lane * 16)) * 16
    flat = jnp.concatenate([a.reshape(-1) for a in small])
    flat = jnp.pad(flat, (0, packed_rows * lane - flat.shape[0])).reshape(packed_rows, lane)
    flat_all, out_all, in_all, up_all, down_all = gather_shards([flat, w_out[0], w_in[0], mlp_up[0], mlp_down[0]])
    everywhere = flat_all.reshape(2, count, packed_rows * lane)
    gathered = [
        (
            in_all[layer * width : (layer + 1) * width], out_all[layer * width : (layer + 1) * width],
            up_all[layer * width : (layer + 1) * width], down_all[layer * hidden : (layer + 1) * hidden],
        )
        for layer in range(2)
    ]
    small_axis = (0, 1, 1, 0, 0, 0, 0, 0, 0)

    def small_of(layer):
        found = []
        offset = 0
        for shape, size, axis in zip(small_shapes, small_sizes, small_axis):
            part = everywhere[layer, :, offset : offset + size].reshape((count,) + shape)
            part = jnp.moveaxis(part, 0, axis)
            full = list(shape)
            full[axis] = shape[axis] * count
            found.append(part.reshape(full).astype(F32))
            offset += size
        return found

    length_row = lax.dynamic_index_in_dim(lengths, core, 0, keepdims=False)
    index_all = jnp.arange(count, dtype=jnp.int32)
    started = jnp.logical_and(length_row[None, :] > 0, index_all[None, :] <= index_all[:, None])
    regions = jnp.max(jnp.where(started, index_all[None, :], 0), axis=1)
    doc_length = jnp.sum(jnp.where(regions[:, None] == index_all[None, :], length_row[None, :], 0), axis=1)
    own_region = jnp.sum(jnp.where(index_all == here, regions, 0))
    own_length = jnp.sum(jnp.where(index_all == here, doc_length, 0))
    last_region = jnp.sum(jnp.where(index_all == here - 1, regions, 0))
    offsets = (here - own_region) * rows + jnp.arange(rows, dtype=jnp.int32)
    valid = (offsets < own_length).astype(F32)[:, None]
    carried_on = jnp.logical_and(here > 0, last_region == own_region).astype(F32)
    same = (regions[:, None] == regions[None, :]).astype(F32)

    def to_columns(values):
        return lax.all_to_all(values.astype(BF), "seq", split_axis=1, concat_axis=0, tiled=True)

    def to_rows(values):
        return lax.all_to_all(values, "seq", split_axis=0, concat_axis=1, tiled=True).astype(F32)

    def filter_stage(layer):
        _, _, in_w, shift_w, freq_w, out_w, decay_w, _, _ = small_of(layer)
        out_cols = lax.dynamic_slice_in_dim(out_w, here * col_width, col_width, 1)
        decay_cols = lax.dynamic_slice_in_dim(decay_w, here * col_width, col_width, 0)
        taps, pull = jax.vjp(
            lambda *p: filter_taps(*p, embedding), in_w, shift_w, freq_w, out_cols, decay_cols
        )
        spectra = jnp.einsum(
            "fs,msc->mfc", table, taps.astype(BF).reshape(count, rows, col_width), preferred_element_type=F32
        )
        before = jnp.concatenate([jnp.zeros_like(spectra[:1]), spectra[:-1]], axis=0)
        return (spectra + scale[:, 1:2] * before) * scale[:, 0:1], pull

    def forward(layer_in, layer):
        gain_one, short_weights, _, _, _, _, _, bias, gain_two = small_of(layer)
        in_matrix, out_matrix, up_matrix, down_matrix = gathered[layer]
        filt, pull = filter_stage(layer)
        normed = layer_norm(layer_in, gain_one).astype(BF)
        projected = dot(normed, in_matrix).astype(BF)
        rim = shifted(projected[rows - 2 :], "seq", 1)
        mixed = short_mix(rim.astype(F32), projected.astype(F32), short_weights, carried_on)
        first, second, third = mixed[:, :width], mixed[:, width : 2 * width], mixed[:, 2 * width :]
        signal = first * third
        x_cols = to_columns(signal * valid)
        y_cols = convolve(same, table, back, filt, x_cols, count, rows)
        filtered = to_rows(y_cols) * valid + bias * signal
        gated = (second * filtered).astype(BF)
        residual = layer_in + dot(gated, out_matrix)
        normed_two = layer_norm(residual, gain_two).astype(BF)
        upward = dot(normed_two, up_matrix)
        active = gelu_tanh(upward).astype(BF)
        layer_out = residual + dot(active, down_matrix)
        stored = (
            layer_in, normed, projected, rim, mixed, signal, filtered, gated, residual, normed_two,
            upward, active, x_cols, filt, pull,
        )
        return layer_out.astype(BF), stored

    def backward(upstream, stored, layer):
        (
            layer_in, normed, projected, rim, mixed, signal, filtered, gated, residual, normed_two,
            upward, active, x_cols, filt, pull,
        ) = stored
        gain_one, short_weights, in_w, shift_w, freq_w, out_w, decay_w, bias, gain_two = small_of(layer)
        in_matrix, out_matrix, up_matrix, down_matrix = gathered[layer]
        grad_hidden = jax.vjp(gelu_tanh, upward)[1](dot_right(upstream, down_matrix))[0].astype(BF)
        grad_norm_two = dot_right(grad_hidden, up_matrix)
        grad_resid_norm, grad_gain_two = jax.vjp(layer_norm, residual, gain_two)[1](grad_norm_two)
        grad_residual = upstream.astype(F32) + grad_resid_norm
        grad_branch = grad_residual.astype(BF)
        grad_gated = dot_right(grad_branch, out_matrix)
        first, second, third = mixed[:, :width], mixed[:, width : 2 * width], mixed[:, 2 * width :]
        grad_second = grad_gated * filtered
        grad_filtered = grad_gated * second
        grad_bias = jnp.sum(grad_filtered * signal, axis=0)
        g_cols = to_columns(grad_filtered * valid)
        dx_cols, grad_taps = correlate(same, table, back, scale, filt, x_cols, g_cols, count, rows)
        grad_signal = to_rows(dx_cols) * valid + bias * grad_filtered
        grad_mixed = jnp.concatenate([grad_signal * third, grad_second, grad_signal * first], axis=1)
        short_pull = jax.vjp(
            lambda a, b, c: short_mix(a, b, c, carried_on), rim.astype(F32), projected.astype(F32), short_weights
        )[1]
        grad_rim, grad_proj, grad_short = short_pull(grad_mixed)
        returned = shifted(grad_rim, "seq", -1)
        tail = grad_proj[rows - 2 :] + returned
        grad_proj = jnp.concatenate([grad_proj[: rows - 2], tail], axis=0)
        grad_proj = grad_proj.astype(BF)
        grad_normed = dot_right(grad_proj, in_matrix)
        grad_norm_in, grad_gain_one = jax.vjp(layer_norm, layer_in, gain_one)[1](grad_normed)
        grad_layer_in = (grad_residual + grad_norm_in).astype(BF)
        d_in, d_shift, d_freq, d_out_cols, d_decay_cols = pull(grad_taps)
        d_out = lax.dynamic_update_slice_in_dim(jnp.zeros_like(out_w), d_out_cols, here * col_width, 1)
        d_decay = lax.dynamic_update_slice_in_dim(jnp.zeros_like(decay_w), d_decay_cols, here * col_width, 0)
        small_grads = (
            grad_gain_one, grad_short, d_in, d_shift, d_freq, d_out, d_decay, grad_bias, grad_gain_two
        )
        parts = []
        for grad, shape, axis in zip(small_grads, small_shapes, small_axis):
            split = list(grad.shape)
            split[axis : axis + 1] = [count, shape[axis]]
            parts.append(jnp.moveaxis(grad.reshape(split), axis, 0).reshape(count, -1))
        packed = jnp.concatenate(parts, axis=1)
        packed = jnp.pad(packed, ((0, 0), (0, packed_rows * lane - packed.shape[1])))
        lefts = [normed_two.T, active.T, normed.T, gated.T]
        rights = [grad_hidden, upstream, grad_proj, grad_branch]
        return grad_layer_in, (lefts, rights, packed.reshape(count * packed_rows, lane))

    def row_of(values):
        return lax.dynamic_index_in_dim(values, core, 0, keepdims=False)

    out_first, stored_first = forward(row_of(tokens).astype(F32), 0)
    out_second, stored_second = forward(out_first.astype(F32), 1)
    grad_second, factors_second = backward(row_of(out_grad), stored_second, 1)
    routed = count == 4 and lax.axis_size("dp") == 4
    if routed:
        own_second = [lax.psum(part, "dp") for part in reduce_layer(*factors_second, False, 1)[0]]
    else:
        own_second = reduce_plain(*factors_second, core)
    grad_first, factors_first = backward(grad_second, stored_first, 0)
    if routed:
        own_first, other_first = reduce_layer(*factors_first, True, 2)
    else:
        own_first = reduce_plain(*factors_first, core)
        other_first = [lax.ppermute(part, "section", [(1, 0)]) for part in own_first]
    other_second = [lax.ppermute(part, "section", [(0, 1)]) for part in own_second]

    def both_rows(of_first, of_second):
        kept = jnp.where(core == 0, of_first, of_second)
        received = core_swap(jnp.where(core == 0, of_second, of_first))
        return jnp.stack([jnp.where(core == 0, kept, received), jnp.where(core == 0, received, kept)])[None]

    layer_outputs = both_rows(out_first, out_second)
    input_grads = both_rows(grad_first, grad_second)

    def finish(index):
        low = jnp.where(core == 0, own_first[index], other_second[index])
        high = jnp.where(core == 0, other_first[index], own_second[index])
        return jnp.concatenate([low, high], axis=1).astype(F32)

    grad_up, grad_down, grad_in, grad_out = (finish(index) for index in range(4))
    small_total = finish(4).reshape(-1)
    small_out = []
    offset = 0
    for shape, size in zip(small_shapes, small_sizes):
        small_out.append(small_total[offset : offset + size].reshape((1,) + shape))
        offset += size
    g_ln1, g_short, g_fin, g_shift, g_freq, g_fout, g_decay, g_bias, g_ln2 = small_out
    return (
        layer_outputs, input_grads, g_ln1, grad_in[None], g_short, g_fin, g_shift, g_freq, g_fout, g_decay, g_bias,
        grad_out[None], g_ln2, grad_up[None], grad_down[None],
    )


def solution(mesh):
    vector = P("section", "seq")
    matrix = P("section", "seq", None)
    last = P("section", None, "seq")
    tokens = P("dp", "seq", None)
    outputs = P("section", "dp", "seq", None)
    in_specs = (
        tokens, tokens, P("dp", None), vector, matrix, last, last, vector, vector, matrix, vector, vector, matrix,
        vector, matrix, matrix,
    )
    out_specs = (
        outputs, outputs, vector, matrix, last, last, vector, vector, matrix, vector, vector, matrix, vector, matrix,
        matrix,
    )
    return jax.shard_map(body, mesh=mesh, in_specs=in_specs, out_specs=out_specs, check_vma=False)
```

```python
import functools
import math

import jax
import jax.numpy as jnp
import numpy as np
from jax import lax
from jax.experimental import pallas as pl
from jax.experimental.pallas import tpu as pltpu
from jax.sharding import PartitionSpec as P

FREQS = 16
PRECISE = lax.Precision.HIGHEST
EPSILON = 1e-05
BF = jnp.bfloat16
F32 = jnp.float32


def dot(left, right):
    return jnp.dot(left, right, preferred_element_type=F32)


def dot_left(left, right):
    return lax.dot_general(left, right, (((0,), (0,)), ((), ())), preferred_element_type=F32)


def dot_right(left, right):
    return lax.dot_general(left, right, (((1,), (1,)), ((), ())), preferred_element_type=F32)


def layer_norm(values, gains):
    row_mean = jnp.mean(values, axis=-1, keepdims=True)
    centered = values - row_mean
    variance = jnp.mean(centered * centered, axis=-1, keepdims=True)
    return centered * lax.rsqrt(variance + EPSILON) * gains


def gelu_tanh(values):
    return jax.nn.gelu(values, approximate=True)


def positions_embedding(slots, harmonic_count):
    steps_all = np.arange(slots)
    scaled = steps_all / slots
    harmonics = np.arange(1, harmonic_count + 1)
    phase = (steps_all[:, None] * harmonics[None, :] % slots) * (2.0 * math.pi / slots)
    both = np.concatenate([scaled[:, None], np.cos(phase), np.sin(phase)], axis=1)
    return both.astype(np.float32)


def filter_taps(filt_in, filt_shift, sine_freq, filt_out, decay, embedding):
    slots = embedding.shape[0]
    inner = jnp.dot(embedding, filt_in, preferred_element_type=F32, precision=PRECISE)
    hidden_sine = jnp.sin(sine_freq * (inner + filt_shift))
    scaled = jnp.arange(slots, dtype=jnp.int32).astype(F32) / slots
    summed = jnp.dot(hidden_sine, filt_out, preferred_element_type=F32, precision=PRECISE)
    return summed * jnp.exp(-decay[None, :] * scaled[:, None])


def short_mix(rim_values, proj_values, weight_values, carried_on):
    total_rows = proj_values.shape[0]
    extended = jnp.concatenate([rim_values * carried_on, proj_values], axis=0)
    return (
        weight_values[0] * extended[2:]
        + weight_values[1] * extended[1 : total_rows + 1]
        + weight_values[2] * extended[:total_rows]
    )


def packed_dft(rows):
    size = 2 * rows
    phase = (np.arange(rows)[:, None] * np.arange(rows)[None, :] % size) * (2.0 * math.pi / size)
    lower = -np.sin(phase)
    lower[0] = 1 - 2 * (np.arange(rows) % 2)
    table = np.concatenate([np.cos(phase), lower], axis=0)
    weight = np.full((size, 1), 2.0 / size)
    weight[0] = weight[rows] = 1.0 / size
    parity = 1.0 - 2.0 * (np.arange(rows) % 2)
    parity = np.concatenate([parity, parity])[:, None]
    parity[rows] = 1 - 2 * (rows % 2)
    return table.astype(np.float32), weight.astype(np.float32), parity.astype(np.float32)


def spectra_rows(table_ref, source_ref, target_ref, blocks, rows):
    for block in range(blocks):
        target_ref[block] = jnp.dot(
            table_ref[...], source_ref[pl.ds(block * rows, rows), :], preferred_element_type=F32
        )


def convolve_kernel(blocks, rows, step, same_ref, table_ref, back_ref, filt_ref, x_ref, y_ref, spec_ref, out_ref):
    spectra_rows(table_ref, x_ref, spec_ref, blocks, rows)
    convolve_spectra(blocks, rows, step, same_ref, filt_ref, spec_ref, out_ref)
    for block in range(blocks):
        y_ref[pl.ds(block * rows, rows), :] = jnp.dot(
            back_ref[...], out_ref[block], preferred_element_type=F32
        ).astype(BF)


def correlate_kernel(
    blocks, rows, step, same_ref, table_ref, back_ref, scale_ref, filt_ref, x_ref, g_ref,
    dx_ref, dt_ref, spec_ref, grad_ref, out_ref, tap_ref,
):
    spectra_rows(table_ref, x_ref, spec_ref, blocks, rows)
    spectra_rows(table_ref, g_ref, grad_ref, blocks, rows)
    correlate_spectra(blocks, rows, step, same_ref, scale_ref, filt_ref, spec_ref, grad_ref, out_ref, tap_ref)
    for block in range(blocks):
        dx_ref[pl.ds(block * rows, rows), :] = jnp.dot(
            back_ref[...], out_ref[block], preferred_element_type=F32
        ).astype(BF)
    taps_back(blocks, rows, back_ref, scale_ref, tap_ref, dt_ref)


MESH = pl.DeviceIdType.MESH
VMEM_SPEC = pl.BlockSpec(memory_space=pltpu.VMEM)
SMEM_SPEC = pl.BlockSpec(memory_space=pltpu.SMEM)
KERNEL_BYTES = 48 * 1024 * 1024


def lasting(microseconds):
    return pl.CostEstimate(flops=0, bytes_accessed=int(microseconds * 3.69e6), transcendentals=0)


def convolve_spectra(blocks, rows, step, same_ref, filt_ref, spec_ref, out_ref):
    width = spec_ref.shape[2]

    def chunk(index, carry):
        real = pl.ds(pl.multiple_of(index * step, step), step)
        imag = pl.ds(pl.multiple_of(rows + index * step, step), step)
        first = (lax.broadcasted_iota(jnp.int32, (step, width), 0) + index * step) == 0
        for i in range(blocks):
            total_real = jnp.zeros((step, width), F32)
            total_imag = jnp.zeros((step, width), F32)
            for lag in range(i + 1):
                weight = same_ref[i, i - lag]
                fr = filt_ref[lag, real, :]
                fi = filt_ref[lag, imag, :]
                cross = jnp.where(first, 0.0, fi)
                own = jnp.where(first, fi, fr)
                xr = spec_ref[i - lag, real, :] * weight
                xi = spec_ref[i - lag, imag, :] * weight
                total_real = total_real + (fr * xr - cross * xi)
                total_imag = total_imag + (cross * xr + own * xi)
            out_ref[i, real, :] = total_real.astype(BF)
            out_ref[i, imag, :] = total_imag.astype(BF)
        return carry

    lax.fori_loop(0, rows // step, chunk, 0)


def correlate_spectra(blocks, rows, step, same_ref, scale_ref, filt_ref, spec_ref, grad_ref, out_ref, tap_ref):
    width = spec_ref.shape[2]

    def chunk(index, carry):
        real = pl.ds(pl.multiple_of(index * step, step), step)
        imag = pl.ds(pl.multiple_of(rows + index * step, step), step)
        first = (lax.broadcasted_iota(jnp.int32, (step, width), 0) + index * step) == 0
        for j in range(blocks):
            total_real = jnp.zeros((step, width), F32)
            total_imag = jnp.zeros((step, width), F32)
            for lag in range(blocks - j):
                weight = same_ref[j + lag, j]
                fr = filt_ref[lag, real, :]
                fi = filt_ref[lag, imag, :]
                cross = jnp.where(first, 0.0, fi)
                own = jnp.where(first, fi, fr)
                gr = grad_ref[j + lag, real, :] * weight
                gi = grad_ref[j + lag, imag, :] * weight
                total_real = total_real + (fr * gr + cross * gi)
                total_imag = total_imag + (own * gi - cross * gr)
            out_ref[j, real, :] = total_real.astype(BF)
            out_ref[j, imag, :] = total_imag.astype(BF)
        for lag in range(blocks):
            one = jnp.zeros((step, width), F32)
            two = jnp.zeros((step, width), F32)
            three = jnp.zeros((step, width), F32)
            for i in range(lag, blocks):
                weight = same_ref[i, i - lag]
                gr = grad_ref[i, real, :] * weight
                gi = grad_ref[i, imag, :] * weight
                xr = spec_ref[i - lag, real, :]
                xi = spec_ref[i - lag, imag, :]
                one = one + xr * gr
                two = two + xi * gi
                three = three + (xr * gi - xi * gr)
            tap_ref[lag, real, :] = (one + jnp.where(first, 0.0, two)) * scale_ref[real, 0:1]
            tap_ref[lag, imag, :] = jnp.where(first, two, three) * scale_ref[imag, 0:1]
        return carry

    lax.fori_loop(0, rows // step, chunk, 0)


def taps_back(blocks, rows, back_ref, scale_ref, tap_ref, dt_ref):
    for block in range(blocks):
        total = tap_ref[block]
        if block + 1 < blocks:
            total = total + scale_ref[:, 1:2] * tap_ref[block + 1]
        dt_ref[pl.ds(block * rows, rows), :] = jnp.dot(
            back_ref[...], total.astype(BF), preferred_element_type=F32
        )


class Peers:
    def __init__(self, send, recv):
        self.core, self.here, self.plane = lax.axis_index("section"), lax.axis_index("seq"), lax.axis_index("dp")
        here = self.here
        self.blocks = (3 - here, here + 1 - 2 * (here % 2), (here + 2) % 4)
        self.send, self.recv = send, recv
        barrier = pltpu.get_barrier_semaphore()
        for block in self.blocks:
            pl.semaphore_signal(barrier, inc=1, device_id=self.at(block), device_id_type=MESH)
        pl.semaphore_wait(barrier, 3)

    def at(self, block):
        return (self.core, block, self.plane)

    def copy(self, number, source, target_ref, block):
        return pltpu.make_async_remote_copy(
            src_ref=source, dst_ref=target_ref, send_sem=self.send.at[number], recv_sem=self.recv.at[number],
            device_id=self.at(block), device_id_type=MESH,
        )


def delayed(values, distance, before):
    index = lax.broadcasted_iota(jnp.int32, values.shape, 0)
    result = pltpu.roll(values, distance, 0)
    for row in range(distance):
        result = jnp.where(index == row, before[row], result)
    return result


def advanced(values, distance):
    rows = values.shape[0]
    index = lax.broadcasted_iota(jnp.int32, values.shape, 0)
    return jnp.where(index >= rows - distance, 0.0, pltpu.roll(values, rows - distance, 0))


def mixed_part(proj_ref, rim_ref, weight_ref, carried, columns):
    now = proj_ref[:, columns].astype(F32)
    rim = rim_ref[:, columns].astype(F32) * carried
    size = rim.shape[0]
    last, before_last = rim[size - 1 : size, :], rim[size - 2 : size - 1, :]
    one = delayed(now, 1, (last,))
    two = delayed(now, 2, (before_last, last))
    mixed = weight_ref[0:1, columns] * now + weight_ref[1:2, columns] * one + weight_ref[2:3, columns] * two
    return mixed, now, one, two


def mix_kernel(
    blocks, rows, step, same_ref, carried_ref, table_ref, back_ref, filt_ref, proj_ref, weight_ref, bias_ref, valid_ref,
    rim_out_ref, x_out_ref, filtered_ref, gated_ref,
    rim_ref, x_ref, mask_ref, signal_ref, second_ref, spec_ref, out_ref, y_ref, y_in_ref, send, recv,
):
    peers = Peers(send, recv)
    here, width = peers.here, proj_ref.shape[1] // 3
    group = width // blocks
    tail = rim_ref.shape[0]
    rim_copy = peers.copy(0, proj_ref.at[pl.ds(rows - tail, tail)], rim_ref, (here + 1) % 4)
    rim_copy.start()
    rim_copy.wait()
    carried, valid = carried_ref[0], valid_ref[...]

    def at_rows(block):
        return pl.ds(pl.multiple_of(block * rows, rows), rows)

    outgoing = []
    for number, block in enumerate(peers.blocks + (here,)):
        start = block * group

        def part(which):
            columns = pl.ds(pl.multiple_of(which * width + start, 128), group)
            return mixed_part(proj_ref, rim_ref, weight_ref, carried, columns)[0]

        signal = part(0) * part(2)
        signal_ref[block] = signal
        second_ref[block] = part(1)
        masked = (signal * valid).astype(BF)
        if number < 3:
            mask_ref[block] = masked
            item = peers.copy(1 + number, mask_ref.at[block], x_ref.at[at_rows(here)], block)
            item.start()
            outgoing.append(item)
        else:
            x_ref[at_rows(here), :] = masked
    for item in outgoing:
        item.wait()
    spectra_rows(table_ref, x_ref, spec_ref, blocks, rows)
    convolve_spectra(blocks, rows, step, same_ref, filt_ref, spec_ref, out_ref)
    rim_out_ref[...] = rim_ref[...]
    x_out_ref[...] = x_ref[...]

    def result(block):
        return jnp.dot(back_ref[...], out_ref[block], preferred_element_type=F32).astype(BF)

    outgoing = []
    for number, block in enumerate(peers.blocks):
        y_ref[block] = result(block)
        item = peers.copy(4 + number, y_ref.at[block], y_in_ref.at[here], block)
        item.start()
        outgoing.append(item)
    y_in_ref[here] = result(here)
    for number, block in enumerate((here,) + peers.blocks):
        if number:
            outgoing[number - 1].wait()
        columns = pl.ds(pl.multiple_of(block * group, 128), group)
        filtered = y_in_ref[block].astype(F32) * valid + bias_ref[:, columns] * signal_ref[block]
        filtered_ref[:, columns] = filtered
        gated_ref[:, columns] = (second_ref[block] * filtered).astype(BF)


def mix(same, carried, table, back, filt, projected, weights, bias, valid, blocks, rows, number):
    width = projected.shape[1] // 3
    group = width // blocks
    return pl.pallas_call(
        functools.partial(mix_kernel, blocks, rows, 32),
        out_shape=(
            jax.ShapeDtypeStruct((16, 3 * width), BF),
            jax.ShapeDtypeStruct((blocks * rows, group), BF),
            jax.ShapeDtypeStruct((rows, width), F32),
            jax.ShapeDtypeStruct((rows, width), BF),
        ),
        in_specs=[SMEM_SPEC] * 2 + [VMEM_SPEC] * 7,
        out_specs=(VMEM_SPEC,) * 4,
        scratch_shapes=[
            pltpu.VMEM((16, 3 * width), BF),
            pltpu.VMEM((blocks * rows, group), BF),
            pltpu.VMEM((blocks, rows, group), BF),
            pltpu.VMEM((blocks, rows, group), F32),
            pltpu.VMEM((blocks, rows, group), F32),
            pltpu.VMEM((blocks, 2 * rows, group), F32),
            pltpu.VMEM((blocks, 2 * rows, group), BF),
            pltpu.VMEM((blocks, rows, group), BF),
            pltpu.VMEM((blocks, rows, group), BF),
            pltpu.SemaphoreType.DMA((7,)),
            pltpu.SemaphoreType.DMA((7,)),
        ],
        compiler_params=pltpu.CompilerParams(
            collective_id=number, has_side_effects=True, vmem_limit_bytes=KERNEL_BYTES
        ),
        name="mix",
        cost_estimate=lasting(22),
    )(same, carried, table, back, filt, projected, weights, bias, valid)


def unmix_kernel(
    blocks, rows, step, same_ref, carried_ref, table_ref, back_ref, scale_ref, filt_ref, proj_ref, rim_ref, weight_ref,
    bias_ref, valid_ref, x_ref, filtered_ref, gate_ref,
    dproj_ref, dweight_ref, dbias_ref, dt_ref,
    g_ref, mask_ref, signal_ref, spec_ref, grad_ref, out_ref, tap_ref, dx_ref, dx_in_ref, edge_ref, edge_in_ref, end_ref,
    send, recv,
):
    peers = Peers(send, recv)
    here, width = peers.here, proj_ref.shape[1] // 3
    group = width // blocks
    carried, valid = carried_ref[0], valid_ref[...]

    def at_rows(block):
        return pl.ds(pl.multiple_of(block * rows, rows), rows)

    def columns_of(which, block):
        return pl.ds(pl.multiple_of(which * width + block * group, 128), group)

    def part(which, block):
        return mixed_part(proj_ref, rim_ref, weight_ref, carried, columns_of(which, block))

    outgoing = []
    for number, block in enumerate(peers.blocks + (here,)):
        columns = columns_of(0, block)
        signal = part(0, block)[0] * part(2, block)[0]
        through = gate_ref[:, columns].astype(F32) * part(1, block)[0]
        dbias_ref[:, columns] = jnp.sum(through * signal, axis=0, keepdims=True)
        signal_ref[block] = bias_ref[:, columns] * through
        masked = (through * valid).astype(BF)
        if number < 3:
            mask_ref[block] = masked
            item = peers.copy(number, mask_ref.at[block], g_ref.at[at_rows(here)], block)
            item.start()
            outgoing.append(item)
        else:
            g_ref[at_rows(here), :] = masked
    spectra_rows(table_ref, x_ref, spec_ref, blocks, rows)
    for item in outgoing:
        item.wait()
    spectra_rows(table_ref, g_ref, grad_ref, blocks, rows)
    correlate_spectra(blocks, rows, step, same_ref, scale_ref, filt_ref, spec_ref, grad_ref, out_ref, tap_ref)

    def result(block):
        return jnp.dot(back_ref[...], out_ref[block], preferred_element_type=F32).astype(BF)

    outgoing = []
    for number, block in enumerate(peers.blocks):
        dx_ref[block] = result(block)
        item = peers.copy(3 + number, dx_ref.at[block], dx_in_ref.at[here], block)
        item.start()
        outgoing.append(item)
    dx_in_ref[here] = result(here)
    taps_back(blocks, rows, back_ref, scale_ref, tap_ref, dt_ref)
    tail = end_ref.shape[0]
    for number, block in enumerate((here,) + peers.blocks):
        if number:
            outgoing[number - 1].wait()
        d_signal = dx_in_ref[block].astype(F32) * valid + signal_ref[block]
        gate = gate_ref[:, columns_of(0, block)].astype(F32)
        first, third = part(0, block), part(2, block)
        second_views = part(1, block)
        d_parts = (d_signal * third[0], gate * filtered_ref[:, columns_of(0, block)], d_signal * first[0])
        for which, (grad, views) in enumerate(zip(d_parts, (first, second_views, third))):
            columns = columns_of(which, block)
            weights = [weight_ref[k : k + 1, columns] for k in range(3)]
            for k in range(3):
                dweight_ref[k : k + 1, columns] = jnp.sum(grad * views[1 + k], axis=0, keepdims=True)
            back_one, back_two = advanced(grad, 1), advanced(grad, 2)
            d_proj = weights[0] * grad + weights[1] * back_one + weights[2] * back_two
            dproj_ref[:, columns] = d_proj.astype(BF)
            end_ref[:, columns] = d_proj[rows - tail :, :]
            head = grad[0:8, :]
            index = lax.broadcasted_iota(jnp.int32, head.shape, 0)
            row_zero, row_one = grad[0:1, :], grad[1:2, :]
            older = weights[2] * row_zero
            newer = weights[1] * row_zero + weights[2] * row_one
            edge = jnp.where(index == 6, older, jnp.where(index == 7, newer, 0.0))
            edge_ref[:, columns] = edge * carried
    edge_copy = peers.copy(6, edge_ref, edge_in_ref, (here + 3) % 4)
    edge_copy.start()
    edge_copy.wait()
    ending = end_ref[...]
    extra = jnp.concatenate([jnp.zeros((tail - 8, 3 * width), F32), edge_in_ref[...]], axis=0)
    dproj_ref[pl.ds(rows - tail, tail), :] = (ending + extra).astype(BF)


def unmix(same, carried, table, back, scale, filt, projected, rim, weights, bias, valid, x_cols, filtered, gate, blocks, rows, number):
    width = projected.shape[1] // 3
    group = width // blocks
    return pl.pallas_call(
        functools.partial(unmix_kernel, blocks, rows, 32),
        out_shape=(
            jax.ShapeDtypeStruct((rows, 3 * width), BF),
            jax.ShapeDtypeStruct((3, 3 * width), F32),
            jax.ShapeDtypeStruct((1, width), F32),
            jax.ShapeDtypeStruct((blocks * rows, group), F32),
        ),
        in_specs=[SMEM_SPEC] * 2 + [VMEM_SPEC] * 12,
        out_specs=(VMEM_SPEC,) * 4,
        scratch_shapes=[
            pltpu.VMEM((blocks * rows, group), BF),
            pltpu.VMEM((blocks, rows, group), BF),
            pltpu.VMEM((blocks, rows, group), F32),
            pltpu.VMEM((blocks, 2 * rows, group), F32),
            pltpu.VMEM((blocks, 2 * rows, group), F32),
            pltpu.VMEM((blocks, 2 * rows, group), BF),
            pltpu.VMEM((blocks, 2 * rows, group), F32),
            pltpu.VMEM((blocks, rows, group), BF),
            pltpu.VMEM((blocks, rows, group), BF),
            pltpu.VMEM((8, 3 * width), F32),
            pltpu.VMEM((8, 3 * width), F32),
            pltpu.VMEM((16, 3 * width), F32),
            pltpu.SemaphoreType.DMA((7,)),
            pltpu.SemaphoreType.DMA((7,)),
        ],
        compiler_params=pltpu.CompilerParams(
            collective_id=number, has_side_effects=True, vmem_limit_bytes=KERNEL_BYTES
        ),
        name="unmix",
        cost_estimate=lasting(28),
    )(same, carried, table, back, scale, filt, projected, rim, weights, bias, valid, x_cols, filtered, gate)


def convolve(same, table, back, filt, x_cols, blocks, rows):
    width = x_cols.shape[1]
    return pl.pallas_call(
        functools.partial(convolve_kernel, blocks, rows, min(32, rows)),
        out_shape=jax.ShapeDtypeStruct(x_cols.shape, BF),
        in_specs=[SMEM_SPEC] + [VMEM_SPEC] * 4,
        out_specs=VMEM_SPEC,
        scratch_shapes=[
            pltpu.VMEM((blocks, 2 * rows, width), F32),
            pltpu.VMEM((blocks, 2 * rows, width), BF),
        ],
        compiler_params=pltpu.CompilerParams(vmem_limit_bytes=KERNEL_BYTES),
        name="convolve",
    )(same, table, back, filt, x_cols)


def correlate(same, table, back, scale, filt, x_cols, g_cols, blocks, rows):
    width = x_cols.shape[1]
    return pl.pallas_call(
        functools.partial(correlate_kernel, blocks, rows, min(32, rows)),
        out_shape=(
            jax.ShapeDtypeStruct(x_cols.shape, BF),
            jax.ShapeDtypeStruct(x_cols.shape, F32),
        ),
        in_specs=[SMEM_SPEC] + [VMEM_SPEC] * 6,
        out_specs=(VMEM_SPEC, VMEM_SPEC),
        scratch_shapes=[
            pltpu.VMEM((blocks, 2 * rows, width), F32),
            pltpu.VMEM((blocks, 2 * rows, width), F32),
            pltpu.VMEM((blocks, 2 * rows, width), BF),
            pltpu.VMEM((blocks, 2 * rows, width), F32),
        ],
        compiler_params=pltpu.CompilerParams(vmem_limit_bytes=KERNEL_BYTES),
        name="correlate",
    )(same, table, back, scale, filt, x_cols, g_cols)


def shifted(block, axis, distance):
    devices = range(lax.axis_size(axis))
    route = [(i - distance, i) for i in devices if i - distance in devices]
    return lax.ppermute(block, axis, route)


def core_swap(block):
    return lax.ppermute(block, "section", [(0, 1), (1, 0)])


def shared_rows(rows):
    return rows // 48 * 16 if rows >= 96 else 0


def gather_kernel(chunks, heights, count, *refs):
    total, arrays = len(chunks), len(heights)
    own_refs, out_refs = refs[:arrays], refs[arrays : 2 * arrays]
    send, recv, local, stage = refs[2 * arrays :]
    sizes = [chunk[2] for chunk in chunks]
    core, here, plane = lax.axis_index("section"), lax.axis_index("seq"), lax.axis_index("dp")
    by_x, by_y, far = here + 1 - 2 * (here % 2), (here + 2) % 4, 3 - here
    odd = plane % 2
    to_x, to_y = (core, by_x, plane), (core, by_y, plane)
    to_z, to_core = (core, here, plane + 1 - 2 * odd), (1 - core, here, plane)
    barrier = pltpu.get_barrier_semaphore()
    for target in (to_x, to_y, to_z, to_core):
        pl.semaphore_signal(barrier, inc=1, device_id=target, device_id_type=MESH)
    pl.semaphore_wait(barrier, 4)

    def window(m, block, start, length):
        which, base, _, left, wide = chunks[m]
        first = (core * count + block) * heights[which] + base + start
        return out_refs[which].at[pl.ds(pl.multiple_of(first, 16), length), pl.ds(left, wide)]

    def own_window(m, start, length):
        which, base, _, left, wide = chunks[m]
        return own_refs[which].at[pl.ds(pl.multiple_of(base + start, 16), length), pl.ds(left, wide)]

    def copy(kind, m, source, target_ref, target):
        return pltpu.make_async_remote_copy(
            src_ref=source, dst_ref=target_ref, send_sem=send.at[kind, m], recv_sem=recv.at[kind, m],
            device_id=target, device_id_type=MESH,
        )

    def forward(kind, m, block, start, length, target):
        where = window(m, block, start, length)
        return copy(kind, m, where, where, target)

    started = []

    def go(item):
        item.start()
        started.append(item)
        return item

    def from_own(kind, m, start, length, target):
        return go(copy(kind, m, own_window(m, start, length), window(m, here, start, length), target))

    kept, thirds, lows, begins = [], [], [], []
    for m in range(total):
        third = shared_rows(sizes[m])
        thirds.append(third)
        begins.append(odd * third)
        lows.append(-(-(sizes[m] - third) // 32) * 16)
    direct, cross, side = {}, {}, {}

    def first_hop(m):
        length = sizes[m] - thirds[m]
        direct[m] = (
            from_own(0, m, begins[m], length, to_x), from_own(1, m, begins[m], length, to_y)
        )

    def given(m):
        return odd * (sizes[m] - thirds[m])

    def second_hop(m):
        length, low = sizes[m] - thirds[m], lows[m]
        direct[m][0].wait_recv()
        low_copy = go(forward(2, m, by_x, begins[m], low, to_y))
        if thirds[m]:
            side[m] = [go(forward(4, m, by_x, given(m), thirds[m], to_z))]
        kept.append(go(forward(7, m, by_x, begins[m], length, to_core)))
        direct[m][1].wait_recv()
        high_copy = go(forward(3, m, by_y, begins[m] + low, length - low, to_x))
        if thirds[m]:
            side[m].append(go(forward(5, m, by_y, given(m), thirds[m], to_z)))
        kept.append(go(forward(8, m, by_y, begins[m], length, to_core)))
        cross[m] = (low_copy, high_copy)

    def third_hop(m):
        length = sizes[m] - thirds[m]
        cross[m][0].wait_recv()
        cross[m][1].wait_recv()
        if thirds[m]:
            side[m].append(go(forward(6, m, far, given(m), thirds[m], to_z)))
        kept.append(go(forward(9, m, far, begins[m], length, to_core)))

    def last_hop(m):
        if thirds[m]:
            missing = (1 - odd) * (sizes[m] - thirds[m])
            for k, block in enumerate((by_x, by_y, far)):
                side[m][k].wait_recv()
                kept.append(go(forward(10 + k, m, block, missing, thirds[m], to_core)))

    first_hop(0)
    first_hop(1)
    def through(m, out):
        held = stage.at[m, pl.ds(0, sizes[m])]
        source, target = (held, window(m, here, 0, sizes[m])) if out else (own_window(m, 0, sizes[m]), held)
        return pltpu.make_async_copy(source, target, local.at[m])

    for m in range(total):
        through(m, False).start()
    for m in range(total):
        second_hop(m)
        if m + 2 < total:
            first_hop(m + 2)
        kept.append(from_own(13, m, 0, sizes[m], to_core))
        through(m, False).wait()
        through(m, True).start()
        if m >= 1:
            third_hop(m - 1)
        if m >= 2:
            last_hop(m - 2)
    third_hop(total - 1)
    for m in range(max(total - 2, 0), total):
        last_hop(m)
    for m in range(total):
        through(m, True).wait()
    for item in kept:
        item.wait_recv()
    for item in started:
        item.wait_send()


def gather_shards(shards):
    count = lax.axis_size("seq")
    core = lax.axis_index("section")
    if count != 4 or lax.axis_size("dp") % 2:
        result = []
        for shard in shards:
            whole = lax.all_gather(shard, "seq", axis=0, tiled=True)
            other = core_swap(whole)
            low = jnp.where(core == 0, whole, other)
            result.append(jnp.concatenate([low, jnp.where(core == 0, other, whole)], axis=0))
        return result
    heights = [shard.shape[0] for shard in shards]
    chunks = []
    for which, shard in enumerate(shards):
        high, wide = min(shard.shape[0], 256), min(shard.shape[1], 1024)
        for base in range(0, shard.shape[0], high):
            chunks += [(which, base, high, left, wide) for left in range(0, shard.shape[1], wide)]
    return pl.pallas_call(
        functools.partial(gather_kernel, chunks, heights, count),
        out_shape=[jax.ShapeDtypeStruct((2 * count * a.shape[0], a.shape[1]), a.dtype) for a in shards],
        in_specs=[pl.BlockSpec(memory_space=pl.ANY)] * len(shards),
        out_specs=[pl.BlockSpec(memory_space=pl.ANY)] * len(shards),
        scratch_shapes=[
            pltpu.SemaphoreType.DMA((14, len(chunks))),
            pltpu.SemaphoreType.DMA((14, len(chunks))),
            pltpu.SemaphoreType.DMA((len(chunks),)),
            pltpu.VMEM((len(chunks), max(c[2] for c in chunks), max(c[4] for c in chunks)), shards[0].dtype),
        ],
        compiler_params=pltpu.CompilerParams(
            collective_id=0, has_side_effects=True, vmem_limit_bytes=KERNEL_BYTES
        ),
        name="gather_shards",
        cost_estimate=lasting(190),
    )(*shards)


def core_halves(core, values):
    width = values.shape[1] // 2
    return (
        lax.dynamic_slice_in_dim(values, core * width, width, 1),
        lax.dynamic_slice_in_dim(values, (1 - core) * width, width, 1),
    )


X_FIRST = (0, 2, 1, 3)
Y_FIRST = (0, 1, 2, 3)
PARTS = 4


def reduce_kernel(items, rest, halves, planes, order, *refs):
    whole = len(items)
    total = whole + len(rest)
    sides = len(halves) * 2 + 1

    def take(number):
        nonlocal refs
        first, refs = refs[:number], refs[number:]
        return first

    inputs, rest_in = take(sides), take(len(rest))
    own_out = take(total)
    other_out = dict(zip(planes, take(len(planes))))
    hold, inbox, far_in, near_in = take(total), take(whole), take(whole), take(whole)
    plane_in, cross_in = dict(zip(planes, take(len(planes)))), dict(zip(planes, take(len(planes))))
    send, recv, local = refs
    core, here, plane = lax.axis_index("section"), lax.axis_index("seq"), lax.axis_index("dp")
    by_x, by_y, far = here + 1 - 2 * (here % 2), (here + 2) % 4, 3 - here
    to_x, to_y, to_core = (core, by_x, plane), (core, by_y, plane), (1 - core, here, plane)
    to_inner = (core, here, (plane + 3) // 3)
    to_outer = (core, here, 3 * (plane // 2))
    to_cross = (core, here, 3 - plane)
    outer = jnp.logical_or(plane == 0, plane == 3)
    inner = jnp.logical_and(plane > 0, plane < 3)

    barrier = pltpu.get_barrier_semaphore()

    def greet(target):
        pl.semaphore_signal(barrier, inc=1, device_id=target, device_id_type=MESH)

    for target in (to_x, to_y, to_core):
        greet(target)
    if planes:

        @pl.when(outer)
        def _():
            greet(to_inner)
            pl.semaphore_wait(barrier, 4)

        @pl.when(inner)
        def _():
            greet(to_outer)
            greet(to_cross)
            pl.semaphore_wait(barrier, 5)
    else:
        pl.semaphore_wait(barrier, 3)

    def copy(kind, m, source, target_ref, target):
        return pltpu.make_async_remote_copy(
            src_ref=source, dst_ref=target_ref, send_sem=send.at[kind, m], recv_sem=recv.at[kind, m],
            device_id=target, device_id_type=MESH,
        )

    heights = [item[0] for item in items] + [shape[0] for shape in rest]

    def rows_of(ref, m, slot, slots=1):
        rows = heights[m]
        return ref[m].at[pl.ds(slot * rows, slots * rows)]

    def copies(m):
        along_x = m < whole and items[m][5] == X_FIRST
        return dict(
            load=lambda: pltpu.make_async_copy(rest_in[m - whole], hold[m], local.at[m]),
            core=lambda: copy(0, m, hold[m], inbox[m], to_core),
            far=lambda: copy(1, m, rows_of(hold, m, 2, 2), far_in[m], to_x if along_x else to_y),
            near=lambda: copy(2, m, rows_of(hold, m, 1), near_in[m], to_y if along_x else to_x),
            inward=lambda: copy(3, m, rows_of(hold, m, 0), plane_in[m], to_inner),
            cross=lambda: copy(4, m, rows_of(hold, m, 0), cross_in[m], to_cross),
            outward=lambda: copy(3, m, rows_of(hold, m, 0), plane_in[m], to_outer),
            last_held=lambda: copy(5, m, rows_of(hold, m, 0), other_out[m], to_core),
            last_got=lambda: copy(5, m, plane_in[m], other_out[m], to_core),
            held=lambda: pltpu.make_async_copy(rows_of(hold, m, 0), own_out[m], local.at[m]),
            got=lambda: pltpu.make_async_copy(plane_in[m], own_out[m], local.at[m]),
        )

    moves = [copies(m) for m in range(total)]

    def fill(m, slot, side, adds):
        rows, columns, left, right, first, order = items[m]
        block = {0: here, 1: by_x, 2: by_y, 3: far}[order[slot]]
        high, wide = min(rows, 256), columns if columns <= 768 else 512
        across = columns // wide
        start = side * halves[right] + first if right >= 0 else side * columns

        def step(index, carry):
            down, along = index // across, index % across
            picked = pl.ds(pl.multiple_of(block * rows + down * high, 16), high)
            which = pl.ds(pl.multiple_of(start + along * wide, 128), wide)
            if right >= 0:
                value = jnp.dot(
                    inputs[left][picked, :], inputs[len(halves) + right][:, which], preferred_element_type=F32
                )
            else:
                value = inputs[-1][picked, which]
            where = pl.ds(pl.multiple_of(along * wide, 128), wide)
            for ref, base in adds:
                value = value + ref[m][pl.ds(pl.multiple_of(base * rows + down * high, 16), high), where].astype(F32)
            hold[m][pl.ds(pl.multiple_of(slot * rows + down * high, 16), high), where] = value.astype(BF)
            return carry

        lax.fori_loop(0, rows // high * across, step, 0)

    def add_plane(m, ref):
        rows = heights[m]
        high = min(rows, 64)

        def step(index, carry):
            where = pl.ds(pl.multiple_of(index * high, 16), high)
            value = hold[m][where, :].astype(F32) + ref[m][where, :].astype(F32)
            hold[m][where, :] = value.astype(BF)
            return carry

        lax.fori_loop(0, rows // high, step, 0)

    def to_other_core(m):
        for slot in (2, 3, 1, 0):
            fill(m, slot, 1 - core, [])
        moves[m]["core"]().start()

    def prepare(m):
        moves[m]["core"]().wait()
        for slot in (2, 3):
            fill(m, slot, core, [(inbox, slot)])

    def first_hop(m):
        moves[m]["far"]().start()

    def landed(m):
        moves[m]["far"]().wait_recv()

    def second_hop(m):
        fill(m, 1, core, [(inbox, 1), (far_in, 1)])
        moves[m]["near"]().start()

    def arrive(m):
        moves[m]["near"]().wait_recv()
        fill(m, 0, core, [(inbox, 0), (far_in, 0), (near_in, 0)])
        if m in planes:

            @pl.when(outer)
            def _():
                moves[m]["inward"]().start()
        else:
            moves[m]["held"]().start()

    def meet(m):
        @pl.when(inner)
        def _():
            moves[m]["inward"]().wait_recv()
            add_plane(m, plane_in)
            moves[m]["cross"]().start()

    def settle(m):
        @pl.when(inner)
        def _():
            moves[m]["cross"]().wait()
            add_plane(m, cross_in)
            moves[m]["outward"]().start()
            moves[m]["last_held"]().start()
            moves[m]["held"]().start()

    def finish(m):
        @pl.when(outer)
        def _():
            moves[m]["inward"]().wait()
            moves[m]["last_got"]().start()
            moves[m]["got"]().start()

    def begin(m):
        moves[m]["load"]().wait()

        @pl.when(outer)
        def _():
            moves[m]["inward"]().start()

    names = dict(
        core=to_other_core, fill=prepare, go=first_hop, wait=landed, turn=second_hop, own=arrive, meet=meet, settle=settle,
        finish=finish, load=begin,
    )
    for m in range(whole, total):
        moves[m]["load"]().start()
    for step, pair in order:
        for m in (2 * pair, 2 * pair + 1):
            names[step](m)

    for m in range(total):
        if m < whole:
            moves[m]["far"]().wait_send()
            moves[m]["near"]().wait_send()
        if m in planes:

            @pl.when(inner)
            def _():
                moves[m]["outward"]().wait_send()
                moves[m]["last_held"]().wait()
                moves[m]["held"]().wait()

            @pl.when(outer)
            def _():
                moves[m]["last_got"]().wait()
                moves[m]["got"]().wait()
        else:
            moves[m]["held"]().wait()


def reduce_order(pairs, summed, rest):
    steps = [("load", k) for k in rest] + [("core", pairs[0]), ("fill", pairs[0]), ("go", pairs[0])]
    steps += [("core", k) for k in pairs[1:3]] + [("fill", pairs[1])]
    groups = [list(rest)] + [[pair] if pair in summed else [] for pair in pairs]

    def at(name, number):
        if 0 <= number < len(groups):
            steps.extend((name, k) for k in groups[number])

    for i, pair in enumerate(pairs):
        steps.append(("wait", pair))
        if i + 1 < len(pairs):
            steps.append(("go", pairs[i + 1]))
        steps.append(("turn", pair))
        if i + 3 < len(pairs):
            steps.append(("core", pairs[i + 3]))
        if i + 2 < len(pairs):
            steps.append(("fill", pairs[i + 2]))
        at("meet", i)
        steps.append(("own", pair))
        at("settle", i - 1)
        at("finish", i - 2)
    for i in range(len(pairs), len(pairs) + 3):
        at("meet", i)
        at("settle", i - 1)
        at("finish", i - 2)
    return steps


def reduce_layer(lefts, rights, packed, rest, planes, order, number):
    count = lax.axis_size("seq")
    halves = [right.shape[1] // 2 for right in rights]
    small_rows, small_width = packed.shape[0] // count, packed.shape[1] // 2
    up, down, enter, leave = (left.shape[0] // count for left in lefts)
    items = [
        (leave, halves[3], 3, 3, 0, X_FIRST),
        (small_rows, small_width, -1, -1, 0, Y_FIRST),
        (enter, halves[2] // 2, 2, 2, 0, X_FIRST),
        (enter, halves[2] // 2, 2, 2, halves[2] // 2, Y_FIRST),
    ]
    for part in range(PARTS):
        items += [
            (up, halves[0] // PARTS, 0, 0, part * halves[0] // PARTS, X_FIRST),
            (down, halves[1] // PARTS, 1, 1, part * halves[1] // PARTS, Y_FIRST),
        ]
    pieces = [item[:2] for item in items] + [piece.shape for piece in rest]

    def buffers(slots, shapes):
        return [pltpu.VMEM((slots * shape[0], shape[1]), BF) for shape in shapes]

    hbm = pl.BlockSpec(memory_space=pl.ANY)
    whole, total = len(items), len(pieces)
    planes = list(planes) + list(range(whole, total))
    across = [pieces[m] for m in planes]
    scratch = buffers(4, pieces[:whole]) + buffers(1, pieces[whole:])
    for slots in (4, 2, 1):
        scratch += buffers(slots, pieces[:whole])
    scratch += buffers(1, across) + buffers(1, across)
    semaphores = [pltpu.SemaphoreType.DMA((6, total)), pltpu.SemaphoreType.DMA((6, total)), pltpu.SemaphoreType.DMA((total,))]
    result = pl.pallas_call(
        functools.partial(reduce_kernel, items, pieces[whole:], halves, planes, order),
        out_shape=[jax.ShapeDtypeStruct(shape, BF) for shape in pieces + across],
        in_specs=[VMEM_SPEC] * (2 * len(lefts) + 1) + [hbm] * len(rest),
        out_specs=[hbm] * (total + len(planes)),
        scratch_shapes=scratch + semaphores,
        compiler_params=pltpu.CompilerParams(
            collective_id=number, has_side_effects=True, vmem_limit_bytes=60 * 1024 * 1024
        ),
        name="reduce_layer",
        cost_estimate=lasting(150),
    )(*lefts, *rights, packed, *rest)
    return result[:total], dict(zip(planes, result[total:]))


def join_pieces(pieces):
    ups, downs = pieces[4::2], pieces[5::2]
    return [jnp.concatenate(group, axis=1) for group in (ups, downs, pieces[2:4])] + list(pieces[:2])


def reduce_plain(lefts, rights, packed, core):
    count = lax.axis_size("seq")
    chips = []
    for left, right in zip(lefts, rights):
        keep, send = core_halves(core, right)
        chips.append(dot(left, keep) + core_swap(dot(left, send).astype(BF)).astype(F32))
    keep, send = core_halves(core, packed)
    small = (keep + core_swap(send.astype(BF)).astype(F32)).astype(BF)
    up, down, enter, leave = (chip.astype(BF) for chip in chips)
    out_rows, half = leave.shape[0] // count, leave.shape[1]
    leave = jnp.concatenate([leave.reshape(count, out_rows, half), small.reshape(count, -1, half)], axis=1)
    own = []
    for chip in (up, down, enter, leave.reshape(-1, half)):
        own.append(lax.psum(lax.psum_scatter(chip, "seq", scatter_dimension=0, tiled=True), "dp"))
    return own[:3] + [own[3][:out_rows], own[3][out_rows:]]


def body(
    tokens, out_grad, lengths, ln1_gain, w_in, short_w, filt_in, filt_shift, sine_freq, filt_out,
    decay, filter_bias, w_out, ln2_gain, mlp_up, mlp_down,
):
    micro, rows, width = tokens.shape
    count = lax.axis_size("seq")
    here = lax.axis_index("seq")
    core = lax.axis_index("section")
    routed = count == 4 and lax.axis_size("dp") == 4
    slots = rows * count
    col_width = width // count
    hidden = mlp_up.shape[2]
    hidden_block = hidden // count
    half_block = hidden_block // 2
    table_np, weight_np, parity_np = packed_dft(rows)
    table = jnp.asarray(table_np).astype(BF)
    back = jnp.asarray(np.ascontiguousarray(table_np.T)).astype(BF)
    scale = jnp.asarray(np.concatenate([weight_np, parity_np], axis=1))
    embedding = jnp.asarray(positions_embedding(slots, FREQS))

    small = (ln1_gain, short_w, filt_in, filt_shift, sine_freq, filt_out, decay, filter_bias, ln2_gain)
    small_shapes = [a.shape[1:] for a in small]
    small_sizes = [math.prod(s) for s in small_shapes]
    lane = 1024
    packed_rows = -(-sum(small_sizes) // (lane * 16)) * 16
    flat = jnp.concatenate([a.reshape(-1) for a in small])
    flat = jnp.pad(flat, (0, packed_rows * lane - flat.shape[0])).reshape(packed_rows, lane)
    flat_all, out_all, in_all, up_all, down_all = gather_shards([flat, w_out[0], w_in[0], mlp_up[0], mlp_down[0]])
    everywhere = flat_all.reshape(2, count, packed_rows * lane)
    gathered = [
        (
            in_all[layer * width : (layer + 1) * width], out_all[layer * width : (layer + 1) * width],
            up_all[layer * width : (layer + 1) * width], down_all[layer * hidden : (layer + 1) * hidden],
        )
        for layer in range(2)
    ]
    small_axis = (0, 1, 1, 0, 0, 0, 0, 0, 0)

    def small_of(layer):
        found = []
        offset = 0
        for shape, size, axis in zip(small_shapes, small_sizes, small_axis):
            part = everywhere[layer, :, offset : offset + size].reshape((count,) + shape)
            part = jnp.moveaxis(part, 0, axis)
            full = list(shape)
            full[axis] = shape[axis] * count
            found.append(part.reshape(full).astype(F32))
            offset += size
        return found

    length_row = lax.dynamic_index_in_dim(lengths, core, 0, keepdims=False)
    index_all = jnp.arange(count, dtype=jnp.int32)
    started = jnp.logical_and(length_row[None, :] > 0, index_all[None, :] <= index_all[:, None])
    regions = jnp.max(jnp.where(started, index_all[None, :], 0), axis=1)
    doc_length = jnp.sum(jnp.where(regions[:, None] == index_all[None, :], length_row[None, :], 0), axis=1)
    own_region = jnp.sum(jnp.where(index_all == here, regions, 0))
    own_length = jnp.sum(jnp.where(index_all == here, doc_length, 0))
    last_region = jnp.sum(jnp.where(index_all == here - 1, regions, 0))
    offsets = (here - own_region) * rows + jnp.arange(rows, dtype=jnp.int32)
    valid = (offsets < own_length).astype(F32)[:, None]
    carried_on = jnp.logical_and(here > 0, last_region == own_region).astype(F32)
    same = (regions[:, None] == regions[None, :]).astype(F32)

    def to_columns(values):
        return lax.all_to_all(values.astype(BF), "seq", split_axis=1, concat_axis=0, tiled=True)

    def to_rows(values):
        return lax.all_to_all(values, "seq", split_axis=0, concat_axis=1, tiled=True).astype(F32)

    def filter_stage(layer):
        _, _, in_w, shift_w, freq_w, out_w, decay_w, _, _ = small_of(layer)
        out_cols = lax.dynamic_slice_in_dim(out_w, here * col_width, col_width, 1)
        decay_cols = lax.dynamic_slice_in_dim(decay_w, here * col_width, col_width, 0)
        taps, pull = jax.vjp(
            lambda *p: filter_taps(*p, embedding), in_w, shift_w, freq_w, out_cols, decay_cols
        )
        spectra = jnp.einsum(
            "fs,msc->mfc", table, taps.astype(BF).reshape(count, rows, col_width), preferred_element_type=F32
        )
        before = jnp.concatenate([jnp.zeros_like(spectra[:1]), spectra[:-1]], axis=0)
        return (spectra + scale[:, 1:2] * before) * scale[:, 0:1], pull

    def forward(layer_in, layer):
        gain_one, short_weights, _, _, _, _, _, bias, gain_two = small_of(layer)
        in_matrix, out_matrix, up_matrix, down_matrix = gathered[layer]
        filt, pull = filter_stage(layer)
        normed = layer_norm(layer_in, gain_one).astype(BF)
        projected = dot(normed, in_matrix).astype(BF)
        if routed:
            rim, x_cols, filtered, gated = mix(
                same, carried_on.reshape(1), table, back, filt, projected, short_weights, bias[None], valid, count, rows, 3 + layer
            )
        else:
            rim = shifted(projected[rows - 2 :], "seq", 1)
            mixed = short_mix(rim.astype(F32), projected.astype(F32), short_weights, carried_on)
            first, second, third = mixed[:, :width], mixed[:, width : 2 * width], mixed[:, 2 * width :]
            signal = first * third
            x_cols = to_columns(signal * valid)
            y_cols = convolve(same, table, back, filt, x_cols, count, rows)
            filtered = to_rows(y_cols) * valid + bias * signal
            gated = (second * filtered).astype(BF)
        residual = layer_in + dot(gated, out_matrix)
        normed_two = layer_norm(residual, gain_two).astype(BF)
        upward = dot(normed_two, up_matrix)
        active = gelu_tanh(upward).astype(BF)
        layer_out = residual + dot(active, down_matrix)
        stored = (
            layer_in, normed, projected, rim, filtered, gated, residual, normed_two,
            upward, active, x_cols, filt, pull,
        )
        return layer_out.astype(BF), stored

    def backward(upstream, stored, layer):
        (
            layer_in, normed, projected, rim, filtered, gated, residual, normed_two,
            upward, active, x_cols, filt, pull,
        ) = stored
        gain_one, short_weights, in_w, shift_w, freq_w, out_w, decay_w, bias, gain_two = small_of(layer)
        in_matrix, out_matrix, up_matrix, down_matrix = gathered[layer]
        grad_hidden = jax.vjp(gelu_tanh, upward)[1](dot_right(upstream, down_matrix))[0].astype(BF)
        grad_norm_two = dot_right(grad_hidden, up_matrix)
        grad_resid_norm, grad_gain_two = jax.vjp(layer_norm, residual, gain_two)[1](grad_norm_two)
        grad_residual = upstream.astype(F32) + grad_resid_norm
        grad_branch = grad_residual.astype(BF)
        grad_gated = dot_right(grad_branch, out_matrix)
        if routed:
            grad_proj, grad_short, grad_bias, grad_taps = unmix(
                same, carried_on.reshape(1), table, back, scale, filt, projected, rim, short_weights, bias[None], valid,
                x_cols, filtered, grad_gated, count, rows, 5 + layer,
            )
            grad_bias = grad_bias[0]
        else:
            mixed = short_mix(rim.astype(F32), projected.astype(F32), short_weights, carried_on)
            first, second, third = mixed[:, :width], mixed[:, width : 2 * width], mixed[:, 2 * width :]
            signal = first * third
            grad_second = grad_gated * filtered
            grad_filtered = grad_gated * second
            grad_bias = jnp.sum(grad_filtered * signal, axis=0)
            g_cols = to_columns(grad_filtered * valid)
            dx_cols, grad_taps = correlate(same, table, back, scale, filt, x_cols, g_cols, count, rows)
            grad_signal = to_rows(dx_cols) * valid + bias * grad_filtered
            grad_mixed = jnp.concatenate([grad_signal * third, grad_second, grad_signal * first], axis=1)
            short_pull = jax.vjp(
                lambda a, b, c: short_mix(a, b, c, carried_on), rim.astype(F32), projected.astype(F32), short_weights
            )[1]
            grad_rim, grad_proj, grad_short = short_pull(grad_mixed)
            returned = shifted(grad_rim, "seq", -1)
            tail = grad_proj[rows - 2 :] + returned
            grad_proj = jnp.concatenate([grad_proj[: rows - 2], tail], axis=0)
            grad_proj = grad_proj.astype(BF)
        grad_normed = dot_right(grad_proj, in_matrix)
        grad_norm_in, grad_gain_one = jax.vjp(layer_norm, layer_in, gain_one)[1](grad_normed)
        grad_layer_in = (grad_residual + grad_norm_in).astype(BF)
        d_in, d_shift, d_freq, d_out_cols, d_decay_cols = pull(grad_taps)
        d_out = lax.dynamic_update_slice_in_dim(jnp.zeros_like(out_w), d_out_cols, here * col_width, 1)
        d_decay = lax.dynamic_update_slice_in_dim(jnp.zeros_like(decay_w), d_decay_cols, here * col_width, 0)
        small_grads = (
            grad_gain_one, grad_short, d_in, d_shift, d_freq, d_out, d_decay, grad_bias, grad_gain_two
        )
        parts = []
        for grad, shape, axis in zip(small_grads, small_shapes, small_axis):
            split = list(grad.shape)
            split[axis : axis + 1] = [count, shape[axis]]
            parts.append(jnp.moveaxis(grad.reshape(split), axis, 0).reshape(count, -1))
        packed = jnp.concatenate(parts, axis=1)
        packed = jnp.pad(packed, ((0, 0), (0, packed_rows * lane - packed.shape[1])))
        lefts = [normed_two.T, active.T, normed.T, gated.T]
        rights = [grad_hidden, upstream, grad_proj, grad_branch]
        return grad_layer_in, (lefts, rights, packed.reshape(count * packed_rows, lane))

    def row_of(values):
        return lax.dynamic_index_in_dim(values, core, 0, keepdims=False)

    out_first, stored_first = forward(row_of(tokens).astype(F32), 0)
    out_second, stored_second = forward(out_first.astype(F32), 1)
    grad_second, factors_second = backward(row_of(out_grad), stored_second, 1)
    if routed:
        whole, held_back = 4 + 2 * PARTS, 2
        ready = whole - 2 * held_back
        pairs = [1, *range(2, 2 + PARTS - held_back), 0, *range(2 + PARTS - held_back, 2 + PARTS)]
        order = reduce_order(pairs, range(ready // 2), [])
        own_second, other_second = reduce_layer(*factors_second, [], range(ready), order, 1)
        grad_first, factors_first = backward(grad_second, stored_first, 0)
        order = reduce_order([1, *range(2, 2 + PARTS), 0], range(whole // 2), range(whole // 2, whole // 2 + held_back))
        own_first, other_first = reduce_layer(*factors_first, own_second[ready:], range(whole), order, 2)
        other_second = [other_second[m] for m in range(ready)] + [other_first[m] for m in range(whole, whole + 2 * held_back)]
        own_second = list(own_second[:ready]) + list(own_first[whole:])
        own_first, other_first = own_first[:whole], [other_first[m] for m in range(whole)]
        own_first, own_second, other_first, other_second = (
            join_pieces(part) for part in (own_first, own_second, other_first, other_second)
        )
    else:
        own_second = reduce_plain(*factors_second, core)
        grad_first, factors_first = backward(grad_second, stored_first, 0)
        own_first = reduce_plain(*factors_first, core)
        other_first, other_second = ([core_swap(part) for part in own] for own in (own_first, own_second))

    def both_rows(of_first, of_second):
        kept = jnp.where(core == 0, of_first, of_second)
        received = core_swap(jnp.where(core == 0, of_second, of_first))
        return jnp.stack([jnp.where(core == 0, kept, received), jnp.where(core == 0, received, kept)])[None]

    layer_outputs = both_rows(out_first, out_second)
    input_grads = both_rows(grad_first, grad_second)

    def finish(index):
        low = jnp.where(core == 0, own_first[index], other_second[index])
        high = jnp.where(core == 0, other_first[index], own_second[index])
        return jnp.concatenate([low, high], axis=1).astype(F32)

    grad_up, grad_down, grad_in, grad_out = (finish(index) for index in range(4))
    small_total = finish(4).reshape(-1)
    small_out = []
    offset = 0
    for shape, size in zip(small_shapes, small_sizes):
        small_out.append(small_total[offset : offset + size].reshape((1,) + shape))
        offset += size
    g_ln1, g_short, g_fin, g_shift, g_freq, g_fout, g_decay, g_bias, g_ln2 = small_out
    return (
        layer_outputs, input_grads, g_ln1, grad_in[None], g_short, g_fin, g_shift, g_freq, g_fout, g_decay, g_bias,
        grad_out[None], g_ln2, grad_up[None], grad_down[None],
    )


def solution(mesh):
    vector = P("section", "seq")
    matrix = P("section", "seq", None)
    last = P("section", None, "seq")
    tokens = P("dp", "seq", None)
    outputs = P("section", "dp", "seq", None)
    in_specs = (
        tokens, tokens, P("dp", None), vector, matrix, last, last, vector, vector, matrix, vector, vector, matrix,
        vector, matrix, matrix,
    )
    out_specs = (
        outputs, outputs, vector, matrix, last, last, vector, vector, matrix, vector, vector, matrix, vector, matrix,
        matrix,
    )
    return jax.shard_map(body, mesh=mesh, in_specs=in_specs, out_specs=out_specs, check_vma=False)
```

```python
import functools
import math

import jax
import jax.numpy as jnp
import numpy as np
from jax import lax
from jax.experimental import pallas as pl
from jax.experimental.pallas import tpu as pltpu
from jax.sharding import PartitionSpec as P

FREQS = 16
PRECISE = lax.Precision.HIGHEST
EPSILON = 1e-05
BF = jnp.bfloat16
F32 = jnp.float32


def dot(left, right):
    return jnp.dot(left, right, preferred_element_type=F32)


def dot_left(left, right):
    return lax.dot_general(left, right, (((0,), (0,)), ((), ())), preferred_element_type=F32)


def dot_right(left, right):
    return lax.dot_general(left, right, (((1,), (1,)), ((), ())), preferred_element_type=F32)


def layer_norm(values, gains):
    row_mean = jnp.mean(values, axis=-1, keepdims=True)
    centered = values - row_mean
    variance = jnp.mean(centered * centered, axis=-1, keepdims=True)
    return centered * lax.rsqrt(variance + EPSILON) * gains


def gelu_tanh(values):
    return jax.nn.gelu(values, approximate=True)


def positions_embedding(slots, harmonic_count):
    steps_all = np.arange(slots)
    scaled = steps_all / slots
    harmonics = np.arange(1, harmonic_count + 1)
    phase = (steps_all[:, None] * harmonics[None, :] % slots) * (2.0 * math.pi / slots)
    both = np.concatenate([scaled[:, None], np.cos(phase), np.sin(phase)], axis=1)
    return both.astype(np.float32)


def filter_taps(filt_in, filt_shift, sine_freq, filt_out, decay, embedding):
    slots = embedding.shape[0]
    inner = jnp.dot(embedding, filt_in, preferred_element_type=F32, precision=PRECISE)
    hidden_sine = jnp.sin(sine_freq * (inner + filt_shift))
    scaled = jnp.arange(slots, dtype=jnp.int32).astype(F32) / slots
    summed = jnp.dot(hidden_sine, filt_out, preferred_element_type=F32, precision=PRECISE)
    return summed * jnp.exp(-decay[None, :] * scaled[:, None])


def short_mix(rim_values, proj_values, weight_values, carried_on):
    total_rows = proj_values.shape[0]
    extended = jnp.concatenate([rim_values * carried_on, proj_values], axis=0)
    return (
        weight_values[0] * extended[2:]
        + weight_values[1] * extended[1 : total_rows + 1]
        + weight_values[2] * extended[:total_rows]
    )


def packed_dft(rows):
    size = 2 * rows
    phase = (np.arange(rows)[:, None] * np.arange(rows)[None, :] % size) * (2.0 * math.pi / size)
    lower = -np.sin(phase)
    lower[0] = 1 - 2 * (np.arange(rows) % 2)
    table = np.concatenate([np.cos(phase), lower], axis=0)
    weight = np.full((size, 1), 2.0 / size)
    weight[0] = weight[rows] = 1.0 / size
    parity = 1.0 - 2.0 * (np.arange(rows) % 2)
    parity = np.concatenate([parity, parity])[:, None]
    parity[rows] = 1 - 2 * (rows % 2)
    return table.astype(np.float32), weight.astype(np.float32), parity.astype(np.float32)


def spectra_rows(table_ref, source_ref, target_ref, blocks, rows):
    for block in range(blocks):
        target_ref[block] = jnp.dot(
            table_ref[...], source_ref[pl.ds(block * rows, rows), :], preferred_element_type=F32
        ).astype(target_ref.dtype)


def convolve_kernel(blocks, rows, step, same_ref, table_ref, back_ref, filt_ref, x_ref, y_ref, spec_ref, out_ref):
    spectra_rows(table_ref, x_ref, spec_ref, blocks, rows)
    convolve_spectra(blocks, rows, step, same_ref, filt_ref, spec_ref, out_ref)
    for block in range(blocks):
        y_ref[pl.ds(block * rows, rows), :] = jnp.dot(
            back_ref[...], out_ref[block], preferred_element_type=F32
        ).astype(BF)


def correlate_kernel(
    blocks, rows, step, same_ref, table_ref, back_ref, scale_ref, filt_ref, x_ref, g_ref,
    dx_ref, dt_ref, spec_ref, grad_ref, out_ref, tap_ref,
):
    spectra_rows(table_ref, x_ref, spec_ref, blocks, rows)
    spectra_rows(table_ref, g_ref, grad_ref, blocks, rows)
    correlate_spectra(blocks, rows, step, same_ref, scale_ref, filt_ref, spec_ref, grad_ref, out_ref, tap_ref)
    for block in range(blocks):
        dx_ref[pl.ds(block * rows, rows), :] = jnp.dot(
            back_ref[...], out_ref[block], preferred_element_type=F32
        ).astype(BF)
    taps_back(blocks, rows, back_ref, scale_ref, tap_ref, dt_ref)


MESH = pl.DeviceIdType.MESH
VMEM_SPEC = pl.BlockSpec(memory_space=pltpu.VMEM)
SMEM_SPEC = pl.BlockSpec(memory_space=pltpu.SMEM)
KERNEL_BYTES = 48 * 1024 * 1024


def lasting(microseconds):
    return pl.CostEstimate(flops=0, bytes_accessed=int(microseconds * 3.69e6), transcendentals=0)


def convolve_spectra(blocks, rows, step, same_ref, filt_ref, spec_ref, out_ref):
    width = spec_ref.shape[2]

    def chunk(index, carry):
        real = pl.ds(pl.multiple_of(index * step, step), step)
        imag = pl.ds(pl.multiple_of(rows + index * step, step), step)
        first = (lax.broadcasted_iota(jnp.int32, (step, width), 0) + index * step) == 0
        for i in range(blocks):
            total_real = jnp.zeros((step, width), F32)
            total_imag = jnp.zeros((step, width), F32)
            for lag in range(i + 1):
                weight = same_ref[i, i - lag]
                fr = filt_ref[lag, real, :]
                fi = filt_ref[lag, imag, :]
                cross = jnp.where(first, 0.0, fi)
                own = jnp.where(first, fi, fr)
                xr = spec_ref[i - lag, real, :] * weight
                xi = spec_ref[i - lag, imag, :] * weight
                total_real = total_real + (fr * xr - cross * xi)
                total_imag = total_imag + (cross * xr + own * xi)
            out_ref[i, real, :] = total_real.astype(BF)
            out_ref[i, imag, :] = total_imag.astype(BF)
        return carry

    lax.fori_loop(0, rows // step, chunk, 0)


def correlate_spectra(blocks, rows, step, same_ref, scale_ref, filt_ref, spec_ref, grad_ref, out_ref, tap_ref):
    width = spec_ref.shape[2]

    def chunk(index, carry):
        real = pl.ds(pl.multiple_of(index * step, step), step)
        imag = pl.ds(pl.multiple_of(rows + index * step, step), step)
        first = (lax.broadcasted_iota(jnp.int32, (step, width), 0) + index * step) == 0
        for j in range(blocks):
            total_real = jnp.zeros((step, width), F32)
            total_imag = jnp.zeros((step, width), F32)
            for lag in range(blocks - j):
                weight = same_ref[j + lag, j]
                fr = filt_ref[lag, real, :]
                fi = filt_ref[lag, imag, :]
                cross = jnp.where(first, 0.0, fi)
                own = jnp.where(first, fi, fr)
                gr = grad_ref[j + lag, real, :] * weight
                gi = grad_ref[j + lag, imag, :] * weight
                total_real = total_real + (fr * gr + cross * gi)
                total_imag = total_imag + (own * gi - cross * gr)
            out_ref[j, real, :] = total_real.astype(BF)
            out_ref[j, imag, :] = total_imag.astype(BF)
        for lag in range(blocks):
            one = jnp.zeros((step, width), F32)
            two = jnp.zeros((step, width), F32)
            three = jnp.zeros((step, width), F32)
            for i in range(lag, blocks):
                weight = same_ref[i, i - lag]
                gr = grad_ref[i, real, :] * weight
                gi = grad_ref[i, imag, :] * weight
                xr = spec_ref[i - lag, real, :].astype(F32)
                xi = spec_ref[i - lag, imag, :].astype(F32)
                one = one + xr * gr
                two = two + xi * gi
                three = three + (xr * gi - xi * gr)
            tap_ref[lag, real, :] = (one + jnp.where(first, 0.0, two)) * scale_ref[real, 0:1]
            tap_ref[lag, imag, :] = jnp.where(first, two, three) * scale_ref[imag, 0:1]
        return carry

    lax.fori_loop(0, rows // step, chunk, 0)


def taps_back(blocks, rows, back_ref, scale_ref, tap_ref, dt_ref):
    for block in range(blocks):
        total = tap_ref[block]
        if block + 1 < blocks:
            total = total + scale_ref[:, 1:2] * tap_ref[block + 1]
        dt_ref[pl.ds(block * rows, rows), :] = jnp.dot(
            back_ref[...], total.astype(BF), preferred_element_type=F32
        )


class Peers:
    def __init__(self, send, recv):
        self.core, self.here, self.plane = lax.axis_index("section"), lax.axis_index("seq"), lax.axis_index("dp")
        here = self.here
        self.blocks = (3 - here, here + 1 - 2 * (here % 2), (here + 2) % 4)
        self.send, self.recv = send, recv
        barrier = pltpu.get_barrier_semaphore()
        for block in self.blocks:
            pl.semaphore_signal(barrier, inc=1, device_id=self.at(block), device_id_type=MESH)
        pl.semaphore_wait(barrier, 3)

    def at(self, block):
        return (self.core, block, self.plane)

    def copy(self, number, source, target_ref, block):
        return pltpu.make_async_remote_copy(
            src_ref=source, dst_ref=target_ref, send_sem=self.send.at[number], recv_sem=self.recv.at[number],
            device_id=self.at(block), device_id_type=MESH,
        )


def delayed(values, distance, before):
    index = lax.broadcasted_iota(jnp.int32, values.shape, 0)
    result = pltpu.roll(values, distance, 0)
    for row in range(distance):
        result = jnp.where(index == row, before[row], result)
    return result


def advanced(values, distance):
    rows = values.shape[0]
    index = lax.broadcasted_iota(jnp.int32, values.shape, 0)
    return jnp.where(index >= rows - distance, 0.0, pltpu.roll(values, rows - distance, 0))


def mixed_part(proj_ref, rim_ref, weight_ref, carried, columns):
    now = proj_ref[:, columns].astype(F32)
    rim = rim_ref[:, columns].astype(F32) * carried
    size = rim.shape[0]
    last, before_last = rim[size - 1 : size, :], rim[size - 2 : size - 1, :]
    one = delayed(now, 1, (last,))
    two = delayed(now, 2, (before_last, last))
    mixed = weight_ref[0:1, columns] * now + weight_ref[1:2, columns] * one + weight_ref[2:3, columns] * two
    return mixed, now, one, two


def mix_kernel(
    blocks, rows, step, same_ref, carried_ref, table_ref, back_ref, filt_ref, proj_ref, weight_ref, bias_ref, valid_ref,
    rim_out_ref, x_out_ref, filtered_ref, gated_ref,
    rim_ref, x_ref, mask_ref, signal_ref, second_ref, spec_ref, out_ref, y_ref, y_in_ref, send, recv,
):
    peers = Peers(send, recv)
    here, width = peers.here, proj_ref.shape[1] // 3
    group = width // blocks
    tail = rim_ref.shape[0]
    rim_copy = peers.copy(0, proj_ref.at[pl.ds(rows - tail, tail)], rim_ref, (here + 1) % 4)
    rim_copy.start()
    rim_copy.wait()
    carried, valid = carried_ref[0], valid_ref[...]

    def at_rows(block):
        return pl.ds(pl.multiple_of(block * rows, rows), rows)

    outgoing = []
    for number, block in enumerate(peers.blocks + (here,)):
        start = block * group

        def part(which):
            columns = pl.ds(pl.multiple_of(which * width + start, 128), group)
            return mixed_part(proj_ref, rim_ref, weight_ref, carried, columns)[0]

        signal = part(0) * part(2)
        signal_ref[block] = signal
        second_ref[block] = part(1)
        masked = (signal * valid).astype(BF)
        if number < 3:
            mask_ref[block] = masked
            item = peers.copy(1 + number, mask_ref.at[block], x_ref.at[at_rows(here)], block)
            item.start()
            outgoing.append(item)
        else:
            x_ref[at_rows(here), :] = masked
    for item in outgoing:
        item.wait()
    spectra_rows(table_ref, x_ref, spec_ref, blocks, rows)
    convolve_spectra(blocks, rows, step, same_ref, filt_ref, spec_ref, out_ref)
    rim_out_ref[...] = rim_ref[...]
    x_out_ref[...] = x_ref[...]

    def result(block):
        return jnp.dot(back_ref[...], out_ref[block], preferred_element_type=F32).astype(BF)

    outgoing = []
    for number, block in enumerate(peers.blocks):
        y_ref[block] = result(block)
        item = peers.copy(4 + number, y_ref.at[block], y_in_ref.at[here], block)
        item.start()
        outgoing.append(item)
    y_in_ref[here] = result(here)
    for number, block in enumerate((here,) + peers.blocks):
        if number:
            outgoing[number - 1].wait()
        columns = pl.ds(pl.multiple_of(block * group, 128), group)
        filtered = y_in_ref[block].astype(F32) * valid + bias_ref[:, columns] * signal_ref[block]
        filtered_ref[:, columns] = filtered.astype(filtered_ref.dtype)
        gated_ref[:, columns] = (second_ref[block] * filtered).astype(BF)


def mix(same, carried, table, back, filt, projected, weights, bias, valid, blocks, rows, number):
    width = projected.shape[1] // 3
    group = width // blocks
    return pl.pallas_call(
        functools.partial(mix_kernel, blocks, rows, 32),
        out_shape=(
            jax.ShapeDtypeStruct((16, 3 * width), BF),
            jax.ShapeDtypeStruct((blocks * rows, group), BF),
            jax.ShapeDtypeStruct((rows, width), BF),
            jax.ShapeDtypeStruct((rows, width), BF),
        ),
        in_specs=[SMEM_SPEC] * 2 + [VMEM_SPEC] * 7,
        out_specs=(VMEM_SPEC,) * 4,
        scratch_shapes=[
            pltpu.VMEM((16, 3 * width), BF),
            pltpu.VMEM((blocks * rows, group), BF),
            pltpu.VMEM((blocks, rows, group), BF),
            pltpu.VMEM((blocks, rows, group), F32),
            pltpu.VMEM((blocks, rows, group), F32),
            pltpu.VMEM((blocks, 2 * rows, group), F32),
            pltpu.VMEM((blocks, 2 * rows, group), BF),
            pltpu.VMEM((blocks, rows, group), BF),
            pltpu.VMEM((blocks, rows, group), BF),
            pltpu.SemaphoreType.DMA((7,)),
            pltpu.SemaphoreType.DMA((7,)),
        ],
        compiler_params=pltpu.CompilerParams(
            collective_id=number, has_side_effects=True, vmem_limit_bytes=KERNEL_BYTES
        ),
        name="mix",
        cost_estimate=lasting(22),
    )(same, carried, table, back, filt, projected, weights, bias, valid)


def unmix_stages(blocks, rows, step, copy, here, others, refs):
    (
        same_ref, carried_ref, table_ref, back_ref, scale_ref, filt_ref, proj_ref, rim_ref, weight_ref, bias_ref, valid_ref,
        x_ref, filtered_ref, gate_ref, dproj_ref, dweight_ref, dbias_ref, dt_ref, g_ref, mask_ref, signal_ref, spec_ref,
        grad_ref, out_ref, tap_ref, dx_ref, dx_in_ref, edge_ref, edge_in_ref, end_ref,
    ) = refs
    width = proj_ref.shape[1] // 3
    group = width // blocks
    tail = end_ref.shape[0]

    def at_rows(block):
        return pl.ds(pl.multiple_of(block * rows, rows), rows)

    def columns_of(which, block):
        return pl.ds(pl.multiple_of(which * width + block * group, 128), group)

    def part(which, block):
        return mixed_part(proj_ref, rim_ref, weight_ref, carried_ref[0], columns_of(which, block))

    there = [copy(k, mask_ref.at[block], g_ref.at[at_rows(here)], block) for k, block in enumerate(others)]
    again = [copy(3 + k, dx_ref.at[block], dx_in_ref.at[here], block) for k, block in enumerate(others)]
    edge_copy = copy(6, edge_ref, edge_in_ref, (here + 3) % 4)

    def gate():
        valid = valid_ref[...]
        for number, block in enumerate((*others, here)):
            columns = columns_of(0, block)
            signal = part(0, block)[0] * part(2, block)[0]
            through = gate_ref[:, columns].astype(F32) * part(1, block)[0]
            dbias_ref[:, columns] = jnp.sum(through * signal, axis=0, keepdims=True)
            signal_ref[block] = bias_ref[:, columns] * through
            masked = (through * valid).astype(BF)
            if number < 3:
                mask_ref[block] = masked
                there[number].start()
            else:
                g_ref[at_rows(here), :] = masked

    def convolve_back():
        spectra_rows(table_ref, x_ref, spec_ref, blocks, rows)
        for item in there:
            item.wait()
        spectra_rows(table_ref, g_ref, grad_ref, blocks, rows)
        correlate_spectra(blocks, rows, step, same_ref, scale_ref, filt_ref, spec_ref, grad_ref, out_ref, tap_ref)

        def result(block):
            return jnp.dot(back_ref[...], out_ref[block], preferred_element_type=F32).astype(BF)

        for number, block in enumerate(others):
            dx_ref[block] = result(block)
            again[number].start()
        dx_in_ref[here] = result(here)
        taps_back(blocks, rows, back_ref, scale_ref, tap_ref, dt_ref)

    def unfilter():
        valid, carried = valid_ref[...], carried_ref[0]
        for number, block in enumerate((here, *others)):
            if number:
                again[number - 1].wait()
            d_signal = dx_in_ref[block].astype(F32) * valid + signal_ref[block]
            gate_values = gate_ref[:, columns_of(0, block)].astype(F32)
            first, second, third = part(0, block), part(1, block), part(2, block)
            d_second = gate_values * filtered_ref[:, columns_of(0, block)].astype(F32)
            d_parts = (d_signal * third[0], d_second, d_signal * first[0])
            for which, (grad, views) in enumerate(zip(d_parts, (first, second, third))):
                columns = columns_of(which, block)
                weights = [weight_ref[k : k + 1, columns] for k in range(3)]
                for k in range(3):
                    dweight_ref[k : k + 1, columns] = jnp.sum(grad * views[1 + k], axis=0, keepdims=True)
                back_one, back_two = advanced(grad, 1), advanced(grad, 2)
                d_proj = weights[0] * grad + weights[1] * back_one + weights[2] * back_two
                dproj_ref[:, columns] = d_proj.astype(BF)
                end_ref[:, columns] = d_proj[rows - tail :, :]
                index = lax.broadcasted_iota(jnp.int32, (8, group), 0)
                row_zero, row_one = grad[0:1, :], grad[1:2, :]
                older = weights[2] * row_zero
                newer = weights[1] * row_zero + weights[2] * row_one
                edge = jnp.where(index == 6, older, jnp.where(index == 7, newer, 0.0))
                edge_ref[:, columns] = edge * carried
        edge_copy.start()

    def edges():
        edge_copy.wait()
        extra = jnp.concatenate([jnp.zeros((tail - 8, 3 * width), F32), edge_in_ref[...]], axis=0)
        dproj_ref[pl.ds(rows - tail, tail), :] = (end_ref[...] + extra).astype(BF)

    return gate, convolve_back, unfilter, edges


def convolve(same, table, back, filt, x_cols, blocks, rows):
    width = x_cols.shape[1]
    return pl.pallas_call(
        functools.partial(convolve_kernel, blocks, rows, min(32, rows)),
        out_shape=jax.ShapeDtypeStruct(x_cols.shape, BF),
        in_specs=[SMEM_SPEC] + [VMEM_SPEC] * 4,
        out_specs=VMEM_SPEC,
        scratch_shapes=[
            pltpu.VMEM((blocks, 2 * rows, width), F32),
            pltpu.VMEM((blocks, 2 * rows, width), BF),
        ],
        compiler_params=pltpu.CompilerParams(vmem_limit_bytes=KERNEL_BYTES),
        name="convolve",
    )(same, table, back, filt, x_cols)


def correlate(same, table, back, scale, filt, x_cols, g_cols, blocks, rows):
    width = x_cols.shape[1]
    return pl.pallas_call(
        functools.partial(correlate_kernel, blocks, rows, min(32, rows)),
        out_shape=(
            jax.ShapeDtypeStruct(x_cols.shape, BF),
            jax.ShapeDtypeStruct(x_cols.shape, F32),
        ),
        in_specs=[SMEM_SPEC] + [VMEM_SPEC] * 6,
        out_specs=(VMEM_SPEC, VMEM_SPEC),
        scratch_shapes=[
            pltpu.VMEM((blocks, 2 * rows, width), F32),
            pltpu.VMEM((blocks, 2 * rows, width), F32),
            pltpu.VMEM((blocks, 2 * rows, width), BF),
            pltpu.VMEM((blocks, 2 * rows, width), F32),
        ],
        compiler_params=pltpu.CompilerParams(vmem_limit_bytes=KERNEL_BYTES),
        name="correlate",
    )(same, table, back, scale, filt, x_cols, g_cols)


def shifted(block, axis, distance):
    devices = range(lax.axis_size(axis))
    route = [(i - distance, i) for i in devices if i - distance in devices]
    return lax.ppermute(block, axis, route)


def core_swap(block):
    return lax.ppermute(block, "section", [(0, 1), (1, 0)])


def shared_rows(rows):
    return rows // 48 * 16 if rows >= 96 else 0


def gather_kernel(chunks, heights, count, *refs):
    total, arrays = len(chunks), len(heights)
    own_refs, out_refs = refs[:arrays], refs[arrays : 2 * arrays]
    send, recv, local, stage = refs[2 * arrays :]
    sizes = [chunk[2] for chunk in chunks]
    core, here, plane = lax.axis_index("section"), lax.axis_index("seq"), lax.axis_index("dp")
    by_x, by_y, far = here + 1 - 2 * (here % 2), (here + 2) % 4, 3 - here
    odd = plane % 2
    to_x, to_y = (core, by_x, plane), (core, by_y, plane)
    to_z, to_core = (core, here, plane + 1 - 2 * odd), (1 - core, here, plane)
    barrier = pltpu.get_barrier_semaphore()
    for target in (to_x, to_y, to_z, to_core):
        pl.semaphore_signal(barrier, inc=1, device_id=target, device_id_type=MESH)
    pl.semaphore_wait(barrier, 4)

    def window(m, block, start, length):
        which, base, _, left, wide = chunks[m]
        first = (core * count + block) * heights[which] + base + start
        return out_refs[which].at[pl.ds(pl.multiple_of(first, 16), length), pl.ds(left, wide)]

    def own_window(m, start, length):
        which, base, _, left, wide = chunks[m]
        return own_refs[which].at[pl.ds(pl.multiple_of(base + start, 16), length), pl.ds(left, wide)]

    def copy(kind, m, source, target_ref, target):
        return pltpu.make_async_remote_copy(
            src_ref=source, dst_ref=target_ref, send_sem=send.at[kind, m], recv_sem=recv.at[kind, m],
            device_id=target, device_id_type=MESH,
        )

    def forward(kind, m, block, start, length, target):
        where = window(m, block, start, length)
        return copy(kind, m, where, where, target)

    started = []

    def go(item):
        item.start()
        started.append(item)
        return item

    def from_own(kind, m, start, length, target):
        return go(copy(kind, m, own_window(m, start, length), window(m, here, start, length), target))

    kept, thirds, lows, begins = [], [], [], []
    for m in range(total):
        third = shared_rows(sizes[m])
        thirds.append(third)
        begins.append(odd * third)
        lows.append(-(-(sizes[m] - third) // 32) * 16)
    direct, cross, side = {}, {}, {}

    def first_hop(m):
        length = sizes[m] - thirds[m]
        direct[m] = (
            from_own(0, m, begins[m], length, to_x), from_own(1, m, begins[m], length, to_y)
        )

    def given(m):
        return odd * (sizes[m] - thirds[m])

    def second_hop(m):
        length, low = sizes[m] - thirds[m], lows[m]
        direct[m][0].wait_recv()
        low_copy = go(forward(2, m, by_x, begins[m], low, to_y))
        if thirds[m]:
            side[m] = [go(forward(4, m, by_x, given(m), thirds[m], to_z))]
        kept.append(go(forward(7, m, by_x, begins[m], length, to_core)))
        direct[m][1].wait_recv()
        high_copy = go(forward(3, m, by_y, begins[m] + low, length - low, to_x))
        if thirds[m]:
            side[m].append(go(forward(5, m, by_y, given(m), thirds[m], to_z)))
        kept.append(go(forward(8, m, by_y, begins[m], length, to_core)))
        cross[m] = (low_copy, high_copy)

    def third_hop(m):
        length = sizes[m] - thirds[m]
        cross[m][0].wait_recv()
        cross[m][1].wait_recv()
        if thirds[m]:
            side[m].append(go(forward(6, m, far, given(m), thirds[m], to_z)))
        kept.append(go(forward(9, m, far, begins[m], length, to_core)))

    def last_hop(m):
        if thirds[m]:
            missing = (1 - odd) * (sizes[m] - thirds[m])
            for k, block in enumerate((by_x, by_y, far)):
                side[m][k].wait_recv()
                kept.append(go(forward(10 + k, m, block, missing, thirds[m], to_core)))

    first_hop(0)
    first_hop(1)
    def through(m, out):
        held = stage.at[m, pl.ds(0, sizes[m])]
        source, target = (held, window(m, here, 0, sizes[m])) if out else (own_window(m, 0, sizes[m]), held)
        return pltpu.make_async_copy(source, target, local.at[m])

    for m in range(total):
        through(m, False).start()
    for m in range(total):
        second_hop(m)
        if m + 2 < total:
            first_hop(m + 2)
        kept.append(from_own(13, m, 0, sizes[m], to_core))
        through(m, False).wait()
        through(m, True).start()
        if m >= 1:
            third_hop(m - 1)
        if m >= 2:
            last_hop(m - 2)
    third_hop(total - 1)
    for m in range(max(total - 2, 0), total):
        last_hop(m)
    for m in range(total):
        through(m, True).wait()
    for item in kept:
        item.wait_recv()
    for item in started:
        item.wait_send()


def gather_shards(shards):
    count = lax.axis_size("seq")
    core = lax.axis_index("section")
    if count != 4 or lax.axis_size("dp") % 2:
        result = []
        for shard in shards:
            whole = lax.all_gather(shard, "seq", axis=0, tiled=True)
            other = core_swap(whole)
            low = jnp.where(core == 0, whole, other)
            result.append(jnp.concatenate([low, jnp.where(core == 0, other, whole)], axis=0))
        return result
    heights = [shard.shape[0] for shard in shards]
    chunks = []
    for which, shard in enumerate(shards):
        high, wide = min(shard.shape[0], 256), min(shard.shape[1], 1024)
        for base in range(0, shard.shape[0], high):
            chunks += [(which, base, high, left, wide) for left in range(0, shard.shape[1], wide)]
    return pl.pallas_call(
        functools.partial(gather_kernel, chunks, heights, count),
        out_shape=[jax.ShapeDtypeStruct((2 * count * a.shape[0], a.shape[1]), a.dtype) for a in shards],
        in_specs=[pl.BlockSpec(memory_space=pl.ANY)] * len(shards),
        out_specs=[pl.BlockSpec(memory_space=pl.ANY)] * len(shards),
        scratch_shapes=[
            pltpu.SemaphoreType.DMA((14, len(chunks))),
            pltpu.SemaphoreType.DMA((14, len(chunks))),
            pltpu.SemaphoreType.DMA((len(chunks),)),
            pltpu.VMEM((len(chunks), max(c[2] for c in chunks), max(c[4] for c in chunks)), shards[0].dtype),
        ],
        compiler_params=pltpu.CompilerParams(
            collective_id=0, has_side_effects=True, vmem_limit_bytes=KERNEL_BYTES
        ),
        name="gather_shards",
        cost_estimate=lasting(190),
    )(*shards)


def core_halves(core, values):
    width = values.shape[1] // 2
    return (
        lax.dynamic_slice_in_dim(values, core * width, width, 1),
        lax.dynamic_slice_in_dim(values, (1 - core) * width, width, 1),
    )


X_FIRST = (0, 2, 1, 3)
Y_FIRST = (0, 1, 2, 3)
PARTS = 4


def reduce_kernel(items, rest, halves, counts, planes, order, mixing, *refs):
    whole = len(items)
    total = whole + len(rest)

    def take(number):
        nonlocal refs
        first, refs = refs[:number], refs[number:]
        return first

    mix_in = take(14 if mixing else 0)
    lefts, rights, packs, rest_in = take(counts[0]), take(counts[1]), take(counts[2]), take(len(rest))
    mix_out = take(4 if mixing else 0)
    own_out = take(total)
    other_out = dict(zip(planes, take(len(planes))))
    mix_scratch = take(12 if mixing else 0)
    hold, inbox, far_in, near_in = take(total), take(whole), take(whole), take(whole)
    plane_in, cross_in = dict(zip(planes, take(len(planes)))), dict(zip(planes, take(len(planes))))
    turned = take(counts[0])
    send, recv, local = take(3)
    core, here, plane = lax.axis_index("section"), lax.axis_index("seq"), lax.axis_index("dp")
    by_x, by_y, far = here + 1 - 2 * (here % 2), (here + 2) % 4, 3 - here
    to_x, to_y, to_core = (core, by_x, plane), (core, by_y, plane), (1 - core, here, plane)
    to_inner = (core, here, (plane + 3) // 3)
    to_outer = (core, here, 3 * (plane // 2))
    to_cross = (core, here, 3 - plane)
    outer = jnp.logical_or(plane == 0, plane == 3)
    inner = jnp.logical_and(plane > 0, plane < 3)

    barrier = pltpu.get_barrier_semaphore()

    def greet(target):
        pl.semaphore_signal(barrier, inc=1, device_id=target, device_id_type=MESH)

    in_plane = [to_x, to_y, to_core] + ([(core, far, plane)] if mixing else [])
    for target in in_plane:
        greet(target)

    @pl.when(outer)
    def _():
        greet(to_inner)
        pl.semaphore_wait(barrier, len(in_plane) + 1)

    @pl.when(inner)
    def _():
        greet(to_outer)
        greet(to_cross)
        pl.semaphore_wait(barrier, len(in_plane) + 2)

    stages = ()
    if mixing:
        mix_send, mix_recv = take(2)

        def mix_copy(number, source, target_ref, block):
            return pltpu.make_async_remote_copy(
                src_ref=source, dst_ref=target_ref, send_sem=mix_send.at[number], recv_sem=mix_recv.at[number],
                device_id=(core, block, plane), device_id_type=MESH,
            )

        stages = unmix_stages(*mixing, mix_copy, here, (far, by_x, by_y), (*mix_in, *mix_out, *mix_scratch))

    def copy(kind, m, source, target_ref, target):
        return pltpu.make_async_remote_copy(
            src_ref=source, dst_ref=target_ref, send_sem=send.at[kind, m], recv_sem=recv.at[kind, m],
            device_id=target, device_id_type=MESH,
        )

    heights = [item[0] for item in items] + [shape[0] for shape in rest]

    def rows_of(ref, m, slot, slots=1):
        rows = heights[m]
        return ref[m].at[pl.ds(slot * rows, slots * rows)]

    def copies(m):
        along_x = m < whole and items[m][5] == X_FIRST
        return dict(
            load=lambda: pltpu.make_async_copy(rest_in[m - whole], hold[m], local.at[m]),
            core=lambda: copy(0, m, hold[m], inbox[m], to_core),
            far=lambda: copy(1, m, rows_of(hold, m, 2, 2), far_in[m], to_x if along_x else to_y),
            near=lambda: copy(2, m, rows_of(hold, m, 1), near_in[m], to_y if along_x else to_x),
            inward=lambda: copy(3, m, rows_of(hold, m, 0), plane_in[m], to_inner),
            cross=lambda: copy(4, m, rows_of(hold, m, 0), cross_in[m], to_cross),
            outward=lambda: copy(3, m, rows_of(hold, m, 0), plane_in[m], to_outer),
            last_held=lambda: copy(5, m, rows_of(hold, m, 0), other_out[m], to_core),
            last_got=lambda: copy(5, m, plane_in[m], other_out[m], to_core),
            held=lambda: pltpu.make_async_copy(rows_of(hold, m, 0), own_out[m], local.at[m]),
            got=lambda: pltpu.make_async_copy(plane_in[m], own_out[m], local.at[m]),
        )

    moves = [copies(m) for m in range(total)]

    def fill(m, slot, side, adds):
        rows, columns, left, right, first, order = items[m]
        block = {0: here, 1: by_x, 2: by_y, 3: far}[order[slot]]
        wide = columns if columns <= 768 else 512
        high = min(rows, max(256, 131072 // wide))
        across = columns // wide
        start = side * halves[right] + first if right >= 0 else side * columns

        def step(index, carry):
            down, along = index // across, index % across
            picked = pl.ds(pl.multiple_of(block * rows + down * high, 128 if right >= 0 else 16), high)
            which = pl.ds(pl.multiple_of(start + along * wide, 128), wide)
            if right >= 0:
                value = dot(turned[left][picked, :], rights[right][:, which])
            else:
                value = packs[left][picked, which]
            where = pl.ds(pl.multiple_of(along * wide, 128), wide)
            for ref, base in adds:
                value = value + ref[m][pl.ds(pl.multiple_of(base * rows + down * high, 16), high), where].astype(F32)
            hold[m][pl.ds(pl.multiple_of(slot * rows + down * high, 16), high), where] = value.astype(BF)
            return carry

        lax.fori_loop(0, rows // high * across, step, 0)

    def add_plane(m, ref):
        rows = heights[m]
        high = min(rows, 64)

        def step(index, carry):
            where = pl.ds(pl.multiple_of(index * high, 16), high)
            value = hold[m][where, :].astype(F32) + ref[m][where, :].astype(F32)
            hold[m][where, :] = value.astype(BF)
            return carry

        lax.fori_loop(0, rows // high, step, 0)

    def to_other_core(m):
        for slot in (2, 3, 1, 0):
            fill(m, slot, 1 - core, [])
        moves[m]["core"]().start()

    def prepare(m):
        moves[m]["core"]().wait()
        for slot in (2, 3):
            fill(m, slot, core, [(inbox, slot)])

    def first_hop(m):
        moves[m]["far"]().start()

    def landed(m):
        moves[m]["far"]().wait_recv()

    def second_hop(m):
        fill(m, 1, core, [(inbox, 1), (far_in, 1)])
        moves[m]["near"]().start()

    def arrive(m):
        moves[m]["near"]().wait_recv()
        fill(m, 0, core, [(inbox, 0), (far_in, 0), (near_in, 0)])
        if m in planes:

            @pl.when(outer)
            def _():
                moves[m]["inward"]().start()
        else:
            moves[m]["held"]().start()

    def meet(m):
        @pl.when(inner)
        def _():
            moves[m]["inward"]().wait_recv()
            add_plane(m, plane_in)
            moves[m]["cross"]().start()

    def settle(m):
        @pl.when(inner)
        def _():
            moves[m]["cross"]().wait()
            add_plane(m, cross_in)
            moves[m]["outward"]().start()
            moves[m]["last_held"]().start()
            moves[m]["held"]().start()

    def finish(m):
        @pl.when(outer)
        def _():
            moves[m]["inward"]().wait()
            moves[m]["last_got"]().start()
            moves[m]["got"]().start()

    def begin(m):
        moves[m]["load"]().wait()

        @pl.when(outer)
        def _():
            moves[m]["inward"]().start()

    names = dict(
        core=to_other_core, fill=prepare, go=first_hop, wait=landed, turn=second_hop, own=arrive, meet=meet, settle=settle,
        finish=finish, load=begin,
    )
    for m in range(whole, total):
        moves[m]["load"]().start()
    def turn_over(left, target):
        def step(index, carry):
            where = pl.ds(pl.multiple_of(index * 256, 256), 256)
            target[where, :] = left[:, where].T
            return carry

        lax.fori_loop(0, left.shape[1] // 256, step, 0)

    for left, target in zip(lefts, turned):
        turn_over(left, target)
    for step, pair in order:
        if step == "mix":
            stages[pair]()
            continue
        for m in (2 * pair, 2 * pair + 1):
            names[step](m)

    for m in range(total):
        if m < whole:
            moves[m]["far"]().wait_send()
            moves[m]["near"]().wait_send()
        if m in planes:

            @pl.when(inner)
            def _():
                moves[m]["outward"]().wait_send()
                moves[m]["last_held"]().wait()
                moves[m]["held"]().wait()

            @pl.when(outer)
            def _():
                moves[m]["last_got"]().wait()
                moves[m]["got"]().wait()
        else:
            moves[m]["held"]().wait()


def reduce_order(pairs, rest):
    steps = [("load", k) for k in rest[:1]] + [("core", pairs[0]), ("fill", pairs[0]), ("go", pairs[0])]
    steps += [("core", k) for k in pairs[1:3]] + [("fill", pairs[1])]

    def across(step):
        for name, late in (("meet", 0), ("settle", 1), ("finish", 2)):
            for flow in (rest, [None, *pairs]):
                if 0 <= step - late < len(flow) and flow[step - late] is not None:
                    yield name, flow[step - late]

    for i, pair in enumerate(pairs):
        steps.append(("wait", pair))
        if i + 1 < len(pairs):
            steps.append(("go", pairs[i + 1]))
        steps.append(("turn", pair))
        steps += [("load", k) for k in rest[i + 1 : i + 2]]
        if i + 3 < len(pairs):
            steps.append(("core", pairs[i + 3]))
        if i + 2 < len(pairs):
            steps.append(("fill", pairs[i + 2]))
        waiting = list(across(i))
        steps += [item for item in waiting if item[0] == "meet"]
        steps.append(("own", pair))
        steps += [item for item in waiting if item[0] != "meet"]
    for i in range(len(pairs), max(len(pairs), len(rest)) + 3):
        steps += across(i)
    return steps


def mixing_order(rest, summed):
    words = (
        "load0 mix0 core0 core1 fill0 go0 load1 core2 fill1 go1 core3 mix1 load2 fill2 wait0 turn0 go2 meet0 fill3 wait1 turn1 "
        "go3 meet1 load3 own0 mix2 settle0 meet2 own1 wait2 turn2 settle1 finish0 meet3 own2 Meet0 wait3 turn3 settle2 finish1 "
        "Meet1 mix3 own3 settle3 Settle0 finish2 Settle1 finish3 Finish0 Finish1"
    )
    steps = []
    for word in words.split():
        name, number = word[:-1], int(word[-1])
        if name in ("load", "meet", "settle", "finish"):
            steps += [(name, rest[number])] if number < len(rest) else []
        elif name in ("Meet", "Settle", "Finish"):
            steps += [(name.lower(), number)] if number < summed else []
        else:
            steps.append((name, number))
    return steps


def mlp_items(up, down, wide_up, wide_down):
    items = []
    for part in range(PARTS):
        items += [
            (up, wide_up // PARTS, 0, 0, part * wide_up // PARTS, X_FIRST),
            (down, wide_down // PARTS, 1, 1, part * wide_down // PARTS, Y_FIRST),
        ]
    return items


def reduce_call(items, lefts, rights, packs, rest, planes, order, number, mixing=None, mix_in=()):
    halves = [right.shape[1] // 2 for right in rights]
    pieces = [item[:2] for item in items] + [piece.shape for piece in rest]
    whole, total = len(items), len(pieces)
    planes = list(planes) + list(range(whole, total))
    across = [pieces[m] for m in planes]

    def buffers(slots, shapes):
        return [pltpu.VMEM((slots * shape[0], shape[1]), BF) for shape in shapes]

    mix_out, scratch = [], []
    if mixing:
        blocks, rows, _ = mixing
        width = mix_in[6].shape[1] // 3
        group = width // blocks
        mix_out = [
            jax.ShapeDtypeStruct((rows, 3 * width), BF),
            jax.ShapeDtypeStruct((3, 3 * width), F32),
            jax.ShapeDtypeStruct((1, width), F32),
            jax.ShapeDtypeStruct((blocks * rows, group), F32),
        ]
        scratch = [
            pltpu.VMEM((blocks * rows, group), BF),
            pltpu.VMEM((blocks, rows, group), BF),
            pltpu.VMEM((blocks, rows, group), F32),
            pltpu.VMEM((blocks, 2 * rows, group), BF),
            pltpu.VMEM((blocks, 2 * rows, group), F32),
            pltpu.VMEM((blocks, 2 * rows, group), BF),
            pltpu.VMEM((blocks, 2 * rows, group), F32),
            pltpu.VMEM((blocks, rows, group), BF),
            pltpu.VMEM((blocks, rows, group), BF),
            pltpu.VMEM((8, 3 * width), F32),
            pltpu.VMEM((8, 3 * width), F32),
            pltpu.VMEM((16, 3 * width), F32),
        ]
    hbm = pl.BlockSpec(memory_space=pl.ANY)
    scratch += buffers(4, pieces[:whole]) + buffers(1, pieces[whole:])
    for slots in (4, 2, 1):
        scratch += buffers(slots, pieces[:whole])
    scratch += buffers(1, across) + buffers(1, across)
    scratch += [pltpu.VMEM((left.shape[1], left.shape[0]), left.dtype) for left in lefts]
    scratch += [pltpu.SemaphoreType.DMA((6, total)), pltpu.SemaphoreType.DMA((6, total)), pltpu.SemaphoreType.DMA((total,))]
    if mixing:
        scratch += [pltpu.SemaphoreType.DMA((7,)), pltpu.SemaphoreType.DMA((7,))]
    counts = (len(lefts), len(rights), len(packs))
    result = pl.pallas_call(
        functools.partial(reduce_kernel, items, pieces[whole:], halves, counts, planes, order, mixing),
        out_shape=mix_out + [jax.ShapeDtypeStruct(shape, BF) for shape in pieces + across],
        in_specs=[SMEM_SPEC] * min(len(mix_in), 2) + [VMEM_SPEC] * max(len(mix_in) - 2, 0)
        + [VMEM_SPEC] * sum(counts) + [hbm] * len(rest),
        out_specs=[VMEM_SPEC] * len(mix_out) + [hbm] * (total + len(planes)),
        scratch_shapes=scratch,
        compiler_params=pltpu.CompilerParams(
            collective_id=number, has_side_effects=True, vmem_limit_bytes=60 * 1024 * 1024
        ),
        name="unmix_reduce" if mixing else "reduce",
        cost_estimate=lasting(90),
    )(*mix_in, *lefts, *rights, *packs, *rest)
    mixed, own, other = result[: len(mix_out)], result[len(mix_out) : len(mix_out) + total], result[len(mix_out) + total :]
    return mixed, list(own), dict(zip(planes, other))


def reduce_plain(lefts, rights, packed, core):
    count = lax.axis_size("seq")
    chips = []
    for left, right in zip(lefts, rights):
        keep, send = core_halves(core, right)
        chips.append(dot_left(left, keep) + core_swap(dot_left(left, send).astype(BF)).astype(F32))
    keep, send = core_halves(core, packed)
    small = (keep + core_swap(send.astype(BF)).astype(F32)).astype(BF)
    up, down, enter, leave = (chip.astype(BF) for chip in chips)
    out_rows, half = leave.shape[0] // count, leave.shape[1]
    leave = jnp.concatenate([leave.reshape(count, out_rows, half), small.reshape(count, -1, half)], axis=1)
    own = []
    for chip in (up, down, enter, leave.reshape(-1, half)):
        own.append(lax.psum(lax.psum_scatter(chip, "seq", scatter_dimension=0, tiled=True), "dp"))
    return own[:3] + [own[3][:out_rows], own[3][out_rows:]]


def body(
    tokens, out_grad, lengths, ln1_gain, w_in, short_w, filt_in, filt_shift, sine_freq, filt_out,
    decay, filter_bias, w_out, ln2_gain, mlp_up, mlp_down,
):
    micro, rows, width = tokens.shape
    count = lax.axis_size("seq")
    here = lax.axis_index("seq")
    core = lax.axis_index("section")
    routed = count == 4 and lax.axis_size("dp") == 4
    slots = rows * count
    col_width = width // count
    hidden = mlp_up.shape[2]
    hidden_block = hidden // count
    half_block = hidden_block // 2
    table_np, weight_np, parity_np = packed_dft(rows)
    table = jnp.asarray(table_np).astype(BF)
    back = jnp.asarray(np.ascontiguousarray(table_np.T)).astype(BF)
    scale = jnp.asarray(np.concatenate([weight_np, parity_np], axis=1))
    embedding = jnp.asarray(positions_embedding(slots, FREQS))

    others = (ln1_gain, short_w, filt_in, filt_shift, sine_freq, decay, filter_bias, ln2_gain)
    other_shapes = [a.shape[1:] for a in others]
    other_sizes = [math.prod(shape) for shape in other_shapes]
    other_axis = (0, 1, 1, 0, 0, 0, 0, 0)
    lane, out_rows = width, filt_out.shape[1]
    other_rows = -(-sum(other_sizes) // lane)
    packed_rows = -(-(out_rows + other_rows) // 16) * 16

    def packed_small(top, parts):
        flat = jnp.concatenate(parts, axis=-1)
        lead = flat.shape[:-1]
        none = ((0, 0),) * len(lead)
        flat = jnp.pad(flat, none + ((0, other_rows * lane - flat.shape[-1]),)).reshape(lead + (other_rows, lane))
        flat = jnp.pad(flat, none + ((0, packed_rows - out_rows - other_rows), (0, 0)))
        return jnp.concatenate([top, flat], axis=-2)

    flat = packed_small(filt_out[0], [a.reshape(-1) for a in others])
    flat_all, out_all, in_all, up_all, down_all = gather_shards([flat, w_out[0], w_in[0], mlp_up[0], mlp_down[0]])
    everywhere = flat_all.reshape(2, count, packed_rows, lane)
    gathered = [
        (
            in_all[layer * width : (layer + 1) * width], out_all[layer * width : (layer + 1) * width],
            up_all[layer * width : (layer + 1) * width], down_all[layer * hidden : (layer + 1) * hidden],
        )
        for layer in range(2)
    ]

    def small_of(layer):
        found = []
        offset = 0
        below = everywhere[layer, :, out_rows : out_rows + other_rows].reshape(count, other_rows * lane)
        for shape, size, axis in zip(other_shapes, other_sizes, other_axis):
            part = below[:, offset : offset + size].reshape((count,) + shape)
            part = jnp.moveaxis(part, 0, axis)
            full = list(shape)
            full[axis] = shape[axis] * count
            found.append(part.reshape(full).astype(F32))
            offset += size
        top = everywhere[layer, :, :out_rows].reshape(count * out_rows, lane).astype(F32)
        return found[:5] + [top] + found[5:]

    length_row = lax.dynamic_index_in_dim(lengths, core, 0, keepdims=False)
    index_all = jnp.arange(count, dtype=jnp.int32)
    started = jnp.logical_and(length_row[None, :] > 0, index_all[None, :] <= index_all[:, None])
    regions = jnp.max(jnp.where(started, index_all[None, :], 0), axis=1)
    doc_length = jnp.sum(jnp.where(regions[:, None] == index_all[None, :], length_row[None, :], 0), axis=1)
    own_region = jnp.sum(jnp.where(index_all == here, regions, 0))
    own_length = jnp.sum(jnp.where(index_all == here, doc_length, 0))
    last_region = jnp.sum(jnp.where(index_all == here - 1, regions, 0))
    offsets = (here - own_region) * rows + jnp.arange(rows, dtype=jnp.int32)
    valid = (offsets < own_length).astype(F32)[:, None]
    carried_on = jnp.logical_and(here > 0, last_region == own_region).astype(F32)
    same = (regions[:, None] == regions[None, :]).astype(F32)

    def to_columns(values):
        return lax.all_to_all(values.astype(BF), "seq", split_axis=1, concat_axis=0, tiled=True)

    def to_rows(values):
        return lax.all_to_all(values, "seq", split_axis=0, concat_axis=1, tiled=True).astype(F32)

    def filter_stage(layer):
        _, _, in_w, shift_w, freq_w, out_w, decay_w, _, _ = small_of(layer)
        out_cols = lax.dynamic_slice_in_dim(out_w, here * col_width, col_width, 1)
        decay_cols = lax.dynamic_slice_in_dim(decay_w, here * col_width, col_width, 0)
        taps, pull = jax.vjp(
            lambda *p: filter_taps(*p, embedding), in_w, shift_w, freq_w, out_cols, decay_cols
        )
        spectra = jnp.einsum(
            "fs,msc->mfc", table, taps.astype(BF).reshape(count, rows, col_width), preferred_element_type=F32
        )
        before = jnp.concatenate([jnp.zeros_like(spectra[:1]), spectra[:-1]], axis=0)
        return (spectra + scale[:, 1:2] * before) * scale[:, 0:1], pull

    def forward(layer_in, layer):
        gain_one, short_weights, _, _, _, _, _, bias, gain_two = small_of(layer)
        in_matrix, out_matrix, up_matrix, down_matrix = gathered[layer]
        filt, pull = filter_stage(layer)
        normed = layer_norm(layer_in, gain_one).astype(BF)
        projected = dot(normed, in_matrix).astype(BF)
        if routed:
            rim, x_cols, filtered, gated = mix(
                same, carried_on.reshape(1), table, back, filt, projected, short_weights, bias[None], valid, count, rows, 3 + layer
            )
        else:
            rim = shifted(projected[rows - 2 :], "seq", 1)
            mixed = short_mix(rim.astype(F32), projected.astype(F32), short_weights, carried_on)
            first, second, third = mixed[:, :width], mixed[:, width : 2 * width], mixed[:, 2 * width :]
            signal = first * third
            x_cols = to_columns(signal * valid)
            y_cols = convolve(same, table, back, filt, x_cols, count, rows)
            filtered = to_rows(y_cols) * valid + bias * signal
            gated = (second * filtered).astype(BF)
        residual = layer_in + dot(gated, out_matrix)
        normed_two = layer_norm(residual, gain_two).astype(BF)
        upward = dot(normed_two, up_matrix)
        active = gelu_tanh(upward).astype(BF)
        layer_out = residual + dot(active, down_matrix)
        stored = (
            layer_in, normed, projected, rim, filtered, gated, residual, normed_two,
            upward, active, x_cols, filt, pull,
        )
        return layer_out.astype(BF), stored

    def backward(upstream, stored, layer, rest):
        (
            layer_in, normed, projected, rim, filtered, gated, residual, normed_two,
            upward, active, x_cols, filt, pull,
        ) = stored
        gain_one, short_weights, in_w, shift_w, freq_w, out_w, decay_w, bias, gain_two = small_of(layer)
        in_matrix, out_matrix, up_matrix, down_matrix = gathered[layer]
        grad_hidden = jax.vjp(gelu_tanh, upward)[1](dot_right(upstream, down_matrix))[0].astype(BF)
        grad_norm_two = dot_right(grad_hidden, up_matrix)
        grad_resid_norm, grad_gain_two = jax.vjp(layer_norm, residual, gain_two)[1](grad_norm_two)
        grad_residual = upstream.astype(F32) + grad_resid_norm
        grad_branch = grad_residual.astype(BF)
        grad_gated = dot_right(grad_branch, out_matrix)
        if routed:
            mix_in = (
                same, carried_on.reshape(1), table, back, scale, filt, projected, rim, short_weights, bias[None], valid,
                x_cols, filtered, grad_gated.astype(BF),
            )
            block_rows = width // count
            items = mlp_items(block_rows, hidden_block, hidden // 2, width // 2)
            summed = 0 if layer else PARTS // 2
            order = mixing_order(list(range(PARTS, PARTS + len(rest) // 2)), summed)
            (grad_proj, grad_short, grad_bias, grad_taps), own, other = reduce_call(
                items, [normed_two, active], [grad_hidden, upstream], [], rest, range(2 * summed), order, 5 + layer,
                (count, rows, 32), mix_in,
            )
            grad_bias = grad_bias[0]
        else:
            mixed = short_mix(rim.astype(F32), projected.astype(F32), short_weights, carried_on)
            first, second, third = mixed[:, :width], mixed[:, width : 2 * width], mixed[:, 2 * width :]
            signal = first * third
            grad_second = grad_gated * filtered
            grad_filtered = grad_gated * second
            grad_bias = jnp.sum(grad_filtered * signal, axis=0)
            g_cols = to_columns(grad_filtered * valid)
            dx_cols, grad_taps = correlate(same, table, back, scale, filt, x_cols, g_cols, count, rows)
            grad_signal = to_rows(dx_cols) * valid + bias * grad_filtered
            grad_mixed = jnp.concatenate([grad_signal * third, grad_second, grad_signal * first], axis=1)
            short_pull = jax.vjp(
                lambda a, b, c: short_mix(a, b, c, carried_on), rim.astype(F32), projected.astype(F32), short_weights
            )[1]
            grad_rim, grad_proj, grad_short = short_pull(grad_mixed)
            returned = shifted(grad_rim, "seq", -1)
            tail = grad_proj[rows - 2 :] + returned
            grad_proj = jnp.concatenate([grad_proj[: rows - 2], tail], axis=0)
            grad_proj = grad_proj.astype(BF)
        grad_normed = dot_right(grad_proj, in_matrix)
        grad_norm_in, grad_gain_one = jax.vjp(layer_norm, layer_in, gain_one)[1](grad_normed)
        grad_layer_in = (grad_residual + grad_norm_in).astype(BF)
        d_in, d_shift, d_freq, d_out_cols, d_decay_cols = pull(grad_taps)
        d_out = lax.dynamic_update_slice_in_dim(jnp.zeros_like(out_w), d_out_cols, here * col_width, 1)
        d_decay = lax.dynamic_update_slice_in_dim(jnp.zeros_like(decay_w), d_decay_cols, here * col_width, 0)
        parts = []
        other_grads = (grad_gain_one, grad_short, d_in, d_shift, d_freq, d_decay, grad_bias, grad_gain_two)
        for grad, shape, axis in zip(other_grads, other_shapes, other_axis):
            split = list(grad.shape)
            split[axis : axis + 1] = [count, shape[axis]]
            parts.append(jnp.moveaxis(grad.reshape(split), axis, 0).reshape(count, -1))
        packed = packed_small(d_out.reshape(count, out_rows, lane), parts).reshape(count * packed_rows, lane)
        if routed:
            return grad_layer_in, (own, other, normed, grad_proj, gated, grad_branch, packed)
        factors = ([normed_two, active, normed, gated], [grad_hidden, upstream, grad_proj, grad_branch], packed)
        return grad_layer_in, factors

    def row_of(values):
        return lax.dynamic_index_in_dim(values, core, 0, keepdims=False)

    out_first, stored_first = forward(row_of(tokens).astype(F32), 0)
    out_second, stored_second = forward(out_first.astype(F32), 1)
    if routed:
        grad_second, kept_second = backward(row_of(out_grad), stored_second, 1, [])
        grad_first, kept_first = backward(grad_second, stored_first, 0, kept_second[0])
        items, lefts, rights, packs = [], [], [], []
        for k, (_, _, normed, grad_proj, gated, grad_branch, packed) in enumerate((kept_second, kept_first)):
            lefts += [normed, gated]
            rights += [grad_proj, grad_branch]
            packs.append(packed)
            block_rows, part = width // count, 3 * width // 2 // PARTS
            for piece in range(PARTS):
                order = Y_FIRST if piece % 2 else X_FIRST
                items.append((block_rows, part, 2 * k, 2 * k, piece * part, order))
            items.append((block_rows, width // 2, 2 * k + 1, 2 * k + 1, 0, X_FIRST))
            items.append((packed_rows, lane // 2, k, -1, 0, Y_FIRST))
        each, mlp = PARTS + 2, 2 * PARTS
        done = 2 * (PARTS // 2)
        order = reduce_order([0, 1, 3, 4, 2, 5], list(range(each, each + PARTS - done // 2)))
        _, own, other = reduce_call(items, lefts, rights, packs, kept_first[0][done:mlp], range(2 * each), order, 1)
        other = [other[m] for m in range(2 * each + mlp - done)]

        def assembled(late, mlp_part):
            groups = (mlp_part[::2], mlp_part[1::2], late[:PARTS])
            return [jnp.concatenate(group, axis=1) for group in groups] + list(late[PARTS:])

        second_other = [kept_first[1][m] for m in range(mlp, 2 * mlp)]
        own_second, other_second = assembled(own[:each], kept_first[0][mlp:]), assembled(other[:each], second_other)
        own_first = assembled(own[each : 2 * each], kept_first[0][:done] + own[2 * each :])
        first_other = [kept_first[1][m] for m in range(done)]
        other_first = assembled(other[each : 2 * each], first_other + other[2 * each :])
    else:
        grad_second, factors_second = backward(row_of(out_grad), stored_second, 1, [])
        own_second = reduce_plain(*factors_second, core)
        grad_first, factors_first = backward(grad_second, stored_first, 0, [])
        own_first = reduce_plain(*factors_first, core)
        other_first, other_second = ([core_swap(part) for part in own] for own in (own_first, own_second))

    def both_rows(of_first, of_second):
        kept = jnp.where(core == 0, of_first, of_second)
        received = core_swap(jnp.where(core == 0, of_second, of_first))
        return jnp.stack([jnp.where(core == 0, kept, received), jnp.where(core == 0, received, kept)])[None]

    layer_outputs = both_rows(out_first, out_second)
    input_grads = both_rows(grad_first, grad_second)

    def finish(index):
        low = jnp.where(core == 0, own_first[index], other_second[index])
        high = jnp.where(core == 0, other_first[index], own_second[index])
        return jnp.concatenate([low, high], axis=1).astype(F32)

    grad_up, grad_down, grad_in, grad_out = (finish(index) for index in range(4))
    small_total = finish(4)
    below = small_total[out_rows : out_rows + other_rows].reshape(-1)
    other_out = []
    offset = 0
    for shape, size in zip(other_shapes, other_sizes):
        other_out.append(below[offset : offset + size].reshape((1,) + shape))
        offset += size
    g_ln1, g_short, g_fin, g_shift, g_freq, g_decay, g_bias, g_ln2 = other_out
    g_fout = small_total[:out_rows][None]
    return (
        layer_outputs, input_grads, g_ln1, grad_in[None], g_short, g_fin, g_shift, g_freq, g_fout, g_decay, g_bias,
        grad_out[None], g_ln2, grad_up[None], grad_down[None],
    )


def solution(mesh):
    vector = P("section", "seq")
    matrix = P("section", "seq", None)
    last = P("section", None, "seq")
    tokens = P("dp", "seq", None)
    outputs = P("section", "dp", "seq", None)
    in_specs = (
        tokens, tokens, P("dp", None), vector, matrix, last, last, vector, vector, matrix, vector, vector, matrix,
        vector, matrix, matrix,
    )
    out_specs = (
        outputs, outputs, vector, matrix, last, last, vector, vector, matrix, vector, vector, matrix, vector, matrix,
        matrix,
    )
    return jax.shard_map(body, mesh=mesh, in_specs=in_specs, out_specs=out_specs, check_vma=False)
```

```python
import functools
import math

import jax
import jax.numpy as jnp
import numpy as np
from jax import lax
from jax.experimental import pallas as pl
from jax.experimental.pallas import tpu as pltpu
from jax.sharding import PartitionSpec as P

FREQS = 16
PRECISE = lax.Precision.HIGHEST
EPSILON = 1e-05
BF = jnp.bfloat16
F32 = jnp.float32


def dot(left, right):
    return jnp.dot(left, right, preferred_element_type=F32)


def dot_left(left, right):
    return lax.dot_general(left, right, (((0,), (0,)), ((), ())), preferred_element_type=F32)


def dot_right(left, right):
    return lax.dot_general(left, right, (((1,), (1,)), ((), ())), preferred_element_type=F32)


def layer_norm(values, gains):
    row_mean = jnp.mean(values, axis=-1, keepdims=True)
    centered = values - row_mean
    variance = jnp.mean(centered * centered, axis=-1, keepdims=True)
    return centered * lax.rsqrt(variance + EPSILON) * gains


def gelu_tanh(values):
    return jax.nn.gelu(values, approximate=True)


def positions_embedding(slots, harmonic_count):
    steps_all = np.arange(slots)
    scaled = steps_all / slots
    harmonics = np.arange(1, harmonic_count + 1)
    phase = (steps_all[:, None] * harmonics[None, :] % slots) * (2.0 * math.pi / slots)
    both = np.concatenate([scaled[:, None], np.cos(phase), np.sin(phase)], axis=1)
    return both.astype(np.float32)


def filter_taps(filt_in, filt_shift, sine_freq, filt_out, decay, embedding):
    slots = embedding.shape[0]
    inner = jnp.dot(embedding, filt_in, preferred_element_type=F32, precision=PRECISE)
    hidden_sine = jnp.sin(sine_freq * (inner + filt_shift))
    scaled = jnp.arange(slots, dtype=jnp.int32).astype(F32) / slots
    summed = jnp.dot(hidden_sine, filt_out, preferred_element_type=F32, precision=PRECISE)
    return summed * jnp.exp(-decay[None, :] * scaled[:, None])


def short_mix(rim_values, proj_values, weight_values, carried_on):
    total_rows = proj_values.shape[0]
    extended = jnp.concatenate([rim_values * carried_on, proj_values], axis=0)
    return (
        weight_values[0] * extended[2:]
        + weight_values[1] * extended[1 : total_rows + 1]
        + weight_values[2] * extended[:total_rows]
    )


def packed_dft(rows):
    size = 2 * rows
    phase = (np.arange(rows)[:, None] * np.arange(rows)[None, :] % size) * (2.0 * math.pi / size)
    lower = -np.sin(phase)
    lower[0] = 1 - 2 * (np.arange(rows) % 2)
    table = np.concatenate([np.cos(phase), lower], axis=0)
    weight = np.full((size, 1), 2.0 / size)
    weight[0] = weight[rows] = 1.0 / size
    parity = 1.0 - 2.0 * (np.arange(rows) % 2)
    parity = np.concatenate([parity, parity])[:, None]
    parity[rows] = 1 - 2 * (rows % 2)
    return table.astype(np.float32), weight.astype(np.float32), parity.astype(np.float32)


def spectra_rows(table_ref, source_ref, target_ref, blocks, rows):
    for block in range(blocks):
        target_ref[block] = jnp.dot(
            table_ref[...], source_ref[pl.ds(block * rows, rows), :], preferred_element_type=F32
        ).astype(target_ref.dtype)


def convolve_kernel(blocks, rows, step, same_ref, table_ref, back_ref, filt_ref, x_ref, y_ref, spec_ref, out_ref):
    spectra_rows(table_ref, x_ref, spec_ref, blocks, rows)
    convolve_spectra(blocks, rows, step, same_ref, filt_ref, spec_ref, out_ref)
    for block in range(blocks):
        y_ref[pl.ds(block * rows, rows), :] = jnp.dot(
            back_ref[...], out_ref[block], preferred_element_type=F32
        ).astype(BF)


def correlate_kernel(
    blocks, rows, step, same_ref, table_ref, back_ref, scale_ref, filt_ref, x_ref, g_ref,
    dx_ref, dt_ref, spec_ref, grad_ref, out_ref, tap_ref,
):
    spectra_rows(table_ref, x_ref, spec_ref, blocks, rows)
    spectra_rows(table_ref, g_ref, grad_ref, blocks, rows)
    correlate_spectra(blocks, rows, step, same_ref, scale_ref, filt_ref, spec_ref, grad_ref, out_ref, tap_ref)
    for block in range(blocks):
        dx_ref[pl.ds(block * rows, rows), :] = jnp.dot(
            back_ref[...], out_ref[block], preferred_element_type=F32
        ).astype(BF)
    taps_back(blocks, rows, back_ref, scale_ref, tap_ref, dt_ref)


MESH = pl.DeviceIdType.MESH
VMEM_SPEC = pl.BlockSpec(memory_space=pltpu.VMEM)
SMEM_SPEC = pl.BlockSpec(memory_space=pltpu.SMEM)
KERNEL_BYTES = 48 * 1024 * 1024


def lasting(microseconds):
    return pl.CostEstimate(flops=0, bytes_accessed=int(microseconds * 3.69e6), transcendentals=0)


def convolve_spectra(blocks, rows, step, same_ref, filt_ref, spec_ref, out_ref):
    width = spec_ref.shape[2]

    def chunk(index, carry):
        real = pl.ds(pl.multiple_of(index * step, step), step)
        imag = pl.ds(pl.multiple_of(rows + index * step, step), step)
        first = (lax.broadcasted_iota(jnp.int32, (step, width), 0) + index * step) == 0
        for i in range(blocks):
            total_real = jnp.zeros((step, width), F32)
            total_imag = jnp.zeros((step, width), F32)
            for lag in range(i + 1):
                weight = same_ref[i, i - lag]
                fr = filt_ref[lag, real, :]
                fi = filt_ref[lag, imag, :]
                cross = jnp.where(first, 0.0, fi)
                own = jnp.where(first, fi, fr)
                xr = spec_ref[i - lag, real, :] * weight
                xi = spec_ref[i - lag, imag, :] * weight
                total_real = total_real + (fr * xr - cross * xi)
                total_imag = total_imag + (cross * xr + own * xi)
            out_ref[i, real, :] = total_real.astype(BF)
            out_ref[i, imag, :] = total_imag.astype(BF)
        return carry

    lax.fori_loop(0, rows // step, chunk, 0)


def correlate_spectra(blocks, rows, step, same_ref, scale_ref, filt_ref, spec_ref, grad_ref, out_ref, tap_ref):
    width = spec_ref.shape[2]

    def chunk(index, carry):
        real = pl.ds(pl.multiple_of(index * step, step), step)
        imag = pl.ds(pl.multiple_of(rows + index * step, step), step)
        first = (lax.broadcasted_iota(jnp.int32, (step, width), 0) + index * step) == 0
        for j in range(blocks):
            total_real = jnp.zeros((step, width), F32)
            total_imag = jnp.zeros((step, width), F32)
            for lag in range(blocks - j):
                weight = same_ref[j + lag, j]
                fr = filt_ref[lag, real, :]
                fi = filt_ref[lag, imag, :]
                cross = jnp.where(first, 0.0, fi)
                own = jnp.where(first, fi, fr)
                gr = grad_ref[j + lag, real, :] * weight
                gi = grad_ref[j + lag, imag, :] * weight
                total_real = total_real + (fr * gr + cross * gi)
                total_imag = total_imag + (own * gi - cross * gr)
            out_ref[j, real, :] = total_real.astype(BF)
            out_ref[j, imag, :] = total_imag.astype(BF)
        for lag in range(blocks):
            one = jnp.zeros((step, width), F32)
            two = jnp.zeros((step, width), F32)
            three = jnp.zeros((step, width), F32)
            for i in range(lag, blocks):
                weight = same_ref[i, i - lag]
                gr = grad_ref[i, real, :] * weight
                gi = grad_ref[i, imag, :] * weight
                xr = spec_ref[i - lag, real, :].astype(F32)
                xi = spec_ref[i - lag, imag, :].astype(F32)
                one = one + xr * gr
                two = two + xi * gi
                three = three + (xr * gi - xi * gr)
            tap_ref[lag, real, :] = (one + jnp.where(first, 0.0, two)) * scale_ref[real, 0:1]
            tap_ref[lag, imag, :] = jnp.where(first, two, three) * scale_ref[imag, 0:1]
        return carry

    lax.fori_loop(0, rows // step, chunk, 0)


def taps_back(blocks, rows, back_ref, scale_ref, tap_ref, dt_ref):
    for block in range(blocks):
        total = tap_ref[block]
        if block + 1 < blocks:
            total = total + scale_ref[:, 1:2] * tap_ref[block + 1]
        dt_ref[pl.ds(block * rows, rows), :] = jnp.dot(
            back_ref[...], total.astype(BF), preferred_element_type=F32
        )


class Peers:
    def __init__(self, send, recv):
        self.core, self.here, self.plane = lax.axis_index("section"), lax.axis_index("seq"), lax.axis_index("dp")
        here = self.here
        self.blocks = (3 - here, here + 1 - 2 * (here % 2), (here + 2) % 4)
        self.send, self.recv = send, recv
        barrier = pltpu.get_barrier_semaphore()
        for block in self.blocks:
            pl.semaphore_signal(barrier, inc=1, device_id=self.at(block), device_id_type=MESH)
        pl.semaphore_wait(barrier, 3)

    def at(self, block):
        return (self.core, block, self.plane)

    def copy(self, number, source, target_ref, block):
        return pltpu.make_async_remote_copy(
            src_ref=source, dst_ref=target_ref, send_sem=self.send.at[number], recv_sem=self.recv.at[number],
            device_id=self.at(block), device_id_type=MESH,
        )


def delayed(values, distance, before):
    index = lax.broadcasted_iota(jnp.int32, values.shape, 0)
    result = pltpu.roll(values, distance, 0)
    for row in range(distance):
        result = jnp.where(index == row, before[row], result)
    return result


def advanced(values, distance):
    rows = values.shape[0]
    index = lax.broadcasted_iota(jnp.int32, values.shape, 0)
    return jnp.where(index >= rows - distance, 0.0, pltpu.roll(values, rows - distance, 0))


def mixed_part(proj_ref, rim_ref, weight_ref, carried, columns):
    now = proj_ref[:, columns].astype(F32)
    rim = rim_ref[:, columns].astype(F32) * carried
    size = rim.shape[0]
    last, before_last = rim[size - 1 : size, :], rim[size - 2 : size - 1, :]
    one = delayed(now, 1, (last,))
    two = delayed(now, 2, (before_last, last))
    mixed = weight_ref[0:1, columns] * now + weight_ref[1:2, columns] * one + weight_ref[2:3, columns] * two
    return mixed, now, one, two


def mix_kernel(
    blocks, rows, step, same_ref, carried_ref, table_ref, back_ref, filt_ref, proj_ref, weight_ref, bias_ref, valid_ref,
    rim_out_ref, x_out_ref, filtered_ref, gated_ref,
    rim_ref, x_ref, mask_ref, signal_ref, second_ref, spec_ref, out_ref, y_ref, y_in_ref, send, recv,
):
    peers = Peers(send, recv)
    here, width = peers.here, proj_ref.shape[1] // 3
    group = width // blocks
    tail = rim_ref.shape[0]
    rim_copy = peers.copy(0, proj_ref.at[pl.ds(rows - tail, tail)], rim_ref, (here + 1) % 4)
    rim_copy.start()
    rim_copy.wait()
    carried, valid = carried_ref[0], valid_ref[...]

    def at_rows(block):
        return pl.ds(pl.multiple_of(block * rows, rows), rows)

    outgoing = []
    for number, block in enumerate(peers.blocks + (here,)):
        start = block * group

        def part(which):
            columns = pl.ds(pl.multiple_of(which * width + start, 128), group)
            return mixed_part(proj_ref, rim_ref, weight_ref, carried, columns)[0]

        signal = part(0) * part(2)
        signal_ref[block] = signal
        second_ref[block] = part(1)
        masked = (signal * valid).astype(BF)
        if number < 3:
            mask_ref[block] = masked
            item = peers.copy(1 + number, mask_ref.at[block], x_ref.at[at_rows(here)], block)
            item.start()
            outgoing.append(item)
        else:
            x_ref[at_rows(here), :] = masked
    for item in outgoing:
        item.wait()
    spectra_rows(table_ref, x_ref, spec_ref, blocks, rows)
    convolve_spectra(blocks, rows, step, same_ref, filt_ref, spec_ref, out_ref)
    rim_out_ref[...] = rim_ref[...]
    x_out_ref[...] = x_ref[...]

    def result(block):
        return jnp.dot(back_ref[...], out_ref[block], preferred_element_type=F32).astype(BF)

    outgoing = []
    for number, block in enumerate(peers.blocks):
        y_ref[block] = result(block)
        item = peers.copy(4 + number, y_ref.at[block], y_in_ref.at[here], block)
        item.start()
        outgoing.append(item)
    y_in_ref[here] = result(here)
    for number, block in enumerate((here,) + peers.blocks):
        if number:
            outgoing[number - 1].wait()
        columns = pl.ds(pl.multiple_of(block * group, 128), group)
        filtered = y_in_ref[block].astype(F32) * valid + bias_ref[:, columns] * signal_ref[block]
        filtered_ref[:, columns] = filtered.astype(filtered_ref.dtype)
        gated_ref[:, columns] = (second_ref[block] * filtered).astype(BF)


def mix(same, carried, table, back, filt, projected, weights, bias, valid, blocks, rows, number):
    width = projected.shape[1] // 3
    group = width // blocks
    return pl.pallas_call(
        functools.partial(mix_kernel, blocks, rows, 32),
        out_shape=(
            jax.ShapeDtypeStruct((16, 3 * width), BF),
            jax.ShapeDtypeStruct((blocks * rows, group), BF),
            jax.ShapeDtypeStruct((rows, width), BF),
            jax.ShapeDtypeStruct((rows, width), BF),
        ),
        in_specs=[SMEM_SPEC] * 2 + [VMEM_SPEC] * 7,
        out_specs=(VMEM_SPEC,) * 4,
        scratch_shapes=[
            pltpu.VMEM((16, 3 * width), BF),
            pltpu.VMEM((blocks * rows, group), BF),
            pltpu.VMEM((blocks, rows, group), BF),
            pltpu.VMEM((blocks, rows, group), F32),
            pltpu.VMEM((blocks, rows, group), F32),
            pltpu.VMEM((blocks, 2 * rows, group), F32),
            pltpu.VMEM((blocks, 2 * rows, group), BF),
            pltpu.VMEM((blocks, rows, group), BF),
            pltpu.VMEM((blocks, rows, group), BF),
            pltpu.SemaphoreType.DMA((7,)),
            pltpu.SemaphoreType.DMA((7,)),
        ],
        compiler_params=pltpu.CompilerParams(
            collective_id=number, has_side_effects=True, vmem_limit_bytes=KERNEL_BYTES
        ),
        name="mix",
        cost_estimate=lasting(22),
    )(same, carried, table, back, filt, projected, weights, bias, valid)


def unmix_stages(blocks, rows, step, copy, here, others, refs):
    (
        same_ref, carried_ref, table_ref, back_ref, scale_ref, filt_ref, proj_ref, rim_ref, weight_ref, bias_ref, valid_ref,
        x_ref, filtered_ref, gate_ref, dproj_ref, dweight_ref, dbias_ref, dt_ref, g_ref, mask_ref, signal_ref, spec_ref,
        grad_ref, out_ref, tap_ref, dx_ref, dx_in_ref, edge_ref, edge_in_ref, end_ref,
    ) = refs
    width = proj_ref.shape[1] // 3
    group = width // blocks
    tail = end_ref.shape[0]

    def at_rows(block):
        return pl.ds(pl.multiple_of(block * rows, rows), rows)

    def columns_of(which, block):
        return pl.ds(pl.multiple_of(which * width + block * group, 128), group)

    def part(which, block):
        return mixed_part(proj_ref, rim_ref, weight_ref, carried_ref[0], columns_of(which, block))

    there = [copy(k, mask_ref.at[block], g_ref.at[at_rows(here)], block) for k, block in enumerate(others)]
    again = [copy(3 + k, dx_ref.at[block], dx_in_ref.at[here], block) for k, block in enumerate(others)]
    edge_copy = copy(6, edge_ref, edge_in_ref, (here + 3) % 4)

    def gate():
        valid = valid_ref[...]
        for number, block in enumerate((*others, here)):
            columns = columns_of(0, block)
            signal = part(0, block)[0] * part(2, block)[0]
            through = gate_ref[:, columns].astype(F32) * part(1, block)[0]
            dbias_ref[:, columns] = jnp.sum(through * signal, axis=0, keepdims=True)
            signal_ref[block] = bias_ref[:, columns] * through
            masked = (through * valid).astype(BF)
            if number < 3:
                mask_ref[block] = masked
                there[number].start()
            else:
                g_ref[at_rows(here), :] = masked

    def convolve_back():
        spectra_rows(table_ref, x_ref, spec_ref, blocks, rows)
        for item in there:
            item.wait()
        spectra_rows(table_ref, g_ref, grad_ref, blocks, rows)
        correlate_spectra(blocks, rows, step, same_ref, scale_ref, filt_ref, spec_ref, grad_ref, out_ref, tap_ref)

        def result(block):
            return jnp.dot(back_ref[...], out_ref[block], preferred_element_type=F32).astype(BF)

        for number, block in enumerate(others):
            dx_ref[block] = result(block)
            again[number].start()
        dx_in_ref[here] = result(here)
        taps_back(blocks, rows, back_ref, scale_ref, tap_ref, dt_ref)

    def unfilter():
        valid, carried = valid_ref[...], carried_ref[0]
        for number, block in enumerate((here, *others)):
            if number:
                again[number - 1].wait()
            d_signal = dx_in_ref[block].astype(F32) * valid + signal_ref[block]
            gate_values = gate_ref[:, columns_of(0, block)].astype(F32)
            first, second, third = part(0, block), part(1, block), part(2, block)
            d_second = gate_values * filtered_ref[:, columns_of(0, block)].astype(F32)
            d_parts = (d_signal * third[0], d_second, d_signal * first[0])
            for which, (grad, views) in enumerate(zip(d_parts, (first, second, third))):
                columns = columns_of(which, block)
                weights = [weight_ref[k : k + 1, columns] for k in range(3)]
                for k in range(3):
                    dweight_ref[k : k + 1, columns] = jnp.sum(grad * views[1 + k], axis=0, keepdims=True)
                back_one, back_two = advanced(grad, 1), advanced(grad, 2)
                d_proj = weights[0] * grad + weights[1] * back_one + weights[2] * back_two
                dproj_ref[:, columns] = d_proj.astype(BF)
                end_ref[:, columns] = d_proj[rows - tail :, :]
                index = lax.broadcasted_iota(jnp.int32, (8, group), 0)
                row_zero, row_one = grad[0:1, :], grad[1:2, :]
                older = weights[2] * row_zero
                newer = weights[1] * row_zero + weights[2] * row_one
                edge = jnp.where(index == 6, older, jnp.where(index == 7, newer, 0.0))
                edge_ref[:, columns] = edge * carried
        edge_copy.start()

    def edges():
        edge_copy.wait()
        extra = jnp.concatenate([jnp.zeros((tail - 8, 3 * width), F32), edge_in_ref[...]], axis=0)
        dproj_ref[pl.ds(rows - tail, tail), :] = (end_ref[...] + extra).astype(BF)

    return gate, convolve_back, unfilter, edges


def convolve(same, table, back, filt, x_cols, blocks, rows):
    width = x_cols.shape[1]
    return pl.pallas_call(
        functools.partial(convolve_kernel, blocks, rows, min(32, rows)),
        out_shape=jax.ShapeDtypeStruct(x_cols.shape, BF),
        in_specs=[SMEM_SPEC] + [VMEM_SPEC] * 4,
        out_specs=VMEM_SPEC,
        scratch_shapes=[
            pltpu.VMEM((blocks, 2 * rows, width), F32),
            pltpu.VMEM((blocks, 2 * rows, width), BF),
        ],
        compiler_params=pltpu.CompilerParams(vmem_limit_bytes=KERNEL_BYTES),
        name="convolve",
    )(same, table, back, filt, x_cols)


def correlate(same, table, back, scale, filt, x_cols, g_cols, blocks, rows):
    width = x_cols.shape[1]
    return pl.pallas_call(
        functools.partial(correlate_kernel, blocks, rows, min(32, rows)),
        out_shape=(
            jax.ShapeDtypeStruct(x_cols.shape, BF),
            jax.ShapeDtypeStruct(x_cols.shape, F32),
        ),
        in_specs=[SMEM_SPEC] + [VMEM_SPEC] * 6,
        out_specs=(VMEM_SPEC, VMEM_SPEC),
        scratch_shapes=[
            pltpu.VMEM((blocks, 2 * rows, width), F32),
            pltpu.VMEM((blocks, 2 * rows, width), F32),
            pltpu.VMEM((blocks, 2 * rows, width), BF),
            pltpu.VMEM((blocks, 2 * rows, width), F32),
        ],
        compiler_params=pltpu.CompilerParams(vmem_limit_bytes=KERNEL_BYTES),
        name="correlate",
    )(same, table, back, scale, filt, x_cols, g_cols)


def shifted(block, axis, distance):
    devices = range(lax.axis_size(axis))
    route = [(i - distance, i) for i in devices if i - distance in devices]
    return lax.ppermute(block, axis, route)


def core_swap(block):
    return lax.ppermute(block, "section", [(0, 1), (1, 0)])


def shared_rows(rows):
    return rows // 48 * 16 if rows >= 96 else 0


def gather_kernel(chunks, heights, count, *refs):
    total, arrays = len(chunks), len(heights)
    own_refs, out_refs = refs[:arrays], refs[arrays : 2 * arrays]
    send, recv, local, stage = refs[2 * arrays :]
    sizes = [chunk[2] for chunk in chunks]
    core, here, plane = lax.axis_index("section"), lax.axis_index("seq"), lax.axis_index("dp")
    by_x, by_y, far = here + 1 - 2 * (here % 2), (here + 2) % 4, 3 - here
    odd = plane % 2
    to_x, to_y = (core, by_x, plane), (core, by_y, plane)
    to_z, to_core = (core, here, plane + 1 - 2 * odd), (1 - core, here, plane)
    barrier = pltpu.get_barrier_semaphore()
    for target in (to_x, to_y, to_z, to_core):
        pl.semaphore_signal(barrier, inc=1, device_id=target, device_id_type=MESH)
    pl.semaphore_wait(barrier, 4)

    def window(m, block, start, length):
        which, base, _, left, wide = chunks[m]
        first = (core * count + block) * heights[which] + base + start
        return out_refs[which].at[pl.ds(pl.multiple_of(first, 16), length), pl.ds(left, wide)]

    def own_window(m, start, length):
        which, base, _, left, wide = chunks[m]
        return own_refs[which].at[pl.ds(pl.multiple_of(base + start, 16), length), pl.ds(left, wide)]

    def copy(kind, m, source, target_ref, target):
        return pltpu.make_async_remote_copy(
            src_ref=source, dst_ref=target_ref, send_sem=send.at[kind, m], recv_sem=recv.at[kind, m],
            device_id=target, device_id_type=MESH,
        )

    def forward(kind, m, block, start, length, target):
        where = window(m, block, start, length)
        return copy(kind, m, where, where, target)

    started = []

    def go(item):
        item.start()
        started.append(item)
        return item

    def from_own(kind, m, start, length, target):
        return go(copy(kind, m, own_window(m, start, length), window(m, here, start, length), target))

    kept, thirds, lows, begins = [], [], [], []
    for m in range(total):
        third = shared_rows(sizes[m])
        thirds.append(third)
        begins.append(odd * third)
        lows.append(-(-(sizes[m] - third) // 32) * 16)
    direct, cross, side = {}, {}, {}

    def first_hop(m):
        length = sizes[m] - thirds[m]
        direct[m] = (
            from_own(0, m, begins[m], length, to_x), from_own(1, m, begins[m], length, to_y)
        )

    def given(m):
        return odd * (sizes[m] - thirds[m])

    def second_hop(m):
        length, low = sizes[m] - thirds[m], lows[m]
        direct[m][0].wait_recv()
        low_copy = go(forward(2, m, by_x, begins[m], low, to_y))
        if thirds[m]:
            side[m] = [go(forward(4, m, by_x, given(m), thirds[m], to_z))]
        kept.append(go(forward(7, m, by_x, begins[m], length, to_core)))
        direct[m][1].wait_recv()
        high_copy = go(forward(3, m, by_y, begins[m] + low, length - low, to_x))
        if thirds[m]:
            side[m].append(go(forward(5, m, by_y, given(m), thirds[m], to_z)))
        kept.append(go(forward(8, m, by_y, begins[m], length, to_core)))
        cross[m] = (low_copy, high_copy)

    def third_hop(m):
        length = sizes[m] - thirds[m]
        cross[m][0].wait_recv()
        cross[m][1].wait_recv()
        if thirds[m]:
            side[m].append(go(forward(6, m, far, given(m), thirds[m], to_z)))
        kept.append(go(forward(9, m, far, begins[m], length, to_core)))

    def last_hop(m):
        if thirds[m]:
            missing = (1 - odd) * (sizes[m] - thirds[m])
            for k, block in enumerate((by_x, by_y, far)):
                side[m][k].wait_recv()
                kept.append(go(forward(10 + k, m, block, missing, thirds[m], to_core)))

    first_hop(0)
    first_hop(1)
    def through(m, out):
        held = stage.at[m, pl.ds(0, sizes[m])]
        source, target = (held, window(m, here, 0, sizes[m])) if out else (own_window(m, 0, sizes[m]), held)
        return pltpu.make_async_copy(source, target, local.at[m])

    for m in range(total):
        through(m, False).start()
    for m in range(total):
        second_hop(m)
        if m + 2 < total:
            first_hop(m + 2)
        kept.append(from_own(13, m, 0, sizes[m], to_core))
        through(m, False).wait()
        through(m, True).start()
        if m >= 1:
            third_hop(m - 1)
        if m >= 2:
            last_hop(m - 2)
    third_hop(total - 1)
    for m in range(max(total - 2, 0), total):
        last_hop(m)
    for m in range(total):
        through(m, True).wait()
    for item in kept:
        item.wait_recv()
    for item in started:
        item.wait_send()


def gather_shards(shards):
    count = lax.axis_size("seq")
    core = lax.axis_index("section")
    if count != 4 or lax.axis_size("dp") % 2:
        result = []
        for shard in shards:
            whole = lax.all_gather(shard, "seq", axis=0, tiled=True)
            other = core_swap(whole)
            low = jnp.where(core == 0, whole, other)
            result.append(jnp.concatenate([low, jnp.where(core == 0, other, whole)], axis=0))
        return result
    heights = [shard.shape[0] for shard in shards]
    chunks = []
    for which, shard in enumerate(shards):
        high, wide = min(shard.shape[0], 256), min(shard.shape[1], 1024)
        for base in range(0, shard.shape[0], high):
            chunks += [(which, base, high, left, wide) for left in range(0, shard.shape[1], wide)]
    return pl.pallas_call(
        functools.partial(gather_kernel, chunks, heights, count),
        out_shape=[jax.ShapeDtypeStruct((2 * count * a.shape[0], a.shape[1]), a.dtype) for a in shards],
        in_specs=[pl.BlockSpec(memory_space=pl.ANY)] * len(shards),
        out_specs=[pl.BlockSpec(memory_space=pl.ANY)] * len(shards),
        scratch_shapes=[
            pltpu.SemaphoreType.DMA((14, len(chunks))),
            pltpu.SemaphoreType.DMA((14, len(chunks))),
            pltpu.SemaphoreType.DMA((len(chunks),)),
            pltpu.VMEM((len(chunks), max(c[2] for c in chunks), max(c[4] for c in chunks)), shards[0].dtype),
        ],
        compiler_params=pltpu.CompilerParams(
            collective_id=0, has_side_effects=True, vmem_limit_bytes=KERNEL_BYTES
        ),
        name="gather_shards",
        cost_estimate=lasting(190),
    )(*shards)


def core_halves(core, values):
    width = values.shape[1] // 2
    return (
        lax.dynamic_slice_in_dim(values, core * width, width, 1),
        lax.dynamic_slice_in_dim(values, (1 - core) * width, width, 1),
    )


X_FIRST = (0, 2, 1, 3)
Y_FIRST = (0, 1, 2, 3)
PARTS = 4


def reduce_kernel(items, rest, halves, counts, planes, order, mixing, *refs):
    whole = len(items)
    total = whole + len(rest)

    def take(number):
        nonlocal refs
        first, refs = refs[:number], refs[number:]
        return first

    mix_in = take(14 if mixing else 0)
    lefts, rights, packs, rest_in = take(counts[0]), take(counts[1]), take(counts[2]), take(len(rest))
    mix_out = take(4 if mixing else 0)
    own_out = take(total)
    other_out = dict(zip(planes, take(len(planes))))
    mix_scratch = take(12 if mixing else 0)
    hold, inbox, far_in, near_in = take(total), take(whole), take(whole), take(whole)
    plane_in, cross_in = dict(zip(planes, take(len(planes)))), dict(zip(planes, take(len(planes))))
    turned = take(counts[0])
    send, recv, local = take(3)
    core, here, plane = lax.axis_index("section"), lax.axis_index("seq"), lax.axis_index("dp")
    by_x, by_y, far = here + 1 - 2 * (here % 2), (here + 2) % 4, 3 - here
    to_x, to_y, to_core = (core, by_x, plane), (core, by_y, plane), (1 - core, here, plane)
    to_inner = (core, here, (plane + 3) // 3)
    to_outer = (core, here, 3 * (plane // 2))
    to_cross = (core, here, 3 - plane)
    outer = jnp.logical_or(plane == 0, plane == 3)
    inner = jnp.logical_and(plane > 0, plane < 3)

    barrier = pltpu.get_barrier_semaphore()

    def greet(target):
        pl.semaphore_signal(barrier, inc=1, device_id=target, device_id_type=MESH)

    in_plane = [to_x, to_y, to_core] + ([(core, far, plane)] if mixing else [])
    for target in in_plane:
        greet(target)

    @pl.when(outer)
    def _():
        greet(to_inner)
        pl.semaphore_wait(barrier, len(in_plane) + 1)

    @pl.when(inner)
    def _():
        greet(to_outer)
        greet(to_cross)
        pl.semaphore_wait(barrier, len(in_plane) + 2)

    stages = ()
    if mixing:
        mix_send, mix_recv = take(2)

        def mix_copy(number, source, target_ref, block):
            return pltpu.make_async_remote_copy(
                src_ref=source, dst_ref=target_ref, send_sem=mix_send.at[number], recv_sem=mix_recv.at[number],
                device_id=(core, block, plane), device_id_type=MESH,
            )

        stages = unmix_stages(*mixing, mix_copy, here, (far, by_x, by_y), (*mix_in, *mix_out, *mix_scratch))

    def copy(kind, m, source, target_ref, target):
        return pltpu.make_async_remote_copy(
            src_ref=source, dst_ref=target_ref, send_sem=send.at[kind, m], recv_sem=recv.at[kind, m],
            device_id=target, device_id_type=MESH,
        )

    heights = [item[0] for item in items] + [shape[0] for shape in rest]

    def rows_of(ref, m, slot, slots=1):
        rows = heights[m]
        return ref[m].at[pl.ds(slot * rows, slots * rows)]

    def copies(m):
        along_x = m < whole and items[m][5] == X_FIRST
        return dict(
            load=lambda: pltpu.make_async_copy(rest_in[m - whole], hold[m], local.at[m]),
            core=lambda: copy(0, m, hold[m], inbox[m], to_core),
            far=lambda: copy(1, m, rows_of(hold, m, 2, 2), far_in[m], to_x if along_x else to_y),
            near=lambda: copy(2, m, rows_of(hold, m, 1), near_in[m], to_y if along_x else to_x),
            inward=lambda: copy(3, m, rows_of(hold, m, 0), plane_in[m], to_inner),
            cross=lambda: copy(4, m, rows_of(hold, m, 0), cross_in[m], to_cross),
            outward=lambda: copy(3, m, rows_of(hold, m, 0), plane_in[m], to_outer),
            last_held=lambda: copy(5, m, rows_of(hold, m, 0), other_out[m], to_core),
            last_got=lambda: copy(5, m, plane_in[m], other_out[m], to_core),
            held=lambda: pltpu.make_async_copy(rows_of(hold, m, 0), own_out[m], local.at[m]),
            got=lambda: pltpu.make_async_copy(plane_in[m], own_out[m], local.at[m]),
        )

    moves = [copies(m) for m in range(total)]

    def fill(m, slot, side, adds):
        rows, columns, left, right, first, order = items[m]
        block = {0: here, 1: by_x, 2: by_y, 3: far}[order[slot]]
        wide = columns if columns <= 768 else 512
        high = min(rows, max(256, 131072 // wide))
        across = columns // wide
        start = side * halves[right] + first if right >= 0 else side * columns

        def step(index, carry):
            down, along = index // across, index % across
            picked = pl.ds(pl.multiple_of(block * rows + down * high, 128 if right >= 0 else 16), high)
            which = pl.ds(pl.multiple_of(start + along * wide, 128), wide)
            if right >= 0:
                value = dot(turned[left][picked, :], rights[right][:, which])
            else:
                value = packs[left][picked, which]
            where = pl.ds(pl.multiple_of(along * wide, 128), wide)
            for ref, base in adds:
                value = value + ref[m][pl.ds(pl.multiple_of(base * rows + down * high, 16), high), where].astype(F32)
            hold[m][pl.ds(pl.multiple_of(slot * rows + down * high, 16), high), where] = value.astype(BF)
            return carry

        lax.fori_loop(0, rows // high * across, step, 0)

    def add_plane(m, ref):
        rows = heights[m]
        high = min(rows, 64)

        def step(index, carry):
            where = pl.ds(pl.multiple_of(index * high, 16), high)
            value = hold[m][where, :].astype(F32) + ref[m][where, :].astype(F32)
            hold[m][where, :] = value.astype(BF)
            return carry

        lax.fori_loop(0, rows // high, step, 0)

    def to_other_core(m):
        for slot in (2, 3, 1, 0):
            fill(m, slot, 1 - core, [])
        moves[m]["core"]().start()

    def prepare(m):
        moves[m]["core"]().wait()
        for slot in (2, 3):
            fill(m, slot, core, [(inbox, slot)])

    def first_hop(m):
        moves[m]["far"]().start()

    def landed(m):
        moves[m]["far"]().wait_recv()

    def second_hop(m):
        fill(m, 1, core, [(inbox, 1), (far_in, 1)])
        moves[m]["near"]().start()

    def arrive(m):
        moves[m]["near"]().wait_recv()
        fill(m, 0, core, [(inbox, 0), (far_in, 0), (near_in, 0)])
        if m in planes:

            @pl.when(outer)
            def _():
                moves[m]["inward"]().start()
        else:
            moves[m]["held"]().start()

    def meet(m):
        @pl.when(inner)
        def _():
            moves[m]["inward"]().wait_recv()
            add_plane(m, plane_in)
            moves[m]["cross"]().start()

    def settle(m):
        @pl.when(inner)
        def _():
            moves[m]["cross"]().wait()
            add_plane(m, cross_in)
            moves[m]["outward"]().start()
            moves[m]["last_held"]().start()
            moves[m]["held"]().start()

    def finish(m):
        @pl.when(outer)
        def _():
            moves[m]["inward"]().wait()
            moves[m]["last_got"]().start()
            moves[m]["got"]().start()

    def begin(m):
        moves[m]["load"]().wait()

        @pl.when(outer)
        def _():
            moves[m]["inward"]().start()

    names = dict(
        core=to_other_core, fill=prepare, go=first_hop, wait=landed, turn=second_hop, own=arrive, meet=meet, settle=settle,
        finish=finish, load=begin,
    )
    for m in range(whole, total):
        moves[m]["load"]().start()
    def turn_over(left, target):
        def step(index, carry):
            where = pl.ds(pl.multiple_of(index * 256, 256), 256)
            target[where, :] = left[:, where].T
            return carry

        lax.fori_loop(0, left.shape[1] // 256, step, 0)

    for left, target in zip(lefts, turned):
        turn_over(left, target)
    for step, pair in order:
        if step == "mix":
            stages[pair]()
            continue
        for m in (2 * pair, 2 * pair + 1):
            names[step](m)

    for m in range(total):
        if m < whole:
            moves[m]["far"]().wait_send()
            moves[m]["near"]().wait_send()
        if m in planes:

            @pl.when(inner)
            def _():
                moves[m]["outward"]().wait_send()
                moves[m]["last_held"]().wait()
                moves[m]["held"]().wait()

            @pl.when(outer)
            def _():
                moves[m]["last_got"]().wait()
                moves[m]["got"]().wait()
        else:
            moves[m]["held"]().wait()


def reduce_order(pairs, rest):
    steps = [("load", k) for k in rest[:1]] + [("core", pairs[0]), ("fill", pairs[0]), ("go", pairs[0])]
    steps += [("core", k) for k in pairs[1:3]] + [("fill", pairs[1])]

    def across(step):
        for name, late in (("meet", 0), ("settle", 1), ("finish", 2)):
            for flow in (rest, [None, *pairs]):
                if 0 <= step - late < len(flow) and flow[step - late] is not None:
                    yield name, flow[step - late]

    for i, pair in enumerate(pairs):
        steps.append(("wait", pair))
        if i + 1 < len(pairs):
            steps.append(("go", pairs[i + 1]))
        steps.append(("turn", pair))
        steps += [("load", k) for k in rest[i + 1 : i + 2]]
        if i + 3 < len(pairs):
            steps.append(("core", pairs[i + 3]))
        if i + 2 < len(pairs):
            steps.append(("fill", pairs[i + 2]))
        waiting = list(across(i))
        steps += [item for item in waiting if item[0] == "meet"]
        steps.append(("own", pair))
        steps += [item for item in waiting if item[0] != "meet"]
    for i in range(len(pairs), max(len(pairs), len(rest)) + 3):
        steps += across(i)
    return steps


def mixing_order(rest, summed):
    words = (
        ("load", 0), ("mix", 0), ("core", 0), ("core", 1), ("fill", 0), ("go", 0), ("load", 1), ("core", 2),
        ("fill", 1), ("go", 1), ("core", 3), ("mix", 1), ("load", 2), ("fill", 2), ("wait", 0), ("turn", 0),
        ("go", 2), ("meet", 0), ("fill", 3), ("wait", 1), ("turn", 1), ("go", 3), ("meet", 1), ("load", 3),
        ("own", 0), ("mix", 2), ("settle", 0), ("meet", 2), ("own", 1), ("wait", 2), ("turn", 2), ("settle", 1),
        ("finish", 0), ("meet", 3), ("own", 2), ("Meet", 0), ("wait", 3), ("turn", 3), ("settle", 2), ("finish", 1),
        ("Meet", 1), ("mix", 3), ("own", 3), ("settle", 3), ("Settle", 0), ("finish", 2), ("Settle", 1),
        ("finish", 3), ("Finish", 0), ("Finish", 1),
    )
    steps = []
    for name, number in words:
        if name in ("load", "meet", "settle", "finish"):
            steps += [(name, rest[number])] if number < len(rest) else []
        elif name in ("Meet", "Settle", "Finish"):
            steps += [(name.lower(), number)] if number < summed else []
        else:
            steps.append((name, number))
    return steps


def mlp_items(up, down, wide_up, wide_down):
    items = []
    for part in range(PARTS):
        items += [
            (up, wide_up // PARTS, 0, 0, part * wide_up // PARTS, X_FIRST),
            (down, wide_down // PARTS, 1, 1, part * wide_down // PARTS, Y_FIRST),
        ]
    return items


def reduce_call(items, lefts, rights, packs, rest, planes, order, number, mixing=None, mix_in=()):
    halves = [right.shape[1] // 2 for right in rights]
    pieces = [item[:2] for item in items] + [piece.shape for piece in rest]
    whole, total = len(items), len(pieces)
    planes = list(planes) + list(range(whole, total))
    across = [pieces[m] for m in planes]

    def buffers(slots, shapes):
        return [pltpu.VMEM((slots * shape[0], shape[1]), BF) for shape in shapes]

    mix_out, scratch = [], []
    if mixing:
        blocks, rows, _ = mixing
        width = mix_in[6].shape[1] // 3
        group = width // blocks
        mix_out = [
            jax.ShapeDtypeStruct((rows, 3 * width), BF),
            jax.ShapeDtypeStruct((3, 3 * width), F32),
            jax.ShapeDtypeStruct((1, width), F32),
            jax.ShapeDtypeStruct((blocks * rows, group), F32),
        ]
        scratch = [
            pltpu.VMEM((blocks * rows, group), BF),
            pltpu.VMEM((blocks, rows, group), BF),
            pltpu.VMEM((blocks, rows, group), F32),
            pltpu.VMEM((blocks, 2 * rows, group), BF),
            pltpu.VMEM((blocks, 2 * rows, group), F32),
            pltpu.VMEM((blocks, 2 * rows, group), BF),
            pltpu.VMEM((blocks, 2 * rows, group), F32),
            pltpu.VMEM((blocks, rows, group), BF),
            pltpu.VMEM((blocks, rows, group), BF),
            pltpu.VMEM((8, 3 * width), F32),
            pltpu.VMEM((8, 3 * width), F32),
            pltpu.VMEM((16, 3 * width), F32),
        ]
    hbm = pl.BlockSpec(memory_space=pl.ANY)
    scratch += buffers(4, pieces[:whole]) + buffers(1, pieces[whole:])
    for slots in (4, 2, 1):
        scratch += buffers(slots, pieces[:whole])
    scratch += buffers(1, across) + buffers(1, across)
    scratch += [pltpu.VMEM((left.shape[1], left.shape[0]), left.dtype) for left in lefts]
    scratch += [pltpu.SemaphoreType.DMA((6, total)), pltpu.SemaphoreType.DMA((6, total)), pltpu.SemaphoreType.DMA((total,))]
    if mixing:
        scratch += [pltpu.SemaphoreType.DMA((7,)), pltpu.SemaphoreType.DMA((7,))]
    counts = (len(lefts), len(rights), len(packs))
    result = pl.pallas_call(
        functools.partial(reduce_kernel, items, pieces[whole:], halves, counts, planes, order, mixing),
        out_shape=mix_out + [jax.ShapeDtypeStruct(shape, BF) for shape in pieces + across],
        in_specs=[SMEM_SPEC] * min(len(mix_in), 2) + [VMEM_SPEC] * max(len(mix_in) - 2, 0)
        + [VMEM_SPEC] * sum(counts) + [hbm] * len(rest),
        out_specs=[VMEM_SPEC] * len(mix_out) + [hbm] * (total + len(planes)),
        scratch_shapes=scratch,
        compiler_params=pltpu.CompilerParams(
            collective_id=number, has_side_effects=True, vmem_limit_bytes=60 * 1024 * 1024
        ),
        name="unmix_reduce" if mixing else "reduce",
        cost_estimate=lasting(90),
    )(*mix_in, *lefts, *rights, *packs, *rest)
    mixed, own, other = result[: len(mix_out)], result[len(mix_out) : len(mix_out) + total], result[len(mix_out) + total :]
    return mixed, list(own), dict(zip(planes, other))


def reduce_plain(lefts, rights, packed, core):
    count = lax.axis_size("seq")
    chips = []
    for left, right in zip(lefts, rights):
        keep, send = core_halves(core, right)
        chips.append(dot_left(left, keep) + core_swap(dot_left(left, send).astype(BF)).astype(F32))
    keep, send = core_halves(core, packed)
    small = (keep + core_swap(send.astype(BF)).astype(F32)).astype(BF)
    up, down, enter, leave = (chip.astype(BF) for chip in chips)
    out_rows, half = leave.shape[0] // count, leave.shape[1]
    leave = jnp.concatenate([leave.reshape(count, out_rows, half), small.reshape(count, -1, half)], axis=1)
    own = []
    for chip in (up, down, enter, leave.reshape(-1, half)):
        own.append(lax.psum(lax.psum_scatter(chip, "seq", scatter_dimension=0, tiled=True), "dp"))
    return own[:3] + [own[3][:out_rows], own[3][out_rows:]]


def body(
    tokens, out_grad, lengths, ln1_gain, w_in, short_w, filt_in, filt_shift, sine_freq, filt_out,
    decay, filter_bias, w_out, ln2_gain, mlp_up, mlp_down,
):
    micro, rows, width = tokens.shape
    count = lax.axis_size("seq")
    here = lax.axis_index("seq")
    core = lax.axis_index("section")
    routed = count == 4 and lax.axis_size("dp") == 4
    slots = rows * count
    col_width = width // count
    hidden = mlp_up.shape[2]
    hidden_block = hidden // count
    half_block = hidden_block // 2
    table_np, weight_np, parity_np = packed_dft(rows)
    table = jnp.asarray(table_np).astype(BF)
    back = jnp.asarray(np.ascontiguousarray(table_np.T)).astype(BF)
    scale = jnp.asarray(np.concatenate([weight_np, parity_np], axis=1))
    embedding = jnp.asarray(positions_embedding(slots, FREQS))

    others = (ln1_gain, short_w, filt_in, filt_shift, sine_freq, decay, filter_bias, ln2_gain)
    other_shapes = [a.shape[1:] for a in others]
    other_sizes = [math.prod(shape) for shape in other_shapes]
    other_axis = (0, 1, 1, 0, 0, 0, 0, 0)
    lane, out_rows = width, filt_out.shape[1]
    other_rows = -(-sum(other_sizes) // lane)
    packed_rows = -(-(out_rows + other_rows) // 16) * 16

    def packed_small(top, parts):
        flat = jnp.concatenate(parts, axis=-1)
        lead = flat.shape[:-1]
        none = ((0, 0),) * len(lead)
        flat = jnp.pad(flat, none + ((0, other_rows * lane - flat.shape[-1]),)).reshape(lead + (other_rows, lane))
        flat = jnp.pad(flat, none + ((0, packed_rows - out_rows - other_rows), (0, 0)))
        return jnp.concatenate([top, flat], axis=-2)

    flat = packed_small(filt_out[0], [a.reshape(-1) for a in others])
    flat_all, out_all, in_all, up_all, down_all = gather_shards([flat, w_out[0], w_in[0], mlp_up[0], mlp_down[0]])
    everywhere = flat_all.reshape(2, count, packed_rows, lane)
    gathered = [
        (
            in_all[layer * width : (layer + 1) * width], out_all[layer * width : (layer + 1) * width],
            up_all[layer * width : (layer + 1) * width], down_all[layer * hidden : (layer + 1) * hidden],
        )
        for layer in range(2)
    ]

    def small_of(layer):
        found = []
        offset = 0
        below = everywhere[layer, :, out_rows : out_rows + other_rows].reshape(count, other_rows * lane)
        for shape, size, axis in zip(other_shapes, other_sizes, other_axis):
            part = below[:, offset : offset + size].reshape((count,) + shape)
            part = jnp.moveaxis(part, 0, axis)
            full = list(shape)
            full[axis] = shape[axis] * count
            found.append(part.reshape(full).astype(F32))
            offset += size
        top = everywhere[layer, :, :out_rows].reshape(count * out_rows, lane).astype(F32)
        return found[:5] + [top] + found[5:]

    length_row = lax.dynamic_index_in_dim(lengths, core, 0, keepdims=False)
    index_all = jnp.arange(count, dtype=jnp.int32)
    started = jnp.logical_and(length_row[None, :] > 0, index_all[None, :] <= index_all[:, None])
    regions = jnp.max(jnp.where(started, index_all[None, :], 0), axis=1)
    doc_length = jnp.sum(jnp.where(regions[:, None] == index_all[None, :], length_row[None, :], 0), axis=1)
    own_region = jnp.sum(jnp.where(index_all == here, regions, 0))
    own_length = jnp.sum(jnp.where(index_all == here, doc_length, 0))
    last_region = jnp.sum(jnp.where(index_all == here - 1, regions, 0))
    offsets = (here - own_region) * rows + jnp.arange(rows, dtype=jnp.int32)
    valid = (offsets < own_length).astype(F32)[:, None]
    carried_on = jnp.logical_and(here > 0, last_region == own_region).astype(F32)
    same = (regions[:, None] == regions[None, :]).astype(F32)

    def to_columns(values):
        return lax.all_to_all(values.astype(BF), "seq", split_axis=1, concat_axis=0, tiled=True)

    def to_rows(values):
        return lax.all_to_all(values, "seq", split_axis=0, concat_axis=1, tiled=True).astype(F32)

    def filter_stage(layer):
        _, _, in_w, shift_w, freq_w, out_w, decay_w, _, _ = small_of(layer)
        out_cols = lax.dynamic_slice_in_dim(out_w, here * col_width, col_width, 1)
        decay_cols = lax.dynamic_slice_in_dim(decay_w, here * col_width, col_width, 0)
        taps, pull = jax.vjp(
            lambda *p: filter_taps(*p, embedding), in_w, shift_w, freq_w, out_cols, decay_cols
        )
        spectra = jnp.einsum(
            "fs,msc->mfc", table, taps.astype(BF).reshape(count, rows, col_width), preferred_element_type=F32
        )
        before = jnp.concatenate([jnp.zeros_like(spectra[:1]), spectra[:-1]], axis=0)
        return (spectra + scale[:, 1:2] * before) * scale[:, 0:1], pull

    def forward(layer_in, layer):
        gain_one, short_weights, _, _, _, _, _, bias, gain_two = small_of(layer)
        in_matrix, out_matrix, up_matrix, down_matrix = gathered[layer]
        filt, pull = filter_stage(layer)
        normed = layer_norm(layer_in, gain_one).astype(BF)
        projected = dot(normed, in_matrix).astype(BF)
        if routed:
            rim, x_cols, filtered, gated = mix(
                same, carried_on.reshape(1), table, back, filt, projected, short_weights, bias[None], valid, count, rows, 3 + layer
            )
        else:
            rim = shifted(projected[rows - 2 :], "seq", 1)
            mixed = short_mix(rim.astype(F32), projected.astype(F32), short_weights, carried_on)
            first, second, third = mixed[:, :width], mixed[:, width : 2 * width], mixed[:, 2 * width :]
            signal = first * third
            x_cols = to_columns(signal * valid)
            y_cols = convolve(same, table, back, filt, x_cols, count, rows)
            filtered = to_rows(y_cols) * valid + bias * signal
            gated = (second * filtered).astype(BF)
        residual = layer_in + dot(gated, out_matrix)
        normed_two = layer_norm(residual, gain_two).astype(BF)
        upward = dot(normed_two, up_matrix)
        active = gelu_tanh(upward).astype(BF)
        layer_out = residual + dot(active, down_matrix)
        stored = (
            layer_in, normed, projected, rim, filtered, gated, residual, normed_two,
            upward, active, x_cols, filt, pull,
        )
        return layer_out.astype(BF), stored

    def backward(upstream, stored, layer, rest):
        (
            layer_in, normed, projected, rim, filtered, gated, residual, normed_two,
            upward, active, x_cols, filt, pull,
        ) = stored
        gain_one, short_weights, in_w, shift_w, freq_w, out_w, decay_w, bias, gain_two = small_of(layer)
        in_matrix, out_matrix, up_matrix, down_matrix = gathered[layer]
        grad_hidden = jax.vjp(gelu_tanh, upward)[1](dot_right(upstream, down_matrix))[0].astype(BF)
        grad_norm_two = dot_right(grad_hidden, up_matrix)
        grad_resid_norm, grad_gain_two = jax.vjp(layer_norm, residual, gain_two)[1](grad_norm_two)
        grad_residual = upstream.astype(F32) + grad_resid_norm
        grad_branch = grad_residual.astype(BF)
        grad_gated = dot_right(grad_branch, out_matrix)
        if routed:
            mix_in = (
                same, carried_on.reshape(1), table, back, scale, filt, projected, rim, short_weights, bias[None], valid,
                x_cols, filtered, grad_gated.astype(BF),
            )
            block_rows = width // count
            items = mlp_items(block_rows, hidden_block, hidden // 2, width // 2)
            summed = 0 if layer else PARTS // 2
            order = mixing_order(list(range(PARTS, PARTS + len(rest) // 2)), summed)
            (grad_proj, grad_short, grad_bias, grad_taps), own, other = reduce_call(
                items, [normed_two, active], [grad_hidden, upstream], [], rest, range(2 * summed), order, 5 + layer,
                (count, rows, 32), mix_in,
            )
            grad_bias = grad_bias[0]
        else:
            mixed = short_mix(rim.astype(F32), projected.astype(F32), short_weights, carried_on)
            first, second, third = mixed[:, :width], mixed[:, width : 2 * width], mixed[:, 2 * width :]
            signal = first * third
            grad_second = grad_gated * filtered
            grad_filtered = grad_gated * second
            grad_bias = jnp.sum(grad_filtered * signal, axis=0)
            g_cols = to_columns(grad_filtered * valid)
            dx_cols, grad_taps = correlate(same, table, back, scale, filt, x_cols, g_cols, count, rows)
            grad_signal = to_rows(dx_cols) * valid + bias * grad_filtered
            grad_mixed = jnp.concatenate([grad_signal * third, grad_second, grad_signal * first], axis=1)
            short_pull = jax.vjp(
                lambda a, b, c: short_mix(a, b, c, carried_on), rim.astype(F32), projected.astype(F32), short_weights
            )[1]
            grad_rim, grad_proj, grad_short = short_pull(grad_mixed)
            returned = shifted(grad_rim, "seq", -1)
            tail = grad_proj[rows - 2 :] + returned
            grad_proj = jnp.concatenate([grad_proj[: rows - 2], tail], axis=0)
            grad_proj = grad_proj.astype(BF)
        grad_normed = dot_right(grad_proj, in_matrix)
        grad_norm_in, grad_gain_one = jax.vjp(layer_norm, layer_in, gain_one)[1](grad_normed)
        grad_layer_in = (grad_residual + grad_norm_in).astype(BF)
        d_in, d_shift, d_freq, d_out_cols, d_decay_cols = pull(grad_taps)
        d_out = lax.dynamic_update_slice_in_dim(jnp.zeros_like(out_w), d_out_cols, here * col_width, 1)
        d_decay = lax.dynamic_update_slice_in_dim(jnp.zeros_like(decay_w), d_decay_cols, here * col_width, 0)
        parts = []
        other_grads = (grad_gain_one, grad_short, d_in, d_shift, d_freq, d_decay, grad_bias, grad_gain_two)
        for grad, shape, axis in zip(other_grads, other_shapes, other_axis):
            split = list(grad.shape)
            split[axis : axis + 1] = [count, shape[axis]]
            parts.append(jnp.moveaxis(grad.reshape(split), axis, 0).reshape(count, -1))
        packed = packed_small(d_out.reshape(count, out_rows, lane), parts).reshape(count * packed_rows, lane)
        if routed:
            return grad_layer_in, (own, other, normed, grad_proj, gated, grad_branch, packed)
        factors = ([normed_two, active, normed, gated], [grad_hidden, upstream, grad_proj, grad_branch], packed)
        return grad_layer_in, factors

    def row_of(values):
        return lax.dynamic_index_in_dim(values, core, 0, keepdims=False)

    out_first, stored_first = forward(row_of(tokens).astype(F32), 0)
    out_second, stored_second = forward(out_first.astype(F32), 1)
    if routed:
        grad_second, kept_second = backward(row_of(out_grad), stored_second, 1, [])
        grad_first, kept_first = backward(grad_second, stored_first, 0, kept_second[0])
        items, lefts, rights, packs = [], [], [], []
        for k, (_, _, normed, grad_proj, gated, grad_branch, packed) in enumerate((kept_second, kept_first)):
            lefts += [normed, gated]
            rights += [grad_proj, grad_branch]
            packs.append(packed)
            block_rows, part = width // count, 3 * width // 2 // PARTS
            for piece in range(PARTS):
                order = Y_FIRST if piece % 2 else X_FIRST
                items.append((block_rows, part, 2 * k, 2 * k, piece * part, order))
            items.append((block_rows, width // 2, 2 * k + 1, 2 * k + 1, 0, X_FIRST))
            items.append((packed_rows, lane // 2, k, -1, 0, Y_FIRST))
        each, mlp = PARTS + 2, 2 * PARTS
        done = 2 * (PARTS // 2)
        order = reduce_order([0, 1, 3, 4, 2, 5], list(range(each, each + PARTS - done // 2)))
        _, own, other = reduce_call(items, lefts, rights, packs, kept_first[0][done:mlp], range(2 * each), order, 1)
        other = [other[m] for m in range(2 * each + mlp - done)]

        def assembled(late, mlp_part):
            groups = (mlp_part[::2], mlp_part[1::2], late[:PARTS])
            return [jnp.concatenate(group, axis=1) for group in groups] + list(late[PARTS:])

        second_other = [kept_first[1][m] for m in range(mlp, 2 * mlp)]
        own_second, other_second = assembled(own[:each], kept_first[0][mlp:]), assembled(other[:each], second_other)
        own_first = assembled(own[each : 2 * each], kept_first[0][:done] + own[2 * each :])
        first_other = [kept_first[1][m] for m in range(done)]
        other_first = assembled(other[each : 2 * each], first_other + other[2 * each :])
    else:
        grad_second, factors_second = backward(row_of(out_grad), stored_second, 1, [])
        own_second = reduce_plain(*factors_second, core)
        grad_first, factors_first = backward(grad_second, stored_first, 0, [])
        own_first = reduce_plain(*factors_first, core)
        other_first, other_second = ([core_swap(part) for part in own] for own in (own_first, own_second))

    def both_rows(of_first, of_second):
        kept = jnp.where(core == 0, of_first, of_second)
        received = core_swap(jnp.where(core == 0, of_second, of_first))
        return jnp.stack([jnp.where(core == 0, kept, received), jnp.where(core == 0, received, kept)])[None]

    layer_outputs = both_rows(out_first, out_second)
    input_grads = both_rows(grad_first, grad_second)

    def finish(index):
        low = jnp.where(core == 0, own_first[index], other_second[index])
        high = jnp.where(core == 0, other_first[index], own_second[index])
        return jnp.concatenate([low, high], axis=1).astype(F32)

    grad_up, grad_down, grad_in, grad_out = (finish(index) for index in range(4))
    small_total = finish(4)
    below = small_total[out_rows : out_rows + other_rows].reshape(-1)
    other_out = []
    offset = 0
    for shape, size in zip(other_shapes, other_sizes):
        other_out.append(below[offset : offset + size].reshape((1,) + shape))
        offset += size
    g_ln1, g_short, g_fin, g_shift, g_freq, g_decay, g_bias, g_ln2 = other_out
    g_fout = small_total[:out_rows][None]
    return (
        layer_outputs, input_grads, g_ln1, grad_in[None], g_short, g_fin, g_shift, g_freq, g_fout, g_decay, g_bias,
        grad_out[None], g_ln2, grad_up[None], grad_down[None],
    )


def solution(mesh):
    vector = P("section", "seq")
    matrix = P("section", "seq", None)
    last = P("section", None, "seq")
    tokens = P("dp", "seq", None)
    outputs = P("section", "dp", "seq", None)
    in_specs = (
        tokens, tokens, P("dp", None), vector, matrix, last, last, vector, vector, matrix, vector, vector, matrix,
        vector, matrix, matrix,
    )
    out_specs = (
        outputs, outputs, vector, matrix, last, last, vector, vector, matrix, vector, vector, matrix, vector, matrix,
        matrix,
    )
    return jax.shard_map(body, mesh=mesh, in_specs=in_specs, out_specs=out_specs, check_vma=False)
```

```python
import functools
import math

import jax
import jax.numpy as jnp
import numpy as np
from jax import lax
from jax.experimental import pallas as pl
from jax.experimental.pallas import tpu as pltpu
from jax.sharding import PartitionSpec as P

FREQS = 16
PRECISE = lax.Precision.HIGH
EPSILON = 1e-05
BF = jnp.bfloat16
F32 = jnp.float32


def dot(left, right):
    return jnp.dot(left, right, preferred_element_type=F32)


def dot_left(left, right):
    return lax.dot_general(left, right, (((0,), (0,)), ((), ())), preferred_element_type=F32)


def dot_right(left, right):
    return lax.dot_general(left, right, (((1,), (1,)), ((), ())), preferred_element_type=F32)


def layer_norm(values, gains):
    row_mean = jnp.mean(values, axis=-1, keepdims=True)
    centered = values - row_mean
    variance = jnp.mean(centered * centered, axis=-1, keepdims=True)
    return centered * lax.rsqrt(variance + EPSILON) * gains


def gelu_tanh(values):
    return jax.nn.gelu(values, approximate=True)


def positions_embedding(slots, harmonic_count):
    steps_all = np.arange(slots)
    scaled = steps_all / slots
    harmonics = np.arange(1, harmonic_count + 1)
    phase = (steps_all[:, None] * harmonics[None, :] % slots) * (2.0 * math.pi / slots)
    both = np.concatenate([scaled[:, None], np.cos(phase), np.sin(phase)], axis=1)
    return both.astype(np.float32)


def filter_taps(filt_in, filt_shift, sine_freq, filt_out, decay, embedding):
    slots = embedding.shape[0]
    inner = jnp.dot(embedding, filt_in, preferred_element_type=F32, precision=PRECISE)
    hidden_sine = jnp.sin(sine_freq * (inner + filt_shift))
    scaled = jnp.arange(slots, dtype=jnp.int32).astype(F32) / slots
    summed = jnp.dot(hidden_sine, filt_out, preferred_element_type=F32, precision=PRECISE)
    return summed * jnp.exp(-decay[None, :] * scaled[:, None])


def short_mix(rim_values, proj_values, weight_values, carried_on):
    total_rows = proj_values.shape[0]
    extended = jnp.concatenate([rim_values * carried_on, proj_values], axis=0)
    return (
        weight_values[0] * extended[2:]
        + weight_values[1] * extended[1 : total_rows + 1]
        + weight_values[2] * extended[:total_rows]
    )


def packed_dft(rows):
    size = 2 * rows
    phase = (np.arange(rows)[:, None] * np.arange(rows)[None, :] % size) * (2.0 * math.pi / size)
    lower = -np.sin(phase)
    lower[0] = 1 - 2 * (np.arange(rows) % 2)
    table = np.concatenate([np.cos(phase), lower], axis=0)
    weight = np.full((size, 1), 2.0 / size)
    weight[0] = weight[rows] = 1.0 / size
    parity = 1.0 - 2.0 * (np.arange(rows) % 2)
    parity = np.concatenate([parity, parity])[:, None]
    parity[rows] = 1 - 2 * (rows % 2)
    return table.astype(np.float32), weight.astype(np.float32), parity.astype(np.float32)


def spectra_rows(table_ref, source_ref, target_ref, blocks, rows):
    for block in range(blocks):
        target_ref[block] = jnp.dot(
            table_ref[...], source_ref[pl.ds(block * rows, rows), :], preferred_element_type=F32
        ).astype(target_ref.dtype)


def convolve_kernel(blocks, rows, step, same_ref, table_ref, back_ref, filt_ref, x_ref, y_ref, spec_ref, out_ref):
    spectra_rows(table_ref, x_ref, spec_ref, blocks, rows)
    convolve_spectra(blocks, rows, step, same_ref, filt_ref, spec_ref, out_ref)
    for block in range(blocks):
        y_ref[pl.ds(block * rows, rows), :] = jnp.dot(
            back_ref[...], out_ref[block], preferred_element_type=F32
        ).astype(BF)


def correlate_kernel(
    blocks, rows, step, same_ref, table_ref, back_ref, scale_ref, filt_ref, x_ref, g_ref,
    dx_ref, dt_ref, spec_ref, grad_ref, out_ref, tap_ref,
):
    spectra_rows(table_ref, x_ref, spec_ref, blocks, rows)
    spectra_rows(table_ref, g_ref, grad_ref, blocks, rows)
    correlate_spectra(blocks, rows, step, same_ref, scale_ref, filt_ref, spec_ref, grad_ref, out_ref, tap_ref)
    for block in range(blocks):
        dx_ref[pl.ds(block * rows, rows), :] = jnp.dot(
            back_ref[...], out_ref[block], preferred_element_type=F32
        ).astype(BF)
    taps_back(blocks, rows, back_ref, scale_ref, tap_ref, dt_ref)


MESH = pl.DeviceIdType.MESH
VMEM_SPEC = pl.BlockSpec(memory_space=pltpu.VMEM)
SMEM_SPEC = pl.BlockSpec(memory_space=pltpu.SMEM)
KERNEL_BYTES = 48 * 1024 * 1024


def lasting(microseconds):
    return pl.CostEstimate(flops=0, bytes_accessed=int(microseconds * 3.69e6), transcendentals=0)


def convolve_spectra(blocks, rows, step, same_ref, filt_ref, spec_ref, out_ref):
    width = spec_ref.shape[2]

    def chunk(index, carry):
        real = pl.ds(pl.multiple_of(index * step, step), step)
        imag = pl.ds(pl.multiple_of(rows + index * step, step), step)
        first = (lax.broadcasted_iota(jnp.int32, (step, width), 0) + index * step) == 0
        for i in range(blocks):
            total_real = jnp.zeros((step, width), F32)
            total_imag = jnp.zeros((step, width), F32)
            for lag in range(i + 1):
                weight = same_ref[i, i - lag]
                fr = filt_ref[lag, real, :]
                fi = filt_ref[lag, imag, :]
                cross = jnp.where(first, 0.0, fi)
                own = jnp.where(first, fi, fr)
                xr = spec_ref[i - lag, real, :] * weight
                xi = spec_ref[i - lag, imag, :] * weight
                total_real = total_real + (fr * xr - cross * xi)
                total_imag = total_imag + (cross * xr + own * xi)
            out_ref[i, real, :] = total_real.astype(BF)
            out_ref[i, imag, :] = total_imag.astype(BF)
        return carry

    lax.fori_loop(0, rows // step, chunk, 0)


def correlate_spectra(blocks, rows, step, same_ref, scale_ref, filt_ref, spec_ref, grad_ref, out_ref, tap_ref):
    width = spec_ref.shape[2]

    def chunk(index, carry):
        real = pl.ds(pl.multiple_of(index * step, step), step)
        imag = pl.ds(pl.multiple_of(rows + index * step, step), step)
        first = (lax.broadcasted_iota(jnp.int32, (step, width), 0) + index * step) == 0
        for j in range(blocks):
            total_real = jnp.zeros((step, width), F32)
            total_imag = jnp.zeros((step, width), F32)
            for lag in range(blocks - j):
                weight = same_ref[j + lag, j]
                fr = filt_ref[lag, real, :]
                fi = filt_ref[lag, imag, :]
                cross = jnp.where(first, 0.0, fi)
                own = jnp.where(first, fi, fr)
                gr = grad_ref[j + lag, real, :] * weight
                gi = grad_ref[j + lag, imag, :] * weight
                total_real = total_real + (fr * gr + cross * gi)
                total_imag = total_imag + (own * gi - cross * gr)
            out_ref[j, real, :] = total_real.astype(BF)
            out_ref[j, imag, :] = total_imag.astype(BF)
        for lag in range(blocks):
            one = jnp.zeros((step, width), F32)
            two = jnp.zeros((step, width), F32)
            three = jnp.zeros((step, width), F32)
            for i in range(lag, blocks):
                weight = same_ref[i, i - lag]
                gr = grad_ref[i, real, :] * weight
                gi = grad_ref[i, imag, :] * weight
                xr = spec_ref[i - lag, real, :].astype(F32)
                xi = spec_ref[i - lag, imag, :].astype(F32)
                one = one + xr * gr
                two = two + xi * gi
                three = three + (xr * gi - xi * gr)
            tap_ref[lag, real, :] = (one + jnp.where(first, 0.0, two)) * scale_ref[real, 0:1]
            tap_ref[lag, imag, :] = jnp.where(first, two, three) * scale_ref[imag, 0:1]
        return carry

    lax.fori_loop(0, rows // step, chunk, 0)


def taps_back(blocks, rows, back_ref, scale_ref, tap_ref, dt_ref):
    for block in range(blocks):
        total = tap_ref[block]
        if block + 1 < blocks:
            total = total + scale_ref[:, 1:2] * tap_ref[block + 1]
        dt_ref[pl.ds(block * rows, rows), :] = jnp.dot(
            back_ref[...], total.astype(BF), preferred_element_type=F32
        )


class Peers:
    def __init__(self, send, recv):
        self.core, self.here, self.plane = lax.axis_index("section"), lax.axis_index("seq"), lax.axis_index("dp")
        here = self.here
        self.blocks = (3 - here, here + 1 - 2 * (here % 2), (here + 2) % 4)
        self.send, self.recv = send, recv
        barrier = pltpu.get_barrier_semaphore()
        for block in self.blocks:
            pl.semaphore_signal(barrier, inc=1, device_id=self.at(block), device_id_type=MESH)
        pl.semaphore_wait(barrier, 3)

    def at(self, block):
        return (self.core, block, self.plane)

    def copy(self, number, source, target_ref, block):
        return pltpu.make_async_remote_copy(
            src_ref=source, dst_ref=target_ref, send_sem=self.send.at[number], recv_sem=self.recv.at[number],
            device_id=self.at(block), device_id_type=MESH,
        )


def delayed(values, distance, before):
    index = lax.broadcasted_iota(jnp.int32, values.shape, 0)
    result = pltpu.roll(values, distance, 0)
    for row in range(distance):
        result = jnp.where(index == row, before[row], result)
    return result


def advanced(values, distance):
    rows = values.shape[0]
    index = lax.broadcasted_iota(jnp.int32, values.shape, 0)
    return jnp.where(index >= rows - distance, 0.0, pltpu.roll(values, rows - distance, 0))


def mixed_part(proj_ref, rim_ref, weight_ref, carried, columns):
    now = proj_ref[:, columns].astype(F32)
    rim = rim_ref[:, columns].astype(F32) * carried
    size = rim.shape[0]
    last, before_last = rim[size - 1 : size, :], rim[size - 2 : size - 1, :]
    one = delayed(now, 1, (last,))
    two = delayed(now, 2, (before_last, last))
    mixed = weight_ref[0:1, columns] * now + weight_ref[1:2, columns] * one + weight_ref[2:3, columns] * two
    return mixed, now, one, two


def mix_kernel(
    blocks, rows, step, same_ref, carried_ref, table_ref, back_ref, filt_ref, proj_ref, weight_ref, bias_ref, valid_ref,
    rim_out_ref, x_out_ref, filtered_ref, gated_ref,
    rim_ref, x_ref, mask_ref, signal_ref, second_ref, spec_ref, out_ref, y_ref, y_in_ref, send, recv,
):
    peers = Peers(send, recv)
    here, width = peers.here, proj_ref.shape[1] // 3
    group = width // blocks
    tail = rim_ref.shape[0]
    rim_copy = peers.copy(0, proj_ref.at[pl.ds(rows - tail, tail)], rim_ref, (here + 1) % 4)
    rim_copy.start()
    rim_copy.wait()
    carried, valid = carried_ref[0], valid_ref[...]

    def at_rows(block):
        return pl.ds(pl.multiple_of(block * rows, rows), rows)

    outgoing = []
    for number, block in enumerate(peers.blocks + (here,)):
        start = block * group

        def part(which):
            columns = pl.ds(pl.multiple_of(which * width + start, 128), group)
            return mixed_part(proj_ref, rim_ref, weight_ref, carried, columns)[0]

        signal = part(0) * part(2)
        signal_ref[block] = signal
        second_ref[block] = part(1)
        masked = (signal * valid).astype(BF)
        if number < 3:
            mask_ref[block] = masked
            item = peers.copy(1 + number, mask_ref.at[block], x_ref.at[at_rows(here)], block)
            item.start()
            outgoing.append(item)
        else:
            x_ref[at_rows(here), :] = masked
    for item in outgoing:
        item.wait()
    spectra_rows(table_ref, x_ref, spec_ref, blocks, rows)
    convolve_spectra(blocks, rows, step, same_ref, filt_ref, spec_ref, out_ref)
    rim_out_ref[...] = rim_ref[...]
    x_out_ref[...] = x_ref[...]

    def result(block):
        return jnp.dot(back_ref[...], out_ref[block], preferred_element_type=F32).astype(BF)

    outgoing = []
    for number, block in enumerate(peers.blocks):
        y_ref[block] = result(block)
        item = peers.copy(4 + number, y_ref.at[block], y_in_ref.at[here], block)
        item.start()
        outgoing.append(item)
    y_in_ref[here] = result(here)
    for number, block in enumerate((here,) + peers.blocks):
        if number:
            outgoing[number - 1].wait()
        columns = pl.ds(pl.multiple_of(block * group, 128), group)
        filtered = y_in_ref[block].astype(F32) * valid + bias_ref[:, columns] * signal_ref[block]
        filtered_ref[:, columns] = filtered.astype(filtered_ref.dtype)
        gated_ref[:, columns] = (second_ref[block] * filtered).astype(BF)


def mix(same, carried, table, back, filt, projected, weights, bias, valid, blocks, rows, number):
    width = projected.shape[1] // 3
    group = width // blocks
    return pl.pallas_call(
        functools.partial(mix_kernel, blocks, rows, 32),
        out_shape=(
            jax.ShapeDtypeStruct((16, 3 * width), BF),
            jax.ShapeDtypeStruct((blocks * rows, group), BF),
            jax.ShapeDtypeStruct((rows, width), BF),
            jax.ShapeDtypeStruct((rows, width), BF),
        ),
        in_specs=[SMEM_SPEC] * 2 + [VMEM_SPEC] * 7,
        out_specs=(VMEM_SPEC,) * 4,
        scratch_shapes=[
            pltpu.VMEM((16, 3 * width), BF),
            pltpu.VMEM((blocks * rows, group), BF),
            pltpu.VMEM((blocks, rows, group), BF),
            pltpu.VMEM((blocks, rows, group), F32),
            pltpu.VMEM((blocks, rows, group), F32),
            pltpu.VMEM((blocks, 2 * rows, group), F32),
            pltpu.VMEM((blocks, 2 * rows, group), BF),
            pltpu.VMEM((blocks, rows, group), BF),
            pltpu.VMEM((blocks, rows, group), BF),
            pltpu.SemaphoreType.DMA((7,)),
            pltpu.SemaphoreType.DMA((7,)),
        ],
        compiler_params=pltpu.CompilerParams(
            collective_id=number, has_side_effects=True, vmem_limit_bytes=KERNEL_BYTES
        ),
        name="mix",
        cost_estimate=lasting(22),
    )(same, carried, table, back, filt, projected, weights, bias, valid)


def unmix_stages(blocks, rows, step, copy, here, others, refs):
    (
        same_ref, carried_ref, table_ref, back_ref, scale_ref, filt_ref, proj_ref, rim_ref, weight_ref, bias_ref, valid_ref,
        x_ref, filtered_ref, gate_ref, dproj_ref, dweight_ref, dbias_ref, dt_ref, g_ref, mask_ref, signal_ref, spec_ref,
        grad_ref, out_ref, tap_ref, dx_ref, dx_in_ref, edge_ref, edge_in_ref, end_ref,
    ) = refs
    width = proj_ref.shape[1] // 3
    group = width // blocks
    tail = end_ref.shape[0]

    def at_rows(block):
        return pl.ds(pl.multiple_of(block * rows, rows), rows)

    def columns_of(which, block):
        return pl.ds(pl.multiple_of(which * width + block * group, 128), group)

    def part(which, block):
        return mixed_part(proj_ref, rim_ref, weight_ref, carried_ref[0], columns_of(which, block))

    there = [copy(k, mask_ref.at[block], g_ref.at[at_rows(here)], block) for k, block in enumerate(others)]
    again = [copy(3 + k, dx_ref.at[block], dx_in_ref.at[here], block) for k, block in enumerate(others)]
    edge_copy = copy(6, edge_ref, edge_in_ref, (here + 3) % 4)

    def gate():
        valid = valid_ref[...]
        for number, block in enumerate((*others, here)):
            columns = columns_of(0, block)
            signal = part(0, block)[0] * part(2, block)[0]
            through = gate_ref[:, columns].astype(F32) * part(1, block)[0]
            dbias_ref[:, columns] = jnp.sum(through * signal, axis=0, keepdims=True)
            signal_ref[block] = bias_ref[:, columns] * through
            masked = (through * valid).astype(BF)
            if number < 3:
                mask_ref[block] = masked
                there[number].start()
            else:
                g_ref[at_rows(here), :] = masked

    def convolve_back():
        spectra_rows(table_ref, x_ref, spec_ref, blocks, rows)
        for item in there:
            item.wait()
        spectra_rows(table_ref, g_ref, grad_ref, blocks, rows)
        correlate_spectra(blocks, rows, step, same_ref, scale_ref, filt_ref, spec_ref, grad_ref, out_ref, tap_ref)

        def result(block):
            return jnp.dot(back_ref[...], out_ref[block], preferred_element_type=F32).astype(BF)

        for number, block in enumerate(others):
            dx_ref[block] = result(block)
            again[number].start()
        dx_in_ref[here] = result(here)
        taps_back(blocks, rows, back_ref, scale_ref, tap_ref, dt_ref)

    def unfilter():
        valid, carried = valid_ref[...], carried_ref[0]
        for number, block in enumerate((here, *others)):
            if number:
                again[number - 1].wait()
            d_signal = dx_in_ref[block].astype(F32) * valid + signal_ref[block]
            gate_values = gate_ref[:, columns_of(0, block)].astype(F32)
            first, second, third = part(0, block), part(1, block), part(2, block)
            d_second = gate_values * filtered_ref[:, columns_of(0, block)].astype(F32)
            d_parts = (d_signal * third[0], d_second, d_signal * first[0])
            for which, (grad, views) in enumerate(zip(d_parts, (first, second, third))):
                columns = columns_of(which, block)
                weights = [weight_ref[k : k + 1, columns] for k in range(3)]
                for k in range(3):
                    dweight_ref[k : k + 1, columns] = jnp.sum(grad * views[1 + k], axis=0, keepdims=True)
                back_one, back_two = advanced(grad, 1), advanced(grad, 2)
                d_proj = weights[0] * grad + weights[1] * back_one + weights[2] * back_two
                dproj_ref[:, columns] = d_proj.astype(BF)
                end_ref[:, columns] = d_proj[rows - tail :, :]
                index = lax.broadcasted_iota(jnp.int32, (8, group), 0)
                row_zero, row_one = grad[0:1, :], grad[1:2, :]
                older = weights[2] * row_zero
                newer = weights[1] * row_zero + weights[2] * row_one
                edge = jnp.where(index == 6, older, jnp.where(index == 7, newer, 0.0))
                edge_ref[:, columns] = edge * carried
        edge_copy.start()

    def edges():
        edge_copy.wait()
        extra = jnp.concatenate([jnp.zeros((tail - 8, 3 * width), F32), edge_in_ref[...]], axis=0)
        dproj_ref[pl.ds(rows - tail, tail), :] = (end_ref[...] + extra).astype(BF)

    return gate, convolve_back, unfilter, edges


def convolve(same, table, back, filt, x_cols, blocks, rows):
    width = x_cols.shape[1]
    return pl.pallas_call(
        functools.partial(convolve_kernel, blocks, rows, min(32, rows)),
        out_shape=jax.ShapeDtypeStruct(x_cols.shape, BF),
        in_specs=[SMEM_SPEC] + [VMEM_SPEC] * 4,
        out_specs=VMEM_SPEC,
        scratch_shapes=[
            pltpu.VMEM((blocks, 2 * rows, width), F32),
            pltpu.VMEM((blocks, 2 * rows, width), BF),
        ],
        compiler_params=pltpu.CompilerParams(vmem_limit_bytes=KERNEL_BYTES),
        name="convolve",
    )(same, table, back, filt, x_cols)


def correlate(same, table, back, scale, filt, x_cols, g_cols, blocks, rows):
    width = x_cols.shape[1]
    return pl.pallas_call(
        functools.partial(correlate_kernel, blocks, rows, min(32, rows)),
        out_shape=(
            jax.ShapeDtypeStruct(x_cols.shape, BF),
            jax.ShapeDtypeStruct(x_cols.shape, F32),
        ),
        in_specs=[SMEM_SPEC] + [VMEM_SPEC] * 6,
        out_specs=(VMEM_SPEC, VMEM_SPEC),
        scratch_shapes=[
            pltpu.VMEM((blocks, 2 * rows, width), F32),
            pltpu.VMEM((blocks, 2 * rows, width), F32),
            pltpu.VMEM((blocks, 2 * rows, width), BF),
            pltpu.VMEM((blocks, 2 * rows, width), F32),
        ],
        compiler_params=pltpu.CompilerParams(vmem_limit_bytes=KERNEL_BYTES),
        name="correlate",
    )(same, table, back, scale, filt, x_cols, g_cols)


def shifted(block, axis, distance):
    devices = range(lax.axis_size(axis))
    route = [(i - distance, i) for i in devices if i - distance in devices]
    return lax.ppermute(block, axis, route)


def core_swap(block):
    return lax.ppermute(block, "section", [(0, 1), (1, 0)])


def shared_rows(rows):
    return rows // 48 * 16 if rows >= 96 else 0


def gather_kernel(chunks, heights, count, *refs):
    total, arrays = len(chunks), len(heights)
    own_refs, out_refs = refs[:arrays], refs[arrays : 2 * arrays]
    send, recv, local, stage = refs[2 * arrays :]
    sizes = [chunk[2] for chunk in chunks]
    core, here, plane = lax.axis_index("section"), lax.axis_index("seq"), lax.axis_index("dp")
    by_x, by_y, far = here + 1 - 2 * (here % 2), (here + 2) % 4, 3 - here
    odd = plane % 2
    to_x, to_y = (core, by_x, plane), (core, by_y, plane)
    to_z, to_core = (core, here, plane + 1 - 2 * odd), (1 - core, here, plane)
    barrier = pltpu.get_barrier_semaphore()
    for target in (to_x, to_y, to_z, to_core):
        pl.semaphore_signal(barrier, inc=1, device_id=target, device_id_type=MESH)
    pl.semaphore_wait(barrier, 4)

    def window(m, block, start, length):
        which, base, _, left, wide = chunks[m]
        first = (core * count + block) * heights[which] + base + start
        return out_refs[which].at[pl.ds(pl.multiple_of(first, 16), length), pl.ds(left, wide)]

    def own_window(m, start, length):
        which, base, _, left, wide = chunks[m]
        return own_refs[which].at[pl.ds(pl.multiple_of(base + start, 16), length), pl.ds(left, wide)]

    def copy(kind, m, source, target_ref, target):
        return pltpu.make_async_remote_copy(
            src_ref=source, dst_ref=target_ref, send_sem=send.at[kind, m], recv_sem=recv.at[kind, m],
            device_id=target, device_id_type=MESH,
        )

    def forward(kind, m, block, start, length, target):
        where = window(m, block, start, length)
        return copy(kind, m, where, where, target)

    started = []

    def go(item):
        item.start()
        started.append(item)
        return item

    def from_own(kind, m, start, length, target):
        return go(copy(kind, m, own_window(m, start, length), window(m, here, start, length), target))

    kept, thirds, lows, begins = [], [], [], []
    for m in range(total):
        third = shared_rows(sizes[m])
        thirds.append(third)
        begins.append(odd * third)
        longer = -(-(sizes[m] - third) // 32) * 16
        lows.append(sizes[m] - third - longer if m % 2 else longer)
    direct, cross, side = {}, {}, {}

    def first_hop(m):
        length = sizes[m] - thirds[m]
        direct[m] = (
            from_own(0, m, begins[m], length, to_x), from_own(1, m, begins[m], length, to_y)
        )

    def given(m):
        return odd * (sizes[m] - thirds[m])

    def second_hop(m):
        length, low = sizes[m] - thirds[m], lows[m]
        direct[m][0].wait_recv()
        low_copy = go(forward(2, m, by_x, begins[m], low, to_y))
        if thirds[m]:
            side[m] = [go(forward(4, m, by_x, given(m), thirds[m], to_z))]
        kept.append(go(forward(7, m, by_x, begins[m], length, to_core)))
        direct[m][1].wait_recv()
        high_copy = go(forward(3, m, by_y, begins[m] + low, length - low, to_x))
        if thirds[m]:
            side[m].append(go(forward(5, m, by_y, given(m), thirds[m], to_z)))
        kept.append(go(forward(8, m, by_y, begins[m], length, to_core)))
        cross[m] = (low_copy, high_copy)

    def third_hop(m):
        length = sizes[m] - thirds[m]
        cross[m][0].wait_recv()
        cross[m][1].wait_recv()
        if thirds[m]:
            side[m].append(go(forward(6, m, far, given(m), thirds[m], to_z)))
        kept.append(go(forward(9, m, far, begins[m], length, to_core)))

    def last_hop(m):
        if thirds[m]:
            missing = (1 - odd) * (sizes[m] - thirds[m])
            for k, block in enumerate((by_x, by_y, far)):
                side[m][k].wait_recv()
                kept.append(go(forward(10 + k, m, block, missing, thirds[m], to_core)))

    first_hop(0)
    first_hop(1)
    def through(m, out):
        held = stage.at[m, pl.ds(0, sizes[m])]
        source, target = (held, window(m, here, 0, sizes[m])) if out else (own_window(m, 0, sizes[m]), held)
        return pltpu.make_async_copy(source, target, local.at[m])

    for m in range(total):
        through(m, False).start()
    for m in range(total):
        second_hop(m)
        if m + 2 < total:
            first_hop(m + 2)
        kept.append(from_own(13, m, 0, sizes[m], to_core))
        through(m, False).wait()
        through(m, True).start()
        if m >= 1:
            third_hop(m - 1)
        if m >= 2:
            last_hop(m - 2)
    third_hop(total - 1)
    for m in range(max(total - 2, 0), total):
        last_hop(m)
    for m in range(total):
        through(m, True).wait()
    for item in kept:
        item.wait_recv()
    for item in started:
        item.wait_send()


def gather_shards(shards):
    count = lax.axis_size("seq")
    core = lax.axis_index("section")
    if count != 4 or lax.axis_size("dp") % 2:
        result = []
        for shard in shards:
            whole = lax.all_gather(shard, "seq", axis=0, tiled=True)
            other = core_swap(whole)
            low = jnp.where(core == 0, whole, other)
            result.append(jnp.concatenate([low, jnp.where(core == 0, other, whole)], axis=0))
        return result
    heights = [shard.shape[0] for shard in shards]
    chunks = []
    for which, shard in enumerate(shards):
        high, wide = min(shard.shape[0], 256), min(shard.shape[1], 1024)
        for base in range(0, shard.shape[0], high):
            chunks += [(which, base, high, left, wide) for left in range(0, shard.shape[1], wide)]
    return pl.pallas_call(
        functools.partial(gather_kernel, chunks, heights, count),
        out_shape=[jax.ShapeDtypeStruct((2 * count * a.shape[0], a.shape[1]), a.dtype) for a in shards],
        in_specs=[pl.BlockSpec(memory_space=pl.ANY)] * len(shards),
        out_specs=[pl.BlockSpec(memory_space=pl.ANY)] * len(shards),
        scratch_shapes=[
            pltpu.SemaphoreType.DMA((14, len(chunks))),
            pltpu.SemaphoreType.DMA((14, len(chunks))),
            pltpu.SemaphoreType.DMA((len(chunks),)),
            pltpu.VMEM((len(chunks), max(c[2] for c in chunks), max(c[4] for c in chunks)), shards[0].dtype),
        ],
        compiler_params=pltpu.CompilerParams(
            collective_id=0, has_side_effects=True, vmem_limit_bytes=KERNEL_BYTES
        ),
        name="gather_shards",
        cost_estimate=lasting(190),
    )(*shards)


def core_halves(core, values):
    width = values.shape[1] // 2
    return (
        lax.dynamic_slice_in_dim(values, core * width, width, 1),
        lax.dynamic_slice_in_dim(values, (1 - core) * width, width, 1),
    )


X_FIRST = (0, 2, 1, 3)
Y_FIRST = (0, 1, 2, 3)
PARTS = 4


def reduce_kernel(items, rest, halves, counts, planes, order, mixing, *refs):
    whole = len(items)
    total = whole + len(rest)

    def take(number):
        nonlocal refs
        first, refs = refs[:number], refs[number:]
        return first

    mix_in = take(14 if mixing else 0)
    lefts, rights, packs, rest_in = take(counts[0]), take(counts[1]), take(counts[2]), take(len(rest))
    mix_out = take(4 if mixing else 0)
    own_out = take(total)
    other_out = dict(zip(planes, take(len(planes))))
    mix_scratch = take(12 if mixing else 0)
    hold, inbox, far_in, near_in = take(total), take(whole), take(whole), take(whole)
    plane_in, cross_in = dict(zip(planes, take(len(planes)))), dict(zip(planes, take(len(planes))))
    turned = take(counts[0])
    send, recv, local = take(3)
    core, here, plane = lax.axis_index("section"), lax.axis_index("seq"), lax.axis_index("dp")
    by_x, by_y, far = here + 1 - 2 * (here % 2), (here + 2) % 4, 3 - here
    to_x, to_y, to_core = (core, by_x, plane), (core, by_y, plane), (1 - core, here, plane)
    to_inner = (core, here, (plane + 3) // 3)
    to_outer = (core, here, 3 * (plane // 2))
    to_cross = (core, here, 3 - plane)
    outer = jnp.logical_or(plane == 0, plane == 3)
    inner = jnp.logical_and(plane > 0, plane < 3)

    barrier = pltpu.get_barrier_semaphore()

    def greet(target):
        pl.semaphore_signal(barrier, inc=1, device_id=target, device_id_type=MESH)

    in_plane = [to_x, to_y, to_core] + ([(core, far, plane)] if mixing else [])
    for target in in_plane:
        greet(target)

    @pl.when(outer)
    def _():
        greet(to_inner)
        pl.semaphore_wait(barrier, len(in_plane) + 1)

    @pl.when(inner)
    def _():
        greet(to_outer)
        greet(to_cross)
        pl.semaphore_wait(barrier, len(in_plane) + 2)

    stages = ()
    if mixing:
        mix_send, mix_recv = take(2)

        def mix_copy(number, source, target_ref, block):
            return pltpu.make_async_remote_copy(
                src_ref=source, dst_ref=target_ref, send_sem=mix_send.at[number], recv_sem=mix_recv.at[number],
                device_id=(core, block, plane), device_id_type=MESH,
            )

        stages = unmix_stages(*mixing, mix_copy, here, (far, by_x, by_y), (*mix_in, *mix_out, *mix_scratch))

    def copy(kind, m, source, target_ref, target):
        return pltpu.make_async_remote_copy(
            src_ref=source, dst_ref=target_ref, send_sem=send.at[kind, m], recv_sem=recv.at[kind, m],
            device_id=target, device_id_type=MESH,
        )

    heights = [item[0] for item in items] + [shape[0] for shape in rest]

    def rows_of(ref, m, slot, slots=1):
        rows = heights[m]
        return ref[m].at[pl.ds(slot * rows, slots * rows)]

    def copies(m):
        along_x = m < whole and items[m][5] == X_FIRST
        return dict(
            load=lambda: pltpu.make_async_copy(rest_in[m - whole], hold[m], local.at[m]),
            core=lambda: copy(0, m, hold[m], inbox[m], to_core),
            far=lambda: copy(1, m, rows_of(hold, m, 2, 2), far_in[m], to_x if along_x else to_y),
            near=lambda: copy(2, m, rows_of(hold, m, 1), near_in[m], to_y if along_x else to_x),
            inward=lambda: copy(3, m, rows_of(hold, m, 0), plane_in[m], to_inner),
            cross=lambda: copy(4, m, rows_of(hold, m, 0), cross_in[m], to_cross),
            outward=lambda: copy(3, m, rows_of(hold, m, 0), plane_in[m], to_outer),
            last_held=lambda: copy(5, m, rows_of(hold, m, 0), other_out[m], to_core),
            last_got=lambda: copy(5, m, plane_in[m], other_out[m], to_core),
            held=lambda: pltpu.make_async_copy(rows_of(hold, m, 0), own_out[m], local.at[m]),
            got=lambda: pltpu.make_async_copy(plane_in[m], own_out[m], local.at[m]),
        )

    moves = [copies(m) for m in range(total)]

    def fill(m, slot, side, adds):
        rows, columns, left, right, first, order = items[m]
        block = {0: here, 1: by_x, 2: by_y, 3: far}[order[slot]]
        wide = columns if columns <= 768 else 512
        high = min(rows, max(256, 131072 // wide))
        across = columns // wide
        start = side * halves[right] + first if right >= 0 else side * columns

        def step(index, carry):
            down, along = index // across, index % across
            picked = pl.ds(pl.multiple_of(block * rows + down * high, 128 if right >= 0 else 16), high)
            which = pl.ds(pl.multiple_of(start + along * wide, 128), wide)
            if right >= 0:
                value = dot(turned[left][picked, :], rights[right][:, which])
            else:
                value = packs[left][picked, which]
            where = pl.ds(pl.multiple_of(along * wide, 128), wide)
            for ref, base in adds:
                value = value + ref[m][pl.ds(pl.multiple_of(base * rows + down * high, 16), high), where].astype(F32)
            hold[m][pl.ds(pl.multiple_of(slot * rows + down * high, 16), high), where] = value.astype(BF)
            return carry

        lax.fori_loop(0, rows // high * across, step, 0)

    def add_plane(m, ref):
        rows = heights[m]
        high = min(rows, 64)

        def step(index, carry):
            where = pl.ds(pl.multiple_of(index * high, 16), high)
            value = hold[m][where, :].astype(F32) + ref[m][where, :].astype(F32)
            hold[m][where, :] = value.astype(BF)
            return carry

        lax.fori_loop(0, rows // high, step, 0)

    def to_other_core(m):
        for slot in (2, 3, 1, 0):
            fill(m, slot, 1 - core, [])
        moves[m]["core"]().start()

    def prepare(m):
        moves[m]["core"]().wait()
        for slot in (2, 3):
            fill(m, slot, core, [(inbox, slot)])

    def first_hop(m):
        moves[m]["far"]().start()

    def landed(m):
        moves[m]["far"]().wait_recv()

    def second_hop(m):
        fill(m, 1, core, [(inbox, 1), (far_in, 1)])
        moves[m]["near"]().start()

    def arrive(m):
        moves[m]["near"]().wait_recv()
        fill(m, 0, core, [(inbox, 0), (far_in, 0), (near_in, 0)])
        if m in planes:

            @pl.when(outer)
            def _():
                moves[m]["inward"]().start()
        else:
            moves[m]["held"]().start()

    def meet(m):
        @pl.when(inner)
        def _():
            moves[m]["inward"]().wait_recv()
            add_plane(m, plane_in)
            moves[m]["cross"]().start()

    def settle(m):
        @pl.when(inner)
        def _():
            moves[m]["cross"]().wait()
            add_plane(m, cross_in)
            moves[m]["outward"]().start()
            moves[m]["last_held"]().start()
            moves[m]["held"]().start()

    def finish(m):
        @pl.when(outer)
        def _():
            moves[m]["inward"]().wait()
            moves[m]["last_got"]().start()
            moves[m]["got"]().start()

    def begin(m):
        moves[m]["load"]().wait()

        @pl.when(outer)
        def _():
            moves[m]["inward"]().start()

    names = dict(
        core=to_other_core, fill=prepare, go=first_hop, wait=landed, turn=second_hop, own=arrive, meet=meet, settle=settle,
        finish=finish, load=begin,
    )
    for m in range(whole, total):
        moves[m]["load"]().start()
    def turn_over(left, target):
        def step(index, carry):
            where = pl.ds(pl.multiple_of(index * 256, 256), 256)
            target[where, :] = left[:, where].T
            return carry

        lax.fori_loop(0, left.shape[1] // 256, step, 0)

    for left, target in zip(lefts, turned):
        turn_over(left, target)
    for step, pair in order:
        if step == "mix":
            stages[pair]()
            continue
        for m in (2 * pair, 2 * pair + 1):
            names[step](m)

    for m in range(total):
        if m < whole:
            moves[m]["far"]().wait_send()
            moves[m]["near"]().wait_send()
        if m in planes:

            @pl.when(inner)
            def _():
                moves[m]["outward"]().wait_send()
                moves[m]["last_held"]().wait()
                moves[m]["held"]().wait()

            @pl.when(outer)
            def _():
                moves[m]["last_got"]().wait()
                moves[m]["got"]().wait()
        else:
            moves[m]["held"]().wait()


def reduce_order(pairs, rest):
    steps = [("load", k) for k in rest[:1]] + [("core", pairs[0]), ("fill", pairs[0]), ("go", pairs[0])]
    steps += [("core", k) for k in pairs[1:3]] + [("fill", pairs[1])]

    def across(step):
        for name, late in (("meet", 0), ("settle", 1), ("finish", 2)):
            for flow in (rest, [None, *pairs]):
                if 0 <= step - late < len(flow) and flow[step - late] is not None:
                    yield name, flow[step - late]

    for i, pair in enumerate(pairs):
        steps.append(("wait", pair))
        if i + 1 < len(pairs):
            steps.append(("go", pairs[i + 1]))
        steps.append(("turn", pair))
        steps += [("load", k) for k in rest[i + 1 : i + 2]]
        if i + 3 < len(pairs):
            steps.append(("core", pairs[i + 3]))
        if i + 2 < len(pairs):
            steps.append(("fill", pairs[i + 2]))
        waiting = list(across(i))
        steps += [item for item in waiting if item[0] == "meet"]
        steps.append(("own", pair))
        steps += [item for item in waiting if item[0] != "meet"]
    for i in range(len(pairs), max(len(pairs), len(rest)) + 3):
        steps += across(i)
    return steps


def mixing_order(rest, summed):
    words = (
        ("load", 0), ("mix", 0), ("core", 0), ("core", 1), ("fill", 0), ("go", 0), ("load", 1), ("core", 2),
        ("fill", 1), ("go", 1), ("core", 3), ("mix", 1), ("load", 2), ("fill", 2), ("wait", 0), ("turn", 0),
        ("go", 2), ("meet", 0), ("fill", 3), ("wait", 1), ("turn", 1), ("go", 3), ("meet", 1), ("load", 3),
        ("own", 0), ("mix", 2), ("settle", 0), ("meet", 2), ("own", 1), ("wait", 2), ("turn", 2), ("settle", 1),
        ("finish", 0), ("meet", 3), ("own", 2), ("Meet", 0), ("wait", 3), ("turn", 3), ("settle", 2), ("finish", 1),
        ("Meet", 1), ("mix", 3), ("own", 3), ("settle", 3), ("Settle", 0), ("finish", 2), ("Settle", 1),
        ("finish", 3), ("Finish", 0), ("Finish", 1),
    )
    steps = []
    for name, number in words:
        if name in ("load", "meet", "settle", "finish"):
            steps += [(name, rest[number])] if number < len(rest) else []
        elif name in ("Meet", "Settle", "Finish"):
            steps += [(name.lower(), number)] if number < summed else []
        else:
            steps.append((name, number))
    return steps


def mlp_items(up, down, wide_up, wide_down):
    items = []
    for part in range(PARTS):
        items += [
            (up, wide_up // PARTS, 0, 0, part * wide_up // PARTS, X_FIRST),
            (down, wide_down // PARTS, 1, 1, part * wide_down // PARTS, Y_FIRST),
        ]
    return items


def reduce_call(items, lefts, rights, packs, rest, planes, order, number, mixing=None, mix_in=()):
    halves = [right.shape[1] // 2 for right in rights]
    pieces = [item[:2] for item in items] + [piece.shape for piece in rest]
    whole, total = len(items), len(pieces)
    planes = list(planes) + list(range(whole, total))
    across = [pieces[m] for m in planes]

    def buffers(slots, shapes):
        return [pltpu.VMEM((slots * shape[0], shape[1]), BF) for shape in shapes]

    mix_out, scratch = [], []
    if mixing:
        blocks, rows, _ = mixing
        width = mix_in[6].shape[1] // 3
        group = width // blocks
        mix_out = [
            jax.ShapeDtypeStruct((rows, 3 * width), BF),
            jax.ShapeDtypeStruct((3, 3 * width), F32),
            jax.ShapeDtypeStruct((1, width), F32),
            jax.ShapeDtypeStruct((blocks * rows, group), F32),
        ]
        scratch = [
            pltpu.VMEM((blocks * rows, group), BF),
            pltpu.VMEM((blocks, rows, group), BF),
            pltpu.VMEM((blocks, rows, group), F32),
            pltpu.VMEM((blocks, 2 * rows, group), BF),
            pltpu.VMEM((blocks, 2 * rows, group), F32),
            pltpu.VMEM((blocks, 2 * rows, group), BF),
            pltpu.VMEM((blocks, 2 * rows, group), F32),
            pltpu.VMEM((blocks, rows, group), BF),
            pltpu.VMEM((blocks, rows, group), BF),
            pltpu.VMEM((8, 3 * width), F32),
            pltpu.VMEM((8, 3 * width), F32),
            pltpu.VMEM((16, 3 * width), F32),
        ]
    hbm = pl.BlockSpec(memory_space=pl.ANY)
    scratch += buffers(4, pieces[:whole]) + buffers(1, pieces[whole:])
    for slots in (4, 2, 1):
        scratch += buffers(slots, pieces[:whole])
    scratch += buffers(1, across) + buffers(1, across)
    scratch += [pltpu.VMEM((left.shape[1], left.shape[0]), left.dtype) for left in lefts]
    scratch += [pltpu.SemaphoreType.DMA((6, total)), pltpu.SemaphoreType.DMA((6, total)), pltpu.SemaphoreType.DMA((total,))]
    if mixing:
        scratch += [pltpu.SemaphoreType.DMA((7,)), pltpu.SemaphoreType.DMA((7,))]
    counts = (len(lefts), len(rights), len(packs))
    result = pl.pallas_call(
        functools.partial(reduce_kernel, items, pieces[whole:], halves, counts, planes, order, mixing),
        out_shape=mix_out + [jax.ShapeDtypeStruct(shape, BF) for shape in pieces + across],
        in_specs=[SMEM_SPEC] * min(len(mix_in), 2) + [VMEM_SPEC] * max(len(mix_in) - 2, 0)
        + [VMEM_SPEC] * sum(counts) + [hbm] * len(rest),
        out_specs=[VMEM_SPEC] * len(mix_out) + [hbm] * (total + len(planes)),
        scratch_shapes=scratch,
        compiler_params=pltpu.CompilerParams(
            collective_id=number, has_side_effects=True, vmem_limit_bytes=60 * 1024 * 1024
        ),
        name="unmix_reduce" if mixing else "reduce",
        cost_estimate=lasting(90),
    )(*mix_in, *lefts, *rights, *packs, *rest)
    mixed, own, other = result[: len(mix_out)], result[len(mix_out) : len(mix_out) + total], result[len(mix_out) + total :]
    return mixed, list(own), dict(zip(planes, other))


def reduce_plain(lefts, rights, packed, core):
    count = lax.axis_size("seq")
    chips = []
    for left, right in zip(lefts, rights):
        keep, send = core_halves(core, right)
        chips.append(dot_left(left, keep) + core_swap(dot_left(left, send).astype(BF)).astype(F32))
    keep, send = core_halves(core, packed)
    small = (keep + core_swap(send.astype(BF)).astype(F32)).astype(BF)
    up, down, enter, leave = (chip.astype(BF) for chip in chips)
    out_rows, half = leave.shape[0] // count, leave.shape[1]
    leave = jnp.concatenate([leave.reshape(count, out_rows, half), small.reshape(count, -1, half)], axis=1)
    own = []
    for chip in (up, down, enter, leave.reshape(-1, half)):
        own.append(lax.psum(lax.psum_scatter(chip, "seq", scatter_dimension=0, tiled=True), "dp"))
    return own[:3] + [own[3][:out_rows], own[3][out_rows:]]


def body(
    tokens, out_grad, lengths, ln1_gain, w_in, short_w, filt_in, filt_shift, sine_freq, filt_out,
    decay, filter_bias, w_out, ln2_gain, mlp_up, mlp_down,
):
    micro, rows, width = tokens.shape
    count = lax.axis_size("seq")
    here = lax.axis_index("seq")
    core = lax.axis_index("section")
    routed = count == 4 and lax.axis_size("dp") == 4
    slots = rows * count
    col_width = width // count
    hidden = mlp_up.shape[2]
    hidden_block = hidden // count
    half_block = hidden_block // 2
    table_np, weight_np, parity_np = packed_dft(rows)
    table = jnp.asarray(table_np).astype(BF)
    back = jnp.asarray(np.ascontiguousarray(table_np.T)).astype(BF)
    scale = jnp.asarray(np.concatenate([weight_np, parity_np], axis=1))
    embedding = jnp.asarray(positions_embedding(slots, FREQS))

    others = (ln1_gain, short_w, filt_in, filt_shift, sine_freq, decay, filter_bias, ln2_gain)
    other_shapes = [a.shape[1:] for a in others]
    other_sizes = [math.prod(shape) for shape in other_shapes]
    other_axis = (0, 1, 1, 0, 0, 0, 0, 0)
    lane, out_rows = width, filt_out.shape[1]
    other_rows = -(-sum(other_sizes) // lane)
    packed_rows = -(-(out_rows + other_rows) // 16) * 16

    def packed_small(top, parts):
        flat = jnp.concatenate(parts, axis=-1)
        lead = flat.shape[:-1]
        none = ((0, 0),) * len(lead)
        flat = jnp.pad(flat, none + ((0, other_rows * lane - flat.shape[-1]),)).reshape(lead + (other_rows, lane))
        flat = jnp.pad(flat, none + ((0, packed_rows - out_rows - other_rows), (0, 0)))
        return jnp.concatenate([top, flat], axis=-2)

    flat = packed_small(filt_out[0], [a.reshape(-1) for a in others])
    flat_all, out_all, in_all, up_all, down_all = gather_shards([flat, w_out[0], w_in[0], mlp_up[0], mlp_down[0]])
    everywhere = flat_all.reshape(2, count, packed_rows, lane)
    gathered = [
        (
            in_all[layer * width : (layer + 1) * width], out_all[layer * width : (layer + 1) * width],
            up_all[layer * width : (layer + 1) * width], down_all[layer * hidden : (layer + 1) * hidden],
        )
        for layer in range(2)
    ]

    def small_of(layer):
        found = []
        offset = 0
        below = everywhere[layer, :, out_rows : out_rows + other_rows].reshape(count, other_rows * lane)
        for shape, size, axis in zip(other_shapes, other_sizes, other_axis):
            part = below[:, offset : offset + size].reshape((count,) + shape)
            part = jnp.moveaxis(part, 0, axis)
            full = list(shape)
            full[axis] = shape[axis] * count
            found.append(part.reshape(full).astype(F32))
            offset += size
        top = everywhere[layer, :, :out_rows].reshape(count * out_rows, lane).astype(F32)
        return found[:5] + [top] + found[5:]

    length_row = lax.dynamic_index_in_dim(lengths, core, 0, keepdims=False)
    index_all = jnp.arange(count, dtype=jnp.int32)
    started = jnp.logical_and(length_row[None, :] > 0, index_all[None, :] <= index_all[:, None])
    regions = jnp.max(jnp.where(started, index_all[None, :], 0), axis=1)
    doc_length = jnp.sum(jnp.where(regions[:, None] == index_all[None, :], length_row[None, :], 0), axis=1)
    own_region = jnp.sum(jnp.where(index_all == here, regions, 0))
    own_length = jnp.sum(jnp.where(index_all == here, doc_length, 0))
    last_region = jnp.sum(jnp.where(index_all == here - 1, regions, 0))
    offsets = (here - own_region) * rows + jnp.arange(rows, dtype=jnp.int32)
    valid = (offsets < own_length).astype(F32)[:, None]
    carried_on = jnp.logical_and(here > 0, last_region == own_region).astype(F32)
    same = (regions[:, None] == regions[None, :]).astype(F32)

    def to_columns(values):
        return lax.all_to_all(values.astype(BF), "seq", split_axis=1, concat_axis=0, tiled=True)

    def to_rows(values):
        return lax.all_to_all(values, "seq", split_axis=0, concat_axis=1, tiled=True).astype(F32)

    def filter_stage(layer):
        _, _, in_w, shift_w, freq_w, out_w, decay_w, _, _ = small_of(layer)
        out_cols = lax.dynamic_slice_in_dim(out_w, here * col_width, col_width, 1)
        decay_cols = lax.dynamic_slice_in_dim(decay_w, here * col_width, col_width, 0)
        taps, pull = jax.vjp(
            lambda *p: filter_taps(*p, embedding), in_w, shift_w, freq_w, out_cols, decay_cols
        )
        spectra = jnp.einsum(
            "fs,msc->mfc", table, taps.astype(BF).reshape(count, rows, col_width), preferred_element_type=F32
        )
        before = jnp.concatenate([jnp.zeros_like(spectra[:1]), spectra[:-1]], axis=0)
        return (spectra + scale[:, 1:2] * before) * scale[:, 0:1], pull

    def forward(layer_in, layer):
        gain_one, short_weights, _, _, _, _, _, bias, gain_two = small_of(layer)
        in_matrix, out_matrix, up_matrix, down_matrix = gathered[layer]
        filt, pull = filter_stage(layer)
        normed = layer_norm(layer_in, gain_one).astype(BF)
        projected = dot(normed, in_matrix).astype(BF)
        if routed:
            rim, x_cols, filtered, gated = mix(
                same, carried_on.reshape(1), table, back, filt, projected, short_weights, bias[None], valid, count, rows, 3 + layer
            )
        else:
            rim = shifted(projected[rows - 2 :], "seq", 1)
            mixed = short_mix(rim.astype(F32), projected.astype(F32), short_weights, carried_on)
            first, second, third = mixed[:, :width], mixed[:, width : 2 * width], mixed[:, 2 * width :]
            signal = first * third
            x_cols = to_columns(signal * valid)
            y_cols = convolve(same, table, back, filt, x_cols, count, rows)
            filtered = to_rows(y_cols) * valid + bias * signal
            gated = (second * filtered).astype(BF)
        residual = layer_in + dot(gated, out_matrix)
        normed_two = layer_norm(residual, gain_two).astype(BF)
        upward = dot(normed_two, up_matrix)
        active = gelu_tanh(upward).astype(BF)
        layer_out = residual + dot(active, down_matrix)
        stored = (
            layer_in, normed, projected, rim, filtered, gated, residual, normed_two,
            upward, active, x_cols, filt, pull,
        )
        return layer_out.astype(BF), stored

    def backward(upstream, stored, layer, rest):
        (
            layer_in, normed, projected, rim, filtered, gated, residual, normed_two,
            upward, active, x_cols, filt, pull,
        ) = stored
        gain_one, short_weights, in_w, shift_w, freq_w, out_w, decay_w, bias, gain_two = small_of(layer)
        in_matrix, out_matrix, up_matrix, down_matrix = gathered[layer]
        grad_hidden = jax.vjp(gelu_tanh, upward)[1](dot_right(upstream, down_matrix))[0].astype(BF)
        grad_norm_two = dot_right(grad_hidden, up_matrix)
        grad_resid_norm, grad_gain_two = jax.vjp(layer_norm, residual, gain_two)[1](grad_norm_two)
        grad_residual = upstream.astype(F32) + grad_resid_norm
        grad_branch = grad_residual.astype(BF)
        grad_gated = dot_right(grad_branch, out_matrix)
        if routed:
            mix_in = (
                same, carried_on.reshape(1), table, back, scale, filt, projected, rim, short_weights, bias[None], valid,
                x_cols, filtered, grad_gated.astype(BF),
            )
            block_rows = width // count
            items = mlp_items(block_rows, hidden_block, hidden // 2, width // 2)
            summed = 0 if layer else PARTS // 2
            order = mixing_order(list(range(PARTS, PARTS + len(rest) // 2)), summed)
            (grad_proj, grad_short, grad_bias, grad_taps), own, other = reduce_call(
                items, [normed_two, active], [grad_hidden, upstream], [], rest, range(2 * summed), order, 5 + layer,
                (count, rows, 32), mix_in,
            )
            grad_bias = grad_bias[0]
        else:
            mixed = short_mix(rim.astype(F32), projected.astype(F32), short_weights, carried_on)
            first, second, third = mixed[:, :width], mixed[:, width : 2 * width], mixed[:, 2 * width :]
            signal = first * third
            grad_second = grad_gated * filtered
            grad_filtered = grad_gated * second
            grad_bias = jnp.sum(grad_filtered * signal, axis=0)
            g_cols = to_columns(grad_filtered * valid)
            dx_cols, grad_taps = correlate(same, table, back, scale, filt, x_cols, g_cols, count, rows)
            grad_signal = to_rows(dx_cols) * valid + bias * grad_filtered
            grad_mixed = jnp.concatenate([grad_signal * third, grad_second, grad_signal * first], axis=1)
            short_pull = jax.vjp(
                lambda a, b, c: short_mix(a, b, c, carried_on), rim.astype(F32), projected.astype(F32), short_weights
            )[1]
            grad_rim, grad_proj, grad_short = short_pull(grad_mixed)
            returned = shifted(grad_rim, "seq", -1)
            tail = grad_proj[rows - 2 :] + returned
            grad_proj = jnp.concatenate([grad_proj[: rows - 2], tail], axis=0)
            grad_proj = grad_proj.astype(BF)
        grad_normed = dot_right(grad_proj, in_matrix)
        grad_norm_in, grad_gain_one = jax.vjp(layer_norm, layer_in, gain_one)[1](grad_normed)
        grad_layer_in = (grad_residual + grad_norm_in).astype(BF)
        d_in, d_shift, d_freq, d_out_cols, d_decay_cols = pull(grad_taps)
        d_out = lax.dynamic_update_slice_in_dim(jnp.zeros_like(out_w), d_out_cols, here * col_width, 1)
        d_decay = lax.dynamic_update_slice_in_dim(jnp.zeros_like(decay_w), d_decay_cols, here * col_width, 0)
        parts = []
        other_grads = (grad_gain_one, grad_short, d_in, d_shift, d_freq, d_decay, grad_bias, grad_gain_two)
        for grad, shape, axis in zip(other_grads, other_shapes, other_axis):
            split = list(grad.shape)
            split[axis : axis + 1] = [count, shape[axis]]
            parts.append(jnp.moveaxis(grad.reshape(split), axis, 0).reshape(count, -1))
        packed = packed_small(d_out.reshape(count, out_rows, lane), parts).reshape(count * packed_rows, lane)
        if routed:
            return grad_layer_in, (own, other, normed, grad_proj, gated, grad_branch, packed)
        factors = ([normed_two, active, normed, gated], [grad_hidden, upstream, grad_proj, grad_branch], packed)
        return grad_layer_in, factors

    def row_of(values):
        return lax.dynamic_index_in_dim(values, core, 0, keepdims=False)

    out_first, stored_first = forward(row_of(tokens).astype(F32), 0)
    out_second, stored_second = forward(out_first.astype(F32), 1)
    if routed:
        grad_second, kept_second = backward(row_of(out_grad), stored_second, 1, [])
        grad_first, kept_first = backward(grad_second, stored_first, 0, kept_second[0])
        items, lefts, rights, packs = [], [], [], []
        for k, (_, _, normed, grad_proj, gated, grad_branch, packed) in enumerate((kept_second, kept_first)):
            lefts += [normed, gated]
            rights += [grad_proj, grad_branch]
            packs.append(packed)
            block_rows, part = width // count, 3 * width // 2 // PARTS
            for piece in range(PARTS):
                order = Y_FIRST if piece % 2 else X_FIRST
                items.append((block_rows, part, 2 * k, 2 * k, piece * part, order))
            items.append((block_rows, width // 2, 2 * k + 1, 2 * k + 1, 0, X_FIRST))
            items.append((packed_rows, lane // 2, k, -1, 0, Y_FIRST))
        each, mlp = PARTS + 2, 2 * PARTS
        done = 2 * (PARTS // 2)
        order = reduce_order([0, 1, 3, 4, 2, 5], list(range(each, each + PARTS - done // 2)))
        _, own, other = reduce_call(items, lefts, rights, packs, kept_first[0][done:mlp], range(2 * each), order, 1)
        other = [other[m] for m in range(2 * each + mlp - done)]

        def assembled(late, mlp_part):
            groups = (mlp_part[::2], mlp_part[1::2], late[:PARTS])
            return [jnp.concatenate(group, axis=1) for group in groups] + list(late[PARTS:])

        second_other = [kept_first[1][m] for m in range(mlp, 2 * mlp)]
        own_second, other_second = assembled(own[:each], kept_first[0][mlp:]), assembled(other[:each], second_other)
        own_first = assembled(own[each : 2 * each], kept_first[0][:done] + own[2 * each :])
        first_other = [kept_first[1][m] for m in range(done)]
        other_first = assembled(other[each : 2 * each], first_other + other[2 * each :])
    else:
        grad_second, factors_second = backward(row_of(out_grad), stored_second, 1, [])
        own_second = reduce_plain(*factors_second, core)
        grad_first, factors_first = backward(grad_second, stored_first, 0, [])
        own_first = reduce_plain(*factors_first, core)
        other_first, other_second = ([core_swap(part) for part in own] for own in (own_first, own_second))

    def both_rows(of_first, of_second):
        kept = jnp.where(core == 0, of_first, of_second)
        received = core_swap(jnp.where(core == 0, of_second, of_first))
        return jnp.stack([jnp.where(core == 0, kept, received), jnp.where(core == 0, received, kept)])[None]

    layer_outputs = both_rows(out_first, out_second)
    input_grads = both_rows(grad_first, grad_second)

    def finish(index):
        low = jnp.where(core == 0, own_first[index], other_second[index])
        high = jnp.where(core == 0, other_first[index], own_second[index])
        return jnp.concatenate([low, high], axis=1).astype(F32)

    grad_up, grad_down, grad_in, grad_out = (finish(index) for index in range(4))
    small_total = finish(4)
    below = small_total[out_rows : out_rows + other_rows].reshape(-1)
    other_out = []
    offset = 0
    for shape, size in zip(other_shapes, other_sizes):
        other_out.append(below[offset : offset + size].reshape((1,) + shape))
        offset += size
    g_ln1, g_short, g_fin, g_shift, g_freq, g_decay, g_bias, g_ln2 = other_out
    g_fout = small_total[:out_rows][None]
    return (
        layer_outputs, input_grads, g_ln1, grad_in[None], g_short, g_fin, g_shift, g_freq, g_fout, g_decay, g_bias,
        grad_out[None], g_ln2, grad_up[None], grad_down[None],
    )


def solution(mesh):
    vector = P("section", "seq")
    matrix = P("section", "seq", None)
    last = P("section", None, "seq")
    tokens = P("dp", "seq", None)
    outputs = P("section", "dp", "seq", None)
    in_specs = (
        tokens, tokens, P("dp", None), vector, matrix, last, last, vector, vector, matrix, vector, vector, matrix,
        vector, matrix, matrix,
    )
    out_specs = (
        outputs, outputs, vector, matrix, last, last, vector, vector, matrix, vector, vector, matrix, vector, matrix,
        matrix,
    )
    return jax.shard_map(body, mesh=mesh, in_specs=in_specs, out_specs=out_specs, check_vma=False)
```
